128 devices in a mesh: shard: 8 (over x, core), owner: 16 (over z, y).
Axes of the slice: x: 4, y: 4, z: 4, core: 2. Of those that a mesh axis runs over, the one named last changes fastest.
Arguments:
- gradient: float32 [128, 2048, 768], P('owner', 'shard'), may hold values from -6 to 6
- old_basis: float32 [128, 2048, 256], P('owner', 'shard'), may hold values from -0.125 to 0.125
- moment_one: float32 [128, 256, 768], P('owner', 'shard'), may hold values from -6 to 6
- moment_two: float32 [128, 256, 768], P('owner', 'shard'), may hold values from 0.01 to 1
- slot_expert: int32 [128], replicated, may hold values from 0 to 127, as said below
- cost: int32 [128], replicated, may hold values from 0 to 5
Outputs:
- new_basis: float32 [128, 2048, 256], P('owner', 'shard')
- new_moment_one: float32 [128, 256, 768], P('owner', 'shard')
- new_moment_two: float32 [128, 256, 768], P('owner', 'shard')
- update: bfloat16 [128, 2048, 768], P('owner', 'shard')
The draws below stay inside these ranges and needn't reach their ends.
Inputs may be any that keep to these rules, and one draw needn't show every extreme that they name: `slot_expert`: A permutation of the 128 experts. Expert e's gradient lies in owner group e // 8; state slot s lies in owner group s // 8. The 8 slots of one owner group hold experts of 8 different owner groups, and the 8 experts of one owner group are held by 8 different owner groups.
All inputs are finite; a program needn't handle non-finite values.
Results may differ from the reference program's by a relative error of at most 0.001.
Values sent between devices are 32-bit elements; how exact they have to be, the bound alone decides.
A program may use at most 192 MiB of HBM per device.

```python
import math
import jax
import jax.numpy as jnp
from jax import lax

ROWS = 2048
COLS = 768
RANK = 256
ITERS = 5
SLOTS = 8
EXPERTS = 128


def joint_tables(key):
    owners = EXPERTS // SLOTS
    key_offset, key_homes, key_local, key_heavy, key_light = jax.random.split(jax.random.fold_in(key, 7), 5)
    offsets = jax.random.permutation(key_offset, owners)[:SLOTS].astype(jnp.int32)
    homes = jax.random.permutation(key_homes, owners).astype(jnp.int32)
    owner_ids = jnp.arange(owners, dtype=jnp.int32)
    home_of = homes[(owner_ids[:, None] + offsets[None, :]) % owners]
    local_perm = jax.vmap(lambda sub_key: jax.random.permutation(sub_key, SLOTS))(jax.random.split(key_local, owners)).astype(jnp.int32)
    slot_ids = jnp.arange(SLOTS, dtype=jnp.int32)
    local_index = local_perm[home_of, slot_ids[None, :]]
    slot_table = (home_of * SLOTS + local_index).reshape(-1).astype(jnp.int32)
    heavy = jax.random.randint(key_heavy, (owners,), 0, SLOTS, dtype=jnp.int32)
    light = jax.random.randint(key_light, (owners, SLOTS), 0, 2, dtype=jnp.int32)
    slot_cost = jnp.where(slot_ids[None, :] == heavy[:, None], ITERS, light).reshape(-1).astype(jnp.int32)
    cost_table = jnp.zeros((EXPERTS,), jnp.int32).at[slot_table].set(slot_cost)
    return (slot_table, cost_table)


def draw_slot_expert(key, part):
    return joint_tables(key)[0]


def draw_cost(key, part):
    return joint_tables(key)[1]


def block_scale(stream_key, extent, cuts, least, high):
    def one(dim, shards_of):
        draws = jax.random.uniform(jax.random.fold_in(jax.random.fold_in(stream_key, 6), dim), (shards_of,), jnp.float32, least / len(cuts), high / len(cuts))
        return jnp.repeat(jnp.exp(draws), extent[dim] // shards_of).reshape((-1,) + (1,) * (len(extent) - dim - 1))

    gain = one(*cuts[0])
    for cut in cuts[1:]:
        gain = gain * one(*cut)
    return gain


def bell_draw(stream_key, dims, scale, most, pieces=(), kind=jnp.bfloat16):
    array = jax.random.normal(stream_key, dims, jnp.float32) * scale
    if len(pieces) > 0:
        array = block_scale(stream_key, dims, pieces, -0.22, 0.18) * array
    return jnp.clip(array, min=-most, max=most).astype(kind)


def setup_inputs(seed: int = 0) -> dict:
    keys = jax.random.split(jax.random.key(seed), 7)
    return {
        "gradient": bell_draw(keys[0], (EXPERTS, ROWS, COLS), 1.0, 6.0, ((0, 16), (1, 8)), jnp.float32),
        "old_basis": bell_draw(keys[1], (EXPERTS, ROWS, RANK), ROWS ** -0.5, 0.125, ((0, 16), (1, 8)), jnp.float32),
        "moment_one": bell_draw(keys[2], (EXPERTS, RANK, COLS), 1.0, 6.0, ((0, 16), (1, 8)), jnp.float32),
        "moment_two": jnp.clip(jnp.exp(math.log(1.0) - 4.6051702 * jax.random.uniform(keys[3], (EXPERTS, RANK, COLS), jnp.float32) ** block_scale(keys[3], (EXPERTS, RANK, COLS), ((0, 16), (1, 8)), -0.2, 0.2)), 0.01, 1.0),
        "slot_expert": draw_slot_expert(jax.random.fold_in(keys[6], 71), 0),
        "cost": draw_cost(jax.random.fold_in(keys[6], 71), 0),
    }


HIGHEST_PREC = lax.Precision.HIGHEST
BETA_ONE = 0.9
BETA_TWO = 0.99
EPSILON = 1e-08
GALORE_SCALE = 0.25

def whole_step(basis_now, grad_now):
    inner_prod = jnp.dot(grad_now.T, basis_now, precision=HIGHEST_PREC)
    tall_block = jnp.dot(grad_now, inner_prod, precision=HIGHEST_PREC)
    gram_matrix = jnp.dot(tall_block.T, tall_block, precision=HIGHEST_PREC)
    factor = jnp.linalg.cholesky(gram_matrix)
    return lax.linalg.triangular_solve(factor, tall_block, left_side=False, lower=True, transpose_a=True)

def refresh(grad_now, basis_now, iter_count):
    return lax.fori_loop(0, iter_count, lambda step_index, current: whole_step(current, grad_now), basis_now)

def reference(gradient, old_basis, moment_one, moment_two, slot_expert, cost):

    def per_slot(slot_index):
        expert = slot_expert[slot_index]
        grad_now = gradient[expert]
        basis_new = refresh(grad_now, old_basis[slot_index], cost[expert])
        projected = jnp.dot(basis_new.T, grad_now, precision=HIGHEST_PREC)
        moment_new = BETA_ONE * moment_one[slot_index] + (1.0 - BETA_ONE) * projected
        second_new = BETA_TWO * moment_two[slot_index] + (1.0 - BETA_TWO) * projected * projected
        normed = moment_new / (jnp.sqrt(second_new) + EPSILON)
        update = (GALORE_SCALE * jnp.dot(basis_new, normed, precision=HIGHEST_PREC)).astype(jnp.bfloat16)
        return (basis_new, moment_new, second_new, update)
    basis_all, moment_all, second_all, update_all = lax.map(per_slot, jnp.arange(EXPERTS, dtype=jnp.int32))
    return (basis_all, moment_all, second_all, update_all)
```

```python
import jax, jax.numpy as jnp
from jax import lax
from jax.experimental import pallas as pl
from jax.sharding import PartitionSpec as P
from jax.experimental.pallas import tpu as pltpu

BF = jnp.bfloat16
F32 = jnp.float32

def split(x):
    hi = x.astype(BF)
    return hi, (x - hi.astype(F32)).astype(BF)

def mm(a, b, dims):
    return lax.dot_general(a, b, (dims, ((), ())), preferred_element_type=F32)

NN = ((1,), (0,))
TN = ((0,), (0,))
NT = ((1,), (1,))

def dot3(a, b, dims):
    ah, al = a
    bh, bl = b
    return mm(ah, bh, dims) + (mm(ah, bl, dims) + mm(al, bh, dims))

NB = 16

def factor(c_ref, rx, rh, rl):
    n = c_ref.shape[0]
    sub = lax.broadcasted_iota(jnp.int32, (NB, 128), 0)
    row = lax.broadcasted_iota(jnp.int32, (NB, n), 0)
    lane = lax.broadcasted_iota(jnp.int32, (NB, n), 1)
    for p in range(n // NB):
        lo = p * NB
        s_a = c_ref[lo:lo + NB, :]
        s_i = jnp.where(lane == row + lo, 1.0, 0.0)
        if p > 0:
            lh, ll = rh[0:lo, 0:n], rl[0:lo, 0:n]
            ch, cl = lh[:, lo:lo + NB], ll[:, lo:lo + NB]
            s_a = s_a - dot3((ch, cl), (lh, ll), TN)
            xh, xl = rh[0:lo, n:2 * n], rl[0:lo, n:2 * n]
            s_i = s_i - dot3((ch, cl), (xh, xl), TN)
        cols = [jnp.broadcast_to(s_a[:, lo + k:lo + k + 1], (NB, 128)) for k in range(NB)]
        pivots = []
        for j in range(NB):
            d = cols[j][j:j + 1, :]
            r = 1.0 / d
            pivots.append(d)
            m = jnp.where(sub > j, cols[j] * r, 0.0)
            for k in range(j + 1, NB):
                cols[k] = cols[k] - m * cols[k][j:j + 1, :]
            m2 = jnp.concatenate([m] * (n // 128), axis=1)
            s_a = s_a - m2 * s_a[j:j + 1, :]
            s_i = s_i - m2 * s_i[j:j + 1, :]
        piv = jnp.concatenate(pivots, axis=0)
        scale = lax.rsqrt(piv)
        scale = jnp.concatenate([scale] * (n // 128), axis=1)
        r_a = jnp.where(lane >= lo + row, s_a * scale, 0.0)
        r_i = s_i * scale
        out = jnp.concatenate([r_a, r_i], axis=1)
        rx[lo:lo + NB, :] = out
        hi = out.astype(BF)
        rh[lo:lo + NB, :] = hi
        rl[lo:lo + NB, :] = (out - hi.astype(F32)).astype(BF)

def body(cnt, g_ref, p_ref, ret_ref, gh, gl, k_h, k_l, z_ref, m_ref, w_ref, c_ref, rx, rh, rl):
    count = cnt[0]
    rows, cols = g_ref.shape
    rank = p_ref.shape[1]
    step = 256
    z_ref[...] = jnp.zeros_like(z_ref)

    @pl.loop(0, rows // step)
    def _(i):
        at = pl.ds(pl.multiple_of(i * step, step), step)
        h, l = split(g_ref[at, :])
        gh[at, :] = h
        gl[at, :] = l
        z_ref[...] += dot3((h, l), split(p_ref[at, :]), TN)

    @pl.when(count > 0)
    def _():
        ct = cols // 256
        for a in range(ct):
            ra = slice(256 * a, 256 * a + 256)
            for b in range(a, ct):
                rb = slice(256 * b, 256 * b + 256)
                blk = mm(gh[:, ra], gh[:, rb], TN) + (mm(gh[:, ra], gl[:, rb], TN) + mm(gl[:, ra], gh[:, rb], TN))
                h, l = split(blk)
                k_h[ra, rb] = h
                k_l[ra, rb] = l
                if b > a:
                    h, l = split(blk.T)
                    k_h[rb, ra] = h
                    k_l[rb, ra] = l

    @pl.loop(0, count)
    def _(it):
        z = split(z_ref[...])
        w_ref[...] = dot3((k_h[...], k_l[...]), z, NN)
        w = split(w_ref[...])
        c_ref[...] = dot3(z, w, TN)
        factor(c_ref, rx, rh, rl)
        x = (rh[:, rank:], rl[:, rank:])
        z_ref[...] = dot3(w, x, NT)

        @pl.when(it == count - 1)
        def _():
            m_ref[...] = dot3(z, x, NT)

    @pl.when(count > 0)
    def _():
        mh, ml = split(m_ref[...])

        @pl.loop(0, rows // step)
        def _(i):
            at = pl.ds(pl.multiple_of(i * step, step), step)
            ret_ref[i, 0:step, :] = dot3((gh[at, :], gl[at, :]), (mh, ml), NN)

    @pl.when(count == 0)
    def _():
        @pl.loop(0, rows // step)
        def _(i):
            at = pl.ds(pl.multiple_of(i * step, step), step)
            ret_ref[i, 0:step, :] = p_ref[at, :]

    for c in range(cols // 256):
        t = z_ref[256 * c:256 * c + 256, :].T
        for s in range(rows // step):
            ret_ref[s, step + 32 * c:step + 32 * c + 32, :] = t[32 * s:32 * s + 32, :]

def refresh(count, g, p):
    rows, cols = g.shape
    rank = p.shape[1]
    V = pltpu.VMEM
    return pl.pallas_call(
        body,
        out_shape=jax.ShapeDtypeStruct((rows // 256, 256 + 96, rank), F32),
        in_specs=[pl.BlockSpec(memory_space=pltpu.SMEM), pl.BlockSpec(memory_space=V), pl.BlockSpec(memory_space=V)],
        out_specs=pl.BlockSpec(memory_space=V),
        scratch_shapes=[V((rows, cols), BF), V((rows, cols), BF), V((cols, cols), BF), V((cols, cols), BF),
                        V((cols, rank), F32), V((cols, rank), F32), V((cols, rank), F32), V((rank, rank), F32),
                        V((rank, 2 * rank), F32), V((rank, 2 * rank), BF), V((rank, 2 * rank), BF)],
        compiler_params=pltpu.CompilerParams(vmem_limit_bytes=56 * 1024 * 1024),
        name="refresh",
    )(count, g, p)


BETA_ONE = 0.9
BETA_TWO = 0.99
EPSILON = 1e-08
GALORE_SCALE = 0.25


def update_body(b_ref, n_ref, o_ref):
    o_ref[0] = (GALORE_SCALE * dot3(split(b_ref[0]), split(n_ref[0]), NN)).astype(BF)


def make_update(basis, normed):
    slots, rows, rank = basis.shape
    cols = normed.shape[2]
    return pl.pallas_call(
        update_body,
        grid=(slots,),
        out_shape=jax.ShapeDtypeStruct((slots, rows, cols), BF),
        in_specs=[
            pl.BlockSpec((1, rows, rank), lambda i: (i, 0, 0)),
            pl.BlockSpec((1, rank, cols), lambda i: (i, 0, 0)),
        ],
        out_specs=pl.BlockSpec((1, rows, cols), lambda i: (i, 0, 0)),
        compiler_params=pltpu.CompilerParams(vmem_limit_bytes=32 * 1024 * 1024),
        name="update",
    )(basis, normed)


def pick(array, index):
    return jnp.stack([lax.dynamic_index_in_dim(array, index[i], 0, keepdims=False) for i in range(index.shape[0])])


def on_device(gradient, old_basis, moment_one, moment_two, slot_expert, cost):
    slots = gradient.shape[0]
    owners = lax.axis_size("owner")
    owner_now = lax.axis_index("owner")
    shard_now = lax.axis_index("shard")
    table = slot_expert.reshape(owners, slots)
    mine = lax.dynamic_index_in_dim(table, owner_now, 0, keepdims=False)
    homes = jnp.arange(owners)
    slot_for = jnp.sum(jnp.where(mine[None, :] // slots == homes[:, None], jnp.arange(slots)[None, :], 0), axis=1)
    own_ids = owner_now * slots + jnp.arange(slots)
    hits = table[None, :, :] == own_ids[:, None, None]
    holder = jnp.sum(jnp.where(hits, homes[None, :, None], 0), axis=(1, 2))
    expert_for = jnp.sum(jnp.where(hits, jnp.arange(slots)[:, None, None], 0), axis=(0, 2))
    count = lax.dynamic_slice_in_dim(cost, owner_now * slots + shard_now, 1)

    grad_whole = lax.all_to_all(gradient, "shard", split_axis=0, concat_axis=1, tiled=True)
    basis_there = lax.all_to_all(pick(old_basis, slot_for), "owner", split_axis=0, concat_axis=0, tiled=True)
    basis_whole = lax.all_to_all(pick(basis_there, holder), "shard", split_axis=0, concat_axis=1, tiled=True)
    result = refresh(count, grad_whole[0], basis_whole[0])
    result = lax.all_to_all(result, "shard", split_axis=0, concat_axis=0, tiled=True)
    result = lax.all_to_all(pick(result, expert_for), "owner", split_axis=0, concat_axis=0, tiled=True)
    result = pick(result, mine // slots)
    basis_slot = result[:, :256, :]
    projected = jnp.concatenate([result[:, 256 + 32 * c : 288 + 32 * c, :] for c in range(3)], axis=2)
    moment_new = BETA_ONE * moment_one + (1.0 - BETA_ONE) * projected
    second_new = BETA_TWO * moment_two + (1.0 - BETA_TWO) * projected * projected
    normed = moment_new / (jnp.sqrt(second_new) + EPSILON)
    update = make_update(basis_slot, lax.all_gather(normed, "shard", axis=1, tiled=True))
    return (basis_slot, moment_new, second_new, update)


def solution(mesh):
    spec = P("owner", "shard", None)
    return jax.shard_map(
        on_device, mesh=mesh, in_specs=(spec,) * 4 + (P(), P()), out_specs=(spec,) * 4, check_vma=False
    )
```

```python
import functools
import jax, jax.numpy as jnp
from jax import lax
from jax.experimental import pallas as pl
from jax.sharding import PartitionSpec as P
from jax.experimental.pallas import tpu as pltpu

BF = jnp.bfloat16
F32 = jnp.float32

def split(x):
    hi = x.astype(BF)
    return hi, (x - hi.astype(F32)).astype(BF)

def mm(a, b, dims):
    return lax.dot_general(a, b, (dims, ((), ())), preferred_element_type=F32)

NN = ((1,), (0,))
TN = ((0,), (0,))
NT = ((1,), (1,))

def dot3(a, b, dims):
    ah, al = a
    bh, bl = b
    return mm(ah, bh, dims) + (mm(ah, bl, dims) + mm(al, bh, dims))

NB = 16

def factor(c_ref, rx, rh, rl):
    n = c_ref.shape[0]
    sub = lax.broadcasted_iota(jnp.int32, (NB, 128), 0)
    row = lax.broadcasted_iota(jnp.int32, (NB, n), 0)
    lane = lax.broadcasted_iota(jnp.int32, (NB, n), 1)
    for p in range(n // NB):
        lo = p * NB
        s_a = c_ref[lo:lo + NB, :]
        s_i = jnp.where(lane == row + lo, 1.0, 0.0)
        if p > 0:
            lh, ll = rh[0:lo, 0:n], rl[0:lo, 0:n]
            ch, cl = lh[:, lo:lo + NB], ll[:, lo:lo + NB]
            s_a = s_a - dot3((ch, cl), (lh, ll), TN)
            xh, xl = rh[0:lo, n:2 * n], rl[0:lo, n:2 * n]
            s_i = s_i - dot3((ch, cl), (xh, xl), TN)
        cols = [jnp.broadcast_to(s_a[:, lo + k:lo + k + 1], (NB, 128)) for k in range(NB)]
        pivots = []
        for j in range(NB):
            d = cols[j][j:j + 1, :]
            r = 1.0 / d
            pivots.append(d)
            m = jnp.where(sub > j, cols[j] * r, 0.0)
            for k in range(j + 1, NB):
                cols[k] = cols[k] - m * cols[k][j:j + 1, :]
            m2 = jnp.concatenate([m] * (n // 128), axis=1)
            s_a = s_a - m2 * s_a[j:j + 1, :]
            s_i = s_i - m2 * s_i[j:j + 1, :]
        piv = jnp.concatenate(pivots, axis=0)
        scale = lax.rsqrt(piv)
        scale = jnp.concatenate([scale] * (n // 128), axis=1)
        r_a = jnp.where(lane >= lo + row, s_a * scale, 0.0)
        r_i = s_i * scale
        out = jnp.concatenate([r_a, r_i], axis=1)
        rx[lo:lo + NB, :] = out
        hi = out.astype(BF)
        rh[lo:lo + NB, :] = hi
        rl[lo:lo + NB, :] = (out - hi.astype(F32)).astype(BF)

MESH = pl.DeviceIdType.MESH
V = pltpu.VMEM


def greet(groups):
    barrier = pltpu.get_barrier_semaphore()
    total = 0
    for axis, size in groups:
        me = lax.axis_index(axis)

        @pl.loop(1, size)
        def _(d):
            pl.semaphore_signal(barrier, inc=1, device_id={axis: lax.rem(me + d, size)}, device_id_type=MESH)

        total += size - 1
    pl.semaphore_wait(barrier, total)


def remote(src, dst, send, recv, axis, target):
    return pltpu.make_async_remote_copy(
        src_ref=src, dst_ref=dst, send_sem=send, recv_sem=recv, device_id={axis: target}, device_id_type=MESH
    )


def enter_body(shards, owners, slot_ref, holder_ref, g_ref, b_ref, gh_out, gl_out, kh_out, kl_out, z_out, p_out,
               gland, gh, gl, kacc, stage, landed, stage2, pland,
               g_send, g_recv, a_send, a_recv, b_send, b_recv, own_sem, h_sem, l_sem):
    s_me = lax.axis_index("shard")
    o_me = lax.axis_index("owner")
    greet((("shard", shards), ("owner", owners)))

    def at_shard(d):
        return lax.rem(s_me + d, shards)

    def from_shard(d):
        return lax.rem(s_me - d + shards, shards)

    def at_owner(d):
        return lax.rem(o_me + d, owners)

    def from_owner(d):
        return lax.rem(o_me - d + owners, owners)

    own = pltpu.make_async_copy(g_ref.at[s_me], gland.at[s_me], own_sem)
    own.start()

    @pl.loop(1, owners)
    def _(d):
        t = at_owner(d)
        stage[t] = b_ref[slot_ref[t]]
        remote(stage.at[t], landed.at[o_me], a_send.at[d], a_recv.at[d], "owner", t).start()

    @pl.loop(1, shards)
    def _(d):
        t = at_shard(d)
        remote(g_ref.at[t], gland.at[s_me], g_send.at[d], g_recv.at[d], "shard", t).start()

    landed[o_me] = b_ref[slot_ref[o_me]]
    kacc[...] = jnp.zeros_like(kacc)
    own.wait()
    tiles = kacc.shape[0] // 256

    def gram(f):
        h, l = split(gland[f])
        gh[f] = h
        gl[f] = l
        pltpu.make_async_copy(gh.at[f], gh_out.at[f], h_sem.at[f]).start()
        pltpu.make_async_copy(gl.at[f], gl_out.at[f], l_sem.at[f]).start()
        for a in range(tiles):
            ra = slice(256 * a, 256 * a + 256)
            for b in range(a, tiles):
                rb = slice(256 * b, 256 * b + 256)
                kacc[ra, rb] += dot3((h[:, ra], l[:, ra]), (h[:, rb], l[:, rb]), TN)

    gram(s_me)

    def take_gram(d):
        f = from_shard(d)
        remote(g_ref.at[at_shard(d)], gland.at[f], g_send.at[d], g_recv.at[d], "shard", at_shard(d)).wait_recv()
        gram(f)

    half = EARLY
    pl.loop(1, half)(take_gram)

    @pl.loop(1, owners)
    def _(d):
        remote(stage.at[at_owner(d)], landed.at[from_owner(d)], a_send.at[d], a_recv.at[d], "owner", at_owner(d)).wait()

    @pl.loop(1, shards)
    def _(d):
        t = at_shard(d)
        stage2[t] = landed[holder_ref[t]]
        remote(stage2.at[t], pland.at[s_me], b_send.at[d], b_recv.at[d], "shard", t).start()

    pland[s_me] = landed[holder_ref[s_me]]
    pl.loop(half, shards)(take_gram)

    for a in range(tiles):
        ra = slice(256 * a, 256 * a + 256)
        for b in range(a, tiles):
            rb = slice(256 * b, 256 * b + 256)
            h, l = split(kacc[ra, rb])
            kh_out[ra, rb] = h
            kl_out[ra, rb] = l
            if b > a:
                h, l = split(kacc[ra, rb].T)
                kh_out[rb, ra] = h
                kl_out[rb, ra] = l

    def project(f):
        p_out[f] = pland[f]
        return dot3((gh[f], gl[f]), split(pland[f]), TN)

    z_out[...] = project(s_me)

    @pl.loop(1, shards)
    def _(d):
        f = from_shard(d)
        remote(stage2.at[at_shard(d)], pland.at[f], b_send.at[d], b_recv.at[d], "shard", at_shard(d)).wait()
        z_out[...] += project(f)

    @pl.loop(1, shards)
    def _(d):
        remote(g_ref.at[at_shard(d)], gland.at[from_shard(d)], g_send.at[d], g_recv.at[d], "shard", at_shard(d)).wait_send()

    @pl.loop(0, shards)
    def _(f):
        pltpu.make_async_copy(gh.at[f], gh_out.at[f], h_sem.at[f]).wait()
        pltpu.make_async_copy(gl.at[f], gl_out.at[f], l_sem.at[f]).wait()


EARLY = 5


def enter(slot_for, holder, gradient, basis):
    shards, rows, cols = gradient.shape
    rank = basis.shape[2]
    owners = slot_for.shape[0]
    sem = pltpu.SemaphoreType.DMA
    smem = pl.BlockSpec(memory_space=pltpu.SMEM)
    vmem = pl.BlockSpec(memory_space=V)
    hbm = pl.BlockSpec(memory_space=pl.ANY)
    return pl.pallas_call(
        functools.partial(enter_body, shards, owners),
        out_shape=(
            jax.ShapeDtypeStruct((shards, rows, cols), BF),
            jax.ShapeDtypeStruct((shards, rows, cols), BF),
            jax.ShapeDtypeStruct((cols, cols), BF),
            jax.ShapeDtypeStruct((cols, cols), BF),
            jax.ShapeDtypeStruct((cols, rank), F32),
            jax.ShapeDtypeStruct((shards, rows, rank), F32),
        ),
        in_specs=[smem, smem, hbm, vmem],
        out_specs=(hbm, hbm, vmem, vmem, vmem, vmem),
        scratch_shapes=[
            V((shards, rows, cols), F32), V((shards, rows, cols), BF), V((shards, rows, cols), BF), V((cols, cols), F32),
            V((owners, rows, rank), F32), V((owners, rows, rank), F32), V((shards, rows, rank), F32), V((shards, rows, rank), F32),
            sem((shards,)), sem((shards,)), sem((owners,)), sem((owners,)), sem((shards,)), sem((shards,)),
            sem, sem((shards,)), sem((shards,)),
        ],
        compiler_params=pltpu.CompilerParams(
            collective_id=0, has_side_effects=True, vmem_limit_bytes=56 * 1024 * 1024
        ),
        name="enter",
    )(slot_for, holder, gradient, basis)


def body(cnt, gh_hbm, gl_hbm, kh_ref, kl_ref, zin_ref, p_ref, pn_ref, pj_ref, gh, gl, z_ref, m_ref, w_ref, c_ref, rx, rh, rl, sems):
    count = cnt[0]
    shards, rows, cols = gh.shape
    rank = p_ref.shape[2]
    load_h = pltpu.make_async_copy(gh_hbm, gh, sems.at[0])
    load_l = pltpu.make_async_copy(gl_hbm, gl, sems.at[1])
    load_h.start()
    load_l.start()
    z_ref[...] = zin_ref[...]

    @pl.loop(0, count)
    def _(it):
        z = split(z_ref[...])
        w_ref[...] = dot3((kh_ref[...], kl_ref[...]), z, NN)
        w = split(w_ref[...])
        c_ref[...] = dot3(z, w, TN)
        factor(c_ref, rx, rh, rl)
        x = (rh[:, rank:], rl[:, rank:])
        z_ref[...] = dot3(w, x, NT)

        @pl.when(it == count - 1)
        def _():
            m_ref[...] = dot3(z, x, NT)

    for c in range(cols // 256):
        t = z_ref[256 * c:256 * c + 256, :].T
        for s in range(shards):
            part = rank // shards
            pj_ref[s, :, 256 * c:256 * c + 256] = t[part * s:part * s + part, :]

    load_h.wait()
    load_l.wait()

    @pl.when(count > 0)
    def _():
        mh, ml = split(m_ref[...])

        @pl.loop(0, shards)
        def _(i):
            pn_ref[i] = dot3((gh[i], gl[i]), (mh, ml), NN)

    @pl.when(count == 0)
    def _():
        pn_ref[...] = p_ref[...]


def refresh(count, gh, gl, kh, kl, z, p):
    shards, rows, cols = gh.shape
    rank = p.shape[2]
    smem = pl.BlockSpec(memory_space=pltpu.SMEM)
    vmem = pl.BlockSpec(memory_space=V)
    hbm = pl.BlockSpec(memory_space=pl.ANY)
    return pl.pallas_call(
        body,
        out_shape=(
            jax.ShapeDtypeStruct((shards, rows, rank), F32),
            jax.ShapeDtypeStruct((shards, rank // shards, cols), F32),
        ),
        in_specs=[smem, hbm, hbm, vmem, vmem, vmem, vmem],
        out_specs=(vmem, vmem),
        scratch_shapes=[
            V((shards, rows, cols), BF), V((shards, rows, cols), BF),
            V((cols, rank), F32), V((cols, rank), F32), V((cols, rank), F32), V((rank, rank), F32),
            V((rank, 2 * rank), F32), V((rank, 2 * rank), BF), V((rank, 2 * rank), BF), pltpu.SemaphoreType.DMA((2,)),
        ],
        compiler_params=pltpu.CompilerParams(vmem_limit_bytes=56 * 1024 * 1024),
        name="refresh",
    )(count, gh, gl, kh, kl, z, p)

BETA_ONE = 0.9
BETA_TWO = 0.99
EPSILON = 1e-08
GALORE_SCALE = 0.25


def update_body(b_ref, n_ref, o_ref):
    o_ref[0] = (GALORE_SCALE * dot3(split(b_ref[0]), split(n_ref[0]), NN)).astype(BF)


def make_update(basis, normed):
    slots, rows, rank = basis.shape
    cols = normed.shape[2]
    return pl.pallas_call(
        update_body,
        grid=(slots,),
        out_shape=jax.ShapeDtypeStruct((slots, rows, cols), BF),
        in_specs=[
            pl.BlockSpec((1, rows, rank), lambda i: (i, 0, 0)),
            pl.BlockSpec((1, rank, cols), lambda i: (i, 0, 0)),
        ],
        out_specs=pl.BlockSpec((1, rows, cols), lambda i: (i, 0, 0)),
        compiler_params=pltpu.CompilerParams(vmem_limit_bytes=32 * 1024 * 1024),
        name="update",
    )(basis, normed)


def pick(array, index):
    return jnp.stack([lax.dynamic_index_in_dim(array, index[i], 0, keepdims=False) for i in range(index.shape[0])])


def on_device(gradient, old_basis, moment_one, moment_two, slot_expert, cost):
    slots = gradient.shape[0]
    owners = lax.axis_size("owner")
    owner_now = lax.axis_index("owner")
    shard_now = lax.axis_index("shard")
    table = slot_expert.reshape(owners, slots)
    mine = lax.dynamic_index_in_dim(table, owner_now, 0, keepdims=False)
    homes = jnp.arange(owners)
    slot_for = jnp.sum(jnp.where(mine[None, :] // slots == homes[:, None], jnp.arange(slots)[None, :], 0), axis=1)
    own_ids = owner_now * slots + jnp.arange(slots)
    hits = table[None, :, :] == own_ids[:, None, None]
    holder = jnp.sum(jnp.where(hits, homes[None, :, None], 0), axis=(1, 2))
    expert_for = jnp.sum(jnp.where(hits, jnp.arange(slots)[:, None, None], 0), axis=(0, 2))
    count = lax.dynamic_slice_in_dim(cost, owner_now * slots + shard_now, 1)

    gh, gl, kh, kl, z, whole = enter(slot_for, holder, gradient, old_basis)
    basis, projected = refresh(count, gh, gl, kh, kl, z, whole)
    result = jnp.concatenate([basis] + [projected[:, :, 256 * c : 256 * c + 256] for c in range(3)], axis=1)
    result = lax.all_to_all(result, "shard", split_axis=0, concat_axis=0, tiled=True)
    result = lax.all_to_all(pick(result, expert_for), "owner", split_axis=0, concat_axis=0, tiled=True)
    result = pick(result, mine // slots)
    basis_slot = result[:, :256, :]
    projected = jnp.concatenate([result[:, 256 + 32 * c : 288 + 32 * c, :] for c in range(3)], axis=2)
    moment_new = BETA_ONE * moment_one + (1.0 - BETA_ONE) * projected
    second_new = BETA_TWO * moment_two + (1.0 - BETA_TWO) * projected * projected
    normed = moment_new / (jnp.sqrt(second_new) + EPSILON)
    update = make_update(basis_slot, lax.all_gather(normed, "shard", axis=1, tiled=True))
    return (basis_slot, moment_new, second_new, update)


def solution(mesh):
    spec = P("owner", "shard", None)
    return jax.shard_map(
        on_device, mesh=mesh, in_specs=(spec,) * 4 + (P(), P()), out_specs=(spec,) * 4, check_vma=False
    )
```

```python
import functools
import jax, jax.numpy as jnp
from jax import lax
from jax.experimental import pallas as pl
from jax.sharding import PartitionSpec as P
from jax.experimental.pallas import tpu as pltpu

BF = jnp.bfloat16
F32 = jnp.float32

def split(x):
    hi = x.astype(BF)
    return hi, (x - hi.astype(F32)).astype(BF)

def mm(a, b, dims):
    return lax.dot_general(a, b, (dims, ((), ())), preferred_element_type=F32)

NN = ((1,), (0,))
TN = ((0,), (0,))
NT = ((1,), (1,))

def dot3(a, b, dims):
    ah, al = a
    bh, bl = b
    return mm(ah, bh, dims) + (mm(ah, bl, dims) + mm(al, bh, dims))

NB = 16

def factor(c_ref, rx, rh, rl):
    n = c_ref.shape[0]
    sub = lax.broadcasted_iota(jnp.int32, (NB, 128), 0)
    row = lax.broadcasted_iota(jnp.int32, (NB, n), 0)
    lane = lax.broadcasted_iota(jnp.int32, (NB, n), 1)
    for p in range(n // NB):
        lo = p * NB
        s_a = c_ref[lo:lo + NB, :]
        s_i = jnp.where(lane == row + lo, 1.0, 0.0)
        if p > 0:
            lh, ll = rh[0:lo, 0:n], rl[0:lo, 0:n]
            ch, cl = lh[:, lo:lo + NB], ll[:, lo:lo + NB]
            s_a = s_a - dot3((ch, cl), (lh, ll), TN)
            xh, xl = rh[0:lo, n:2 * n], rl[0:lo, n:2 * n]
            s_i = s_i - dot3((ch, cl), (xh, xl), TN)
        cols = [jnp.broadcast_to(s_a[:, lo + k:lo + k + 1], (NB, 128)) for k in range(NB)]
        pivots = []
        for j in range(NB):
            d = cols[j][j:j + 1, :]
            r = 1.0 / d
            pivots.append(d)
            m = jnp.where(sub > j, cols[j] * r, 0.0)
            for k in range(j + 1, NB):
                cols[k] = cols[k] - m * cols[k][j:j + 1, :]
            m2 = jnp.concatenate([m] * (n // 128), axis=1)
            s_a = s_a - m2 * s_a[j:j + 1, :]
            s_i = s_i - m2 * s_i[j:j + 1, :]
        piv = jnp.concatenate(pivots, axis=0)
        scale = lax.rsqrt(piv)
        scale = jnp.concatenate([scale] * (n // 128), axis=1)
        r_a = jnp.where(lane >= lo + row, s_a * scale, 0.0)
        r_i = s_i * scale
        out = jnp.concatenate([r_a, r_i], axis=1)
        rx[lo:lo + NB, :] = out
        hi = out.astype(BF)
        rh[lo:lo + NB, :] = hi
        rl[lo:lo + NB, :] = (out - hi.astype(F32)).astype(BF)

MESH = pl.DeviceIdType.MESH
V = pltpu.VMEM


def greet(groups):
    barrier = pltpu.get_barrier_semaphore()
    total = 0
    for axis, size in groups:
        me = lax.axis_index(axis)

        @pl.loop(1, size)
        def _(d):
            pl.semaphore_signal(barrier, inc=1, device_id={axis: lax.rem(me + d, size)}, device_id_type=MESH)

        total += size - 1
    pl.semaphore_wait(barrier, total)


def remote(src, dst, send, recv, axis, target):
    return pltpu.make_async_remote_copy(
        src_ref=src, dst_ref=dst, send_sem=send, recv_sem=recv, device_id={axis: target}, device_id_type=MESH
    )


def enter_body(shards, owners, slot_ref, holder_ref, g_ref, b_ref, gh_out, gl_out, kh_out, kl_out, z_out, p_out,
               gland, gh, gl, kacc, stage, landed, stage2, pland,
               g_send, g_recv, a_send, a_recv, b_send, b_recv, own_sem, h_sem, l_sem):
    s_me = lax.axis_index("shard")
    o_me = lax.axis_index("owner")
    greet((("shard", shards), ("owner", owners)))

    def at_shard(d):
        return lax.rem(s_me + d, shards)

    def from_shard(d):
        return lax.rem(s_me - d + shards, shards)

    def at_owner(d):
        return lax.rem(o_me + d, owners)

    def from_owner(d):
        return lax.rem(o_me - d + owners, owners)

    own = pltpu.make_async_copy(g_ref.at[s_me], gland.at[s_me], own_sem)
    own.start()

    @pl.loop(1, owners)
    def _(d):
        t = at_owner(d)
        stage[t] = b_ref[slot_ref[t]]
        remote(stage.at[t], landed.at[o_me], a_send.at[d], a_recv.at[d], "owner", t).start()

    @pl.loop(1, shards)
    def _(d):
        t = at_shard(d)
        remote(g_ref.at[t], gland.at[s_me], g_send.at[d], g_recv.at[d], "shard", t).start()

    landed[o_me] = b_ref[slot_ref[o_me]]
    kacc[...] = jnp.zeros_like(kacc)
    own.wait()
    tiles = kacc.shape[0] // 256

    def gram(f):
        h, l = split(gland[f])
        gh[f] = h
        gl[f] = l
        pltpu.make_async_copy(gh.at[f], gh_out.at[f], h_sem.at[f]).start()
        pltpu.make_async_copy(gl.at[f], gl_out.at[f], l_sem.at[f]).start()
        for a in range(tiles):
            ra = slice(256 * a, 256 * a + 256)
            for b in range(a, tiles):
                rb = slice(256 * b, 256 * b + 256)
                kacc[ra, rb] += dot3((h[:, ra], l[:, ra]), (h[:, rb], l[:, rb]), TN)

    gram(s_me)

    def take_gram(d):
        f = from_shard(d)
        remote(g_ref.at[at_shard(d)], gland.at[f], g_send.at[d], g_recv.at[d], "shard", at_shard(d)).wait_recv()
        gram(f)

    half = EARLY
    pl.loop(1, half)(take_gram)

    @pl.loop(1, owners)
    def _(d):
        remote(stage.at[at_owner(d)], landed.at[from_owner(d)], a_send.at[d], a_recv.at[d], "owner", at_owner(d)).wait()

    @pl.loop(1, shards)
    def _(d):
        t = at_shard(d)
        stage2[t] = landed[holder_ref[t]]
        remote(stage2.at[t], pland.at[s_me], b_send.at[d], b_recv.at[d], "shard", t).start()

    pland[s_me] = landed[holder_ref[s_me]]
    pl.loop(half, shards)(take_gram)

    for a in range(tiles):
        ra = slice(256 * a, 256 * a + 256)
        for b in range(a, tiles):
            rb = slice(256 * b, 256 * b + 256)
            h, l = split(kacc[ra, rb])
            kh_out[ra, rb] = h
            kl_out[ra, rb] = l
            if b > a:
                h, l = split(kacc[ra, rb].T)
                kh_out[rb, ra] = h
                kl_out[rb, ra] = l

    def project(f):
        p_out[f] = pland[f]
        return dot3((gh[f], gl[f]), split(pland[f]), TN)

    z_out[...] = project(s_me)

    @pl.loop(1, shards)
    def _(d):
        f = from_shard(d)
        remote(stage2.at[at_shard(d)], pland.at[f], b_send.at[d], b_recv.at[d], "shard", at_shard(d)).wait()
        z_out[...] += project(f)

    @pl.loop(1, shards)
    def _(d):
        remote(g_ref.at[at_shard(d)], gland.at[from_shard(d)], g_send.at[d], g_recv.at[d], "shard", at_shard(d)).wait_send()

    @pl.loop(0, shards)
    def _(f):
        pltpu.make_async_copy(gh.at[f], gh_out.at[f], h_sem.at[f]).wait()
        pltpu.make_async_copy(gl.at[f], gl_out.at[f], l_sem.at[f]).wait()


EARLY = 5


def enter(slot_for, holder, gradient, basis):
    shards, rows, cols = gradient.shape
    rank = basis.shape[2]
    owners = slot_for.shape[0]
    sem = pltpu.SemaphoreType.DMA
    smem = pl.BlockSpec(memory_space=pltpu.SMEM)
    vmem = pl.BlockSpec(memory_space=V)
    hbm = pl.BlockSpec(memory_space=pl.ANY)
    return pl.pallas_call(
        functools.partial(enter_body, shards, owners),
        out_shape=(
            jax.ShapeDtypeStruct((shards, rows, cols), BF),
            jax.ShapeDtypeStruct((shards, rows, cols), BF),
            jax.ShapeDtypeStruct((cols, cols), BF),
            jax.ShapeDtypeStruct((cols, cols), BF),
            jax.ShapeDtypeStruct((cols, rank), F32),
            jax.ShapeDtypeStruct((shards, rows, rank), F32),
        ),
        in_specs=[smem, smem, hbm, vmem],
        out_specs=(hbm, hbm, vmem, vmem, vmem, vmem),
        scratch_shapes=[
            V((shards, rows, cols), F32), V((shards, rows, cols), BF), V((shards, rows, cols), BF), V((cols, cols), F32),
            V((owners, rows, rank), F32), V((owners, rows, rank), F32), V((shards, rows, rank), F32), V((shards, rows, rank), F32),
            sem((shards,)), sem((shards,)), sem((owners,)), sem((owners,)), sem((shards,)), sem((shards,)),
            sem, sem((shards,)), sem((shards,)),
        ],
        compiler_params=pltpu.CompilerParams(
            collective_id=0, has_side_effects=True, vmem_limit_bytes=56 * 1024 * 1024
        ),
        name="enter",
    )(slot_for, holder, gradient, basis)


def body(cnt, gh_hbm, gl_hbm, kh_ref, kl_ref, zin_ref, p_ref, pn_ref, pj_ref, gh, gl, z_ref, m_ref, w_ref, c_ref, rx, rh, rl, sems):
    count = cnt[0]
    shards, rows, cols = gh.shape
    rank = p_ref.shape[2]
    load_h = pltpu.make_async_copy(gh_hbm, gh, sems.at[0])
    load_l = pltpu.make_async_copy(gl_hbm, gl, sems.at[1])
    load_h.start()
    load_l.start()
    z_ref[...] = zin_ref[...]

    @pl.loop(0, count)
    def _(it):
        z = split(z_ref[...])
        w_ref[...] = dot3((kh_ref[...], kl_ref[...]), z, NN)
        w = split(w_ref[...])
        c_ref[...] = dot3(z, w, TN)
        factor(c_ref, rx, rh, rl)
        x = (rh[:, rank:], rl[:, rank:])
        z_ref[...] = dot3(w, x, NT)

        @pl.when(it == count - 1)
        def _():
            m_ref[...] = dot3(z, x, NT)

    for c in range(cols // 256):
        t = z_ref[256 * c:256 * c + 256, :].T
        for s in range(shards):
            part = rank // shards
            pj_ref[s, :, 256 * c:256 * c + 256] = t[part * s:part * s + part, :]

    load_h.wait()
    load_l.wait()

    @pl.when(count > 0)
    def _():
        mh, ml = split(m_ref[...])

        @pl.loop(0, shards)
        def _(i):
            pn_ref[i] = dot3((gh[i], gl[i]), (mh, ml), NN)

    @pl.when(count == 0)
    def _():
        pn_ref[...] = p_ref[...]


def refresh(count, gh, gl, kh, kl, z, p):
    shards, rows, cols = gh.shape
    rank = p.shape[2]
    smem = pl.BlockSpec(memory_space=pltpu.SMEM)
    vmem = pl.BlockSpec(memory_space=V)
    hbm = pl.BlockSpec(memory_space=pl.ANY)
    return pl.pallas_call(
        body,
        out_shape=(
            jax.ShapeDtypeStruct((shards, rows, rank), F32),
            jax.ShapeDtypeStruct((shards, rank // shards, cols), F32),
        ),
        in_specs=[smem, hbm, hbm, vmem, vmem, vmem, vmem],
        out_specs=(vmem, vmem),
        scratch_shapes=[
            V((shards, rows, cols), BF), V((shards, rows, cols), BF),
            V((cols, rank), F32), V((cols, rank), F32), V((cols, rank), F32), V((rank, rank), F32),
            V((rank, 2 * rank), F32), V((rank, 2 * rank), BF), V((rank, 2 * rank), BF), pltpu.SemaphoreType.DMA((2,)),
        ],
        compiler_params=pltpu.CompilerParams(vmem_limit_bytes=56 * 1024 * 1024),
        name="refresh",
    )(count, gh, gl, kh, kl, z, p)


BETA_ONE = 0.9
BETA_TWO = 0.99
EPSILON = 1e-08
GALORE_SCALE = 0.25
CHUNKS = 2


def leave_body(shards, owners, expert_ref, home_ref, pn_ref, pj_ref, one_ref, two_ref,
               basis_out, one_out, two_out, update_out,
               pj1, pj_stage, pj2, pn1a, pn1b, pn_stage, pn2a, pn2b, normed, nh, nl,
               j_send, j_recv, jo_send, jo_recv, p_send, p_recv, po_send, po_recv, n_send, n_recv, f_send, f_recv, own_sem):
    s_me = lax.axis_index("shard")
    o_me = lax.axis_index("owner")
    pn1, pn2 = (pn1a, pn1b), (pn2a, pn2b)
    chunk = pn1a.shape[1]
    slots = one_ref.shape[0]
    greet((("shard", shards), ("owner", owners)))

    def at_shard(d):
        return lax.rem(s_me + d, shards)

    def from_shard(d):
        return lax.rem(s_me - d + shards, shards)

    def at_owner(d):
        return lax.rem(o_me + d, owners)

    def from_owner(d):
        return lax.rem(o_me - d + owners, owners)

    def rows(c):
        return slice(c * chunk, (c + 1) * chunk)

    own_pj = pltpu.make_async_copy(pj_ref.at[s_me], pj1.at[s_me], own_sem.at[CHUNKS])
    own_pj.start()
    own_pn = [pltpu.make_async_copy(pn_ref.at[s_me, rows(c)], pn1[c].at[s_me], own_sem.at[c]) for c in range(CHUNKS)]

    @pl.loop(1, shards)
    def _(d):
        t = at_shard(d)
        remote(pj_ref.at[t], pj1.at[s_me], j_send.at[d], j_recv.at[d], "shard", t).start()

    for c in range(CHUNKS):
        own_pn[c].start()

        @pl.loop(1, shards)
        def _(d):
            t = at_shard(d)
            remote(pn_ref.at[t, rows(c)], pn1[c].at[s_me], p_send.at[c, d], p_recv.at[c, d], "shard", t).start()

    own_pj.wait()

    @pl.loop(1, shards)
    def _(d):
        remote(pj_ref.at[at_shard(d)], pj1.at[from_shard(d)], j_send.at[d], j_recv.at[d], "shard", at_shard(d)).wait()

    @pl.loop(1, owners)
    def _(d):
        t = at_owner(d)
        pj_stage[t] = pj1[expert_ref[t]]
        remote(pj_stage.at[t], pj2.at[o_me], jo_send.at[d], jo_recv.at[d], "owner", t).start()

    pj2[o_me] = pj1[expert_ref[o_me]]

    for c in range(CHUNKS):
        own_pn[c].wait()

        @pl.loop(1, shards)
        def _(d):
            t = at_shard(d)
            remote(pn_ref.at[t, rows(c)], pn1[c].at[from_shard(d)], p_send.at[c, d], p_recv.at[c, d], "shard", t).wait()

        @pl.loop(1, owners)
        def _(d):
            t = at_owner(d)
            pn_stage[c, t] = pn1[c][expert_ref[t]]
            remote(pn_stage.at[c, t], pn2[c].at[o_me], po_send.at[c, d], po_recv.at[c, d], "owner", t).start()

        pn2[c][o_me] = pn1[c][expert_ref[o_me]]

    @pl.loop(1, owners)
    def _(d):
        remote(pj_stage.at[at_owner(d)], pj2.at[from_owner(d)], jo_send.at[d], jo_recv.at[d], "owner", at_owner(d)).wait()

    @pl.loop(0, slots)
    def _(j):
        projected = pj2[home_ref[j]]
        one = BETA_ONE * one_ref[j] + (1.0 - BETA_ONE) * projected
        two = BETA_TWO * two_ref[j] + (1.0 - BETA_TWO) * projected * projected
        one_out[j] = one
        two_out[j] = two
        normed[s_me, j] = one / (jnp.sqrt(two) + EPSILON)

    other = s_me + 1 - 2 * lax.rem(s_me, 2)
    chips = shards // 2

    @pl.loop(1, chips)
    def _(k):
        t = at_shard(2 * k)
        remote(normed.at[s_me], normed.at[s_me], n_send.at[k], n_recv.at[k], "shard", t).start()

    remote(normed.at[s_me], normed.at[s_me], f_send.at[0], f_recv.at[0], "shard", other).start()

    @pl.loop(1, chips)
    def _(k):
        f = from_shard(2 * k)
        remote(normed.at[s_me], normed.at[f], n_send.at[k], n_recv.at[k], "shard", at_shard(2 * k)).wait()
        remote(normed.at[f], normed.at[f], f_send.at[k], f_recv.at[k], "shard", other).start()

    @pl.loop(0, chips)
    def _(k):
        f = from_shard(2 * k)
        g = lax.rem(other - 2 * k + shards, shards)
        remote(normed.at[f], normed.at[g], f_send.at[k], f_recv.at[k], "shard", other).wait()

    @pl.loop(0, slots)
    def _(j):
        h, l = split(normed[:, j].reshape(nh.shape[1], nh.shape[2]))
        nh[j] = h
        nl[j] = l

    for c in range(CHUNKS):

        @pl.loop(1, owners)
        def _(d):
            t = at_owner(d)
            remote(pn_stage.at[c, t], pn2[c].at[from_owner(d)], po_send.at[c, d], po_recv.at[c, d], "owner", t).wait()

        @pl.loop(0, slots)
        def _(j):
            b = pn2[c][home_ref[j]]
            basis_out[j, rows(c)] = b
            update_out[j, rows(c)] = (GALORE_SCALE * dot3(split(b), (nh[j], nl[j]), NN)).astype(BF)


def leave(expert_for, home, pn, pj, one, two):
    shards, rows, rank = pn.shape
    part, cols = pj.shape[1:]
    slots = one.shape[0]
    owners = expert_for.shape[0]
    chunk = rows // CHUNKS
    dma = pltpu.SemaphoreType.DMA
    smem = pl.BlockSpec(memory_space=pltpu.SMEM)
    vmem = pl.BlockSpec(memory_space=V)
    hbm = pl.BlockSpec(memory_space=pl.ANY)
    return pl.pallas_call(
        functools.partial(leave_body, shards, owners),
        out_shape=(
            jax.ShapeDtypeStruct((slots, rows, rank), F32),
            jax.ShapeDtypeStruct(one.shape, F32),
            jax.ShapeDtypeStruct(two.shape, F32),
            jax.ShapeDtypeStruct((slots, rows, cols), BF),
        ),
        in_specs=[smem, smem, hbm, hbm, vmem, vmem],
        out_specs=(vmem,) * 4,
        scratch_shapes=[
            V((shards, part, cols), F32), V((owners, part, cols), F32), V((owners, part, cols), F32),
            V((shards, chunk, rank), F32), V((shards, chunk, rank), F32), V((CHUNKS, owners, chunk, rank), F32),
            V((owners, chunk, rank), F32), V((owners, chunk, rank), F32),
            V((shards, slots, part, cols), F32), V((slots, rank, cols), BF), V((slots, rank, cols), BF),
            dma((shards,)), dma((shards,)), dma((owners,)), dma((owners,)),
            dma((CHUNKS, shards)), dma((CHUNKS, shards)), dma((CHUNKS, owners)), dma((CHUNKS, owners)),
            dma((shards // 2,)), dma((shards // 2,)), dma((shards // 2,)), dma((shards // 2,)), dma((CHUNKS + 1,)),
        ],
        compiler_params=pltpu.CompilerParams(
            collective_id=1, has_side_effects=True, vmem_limit_bytes=56 * 1024 * 1024
        ),
        name="leave",
    )(expert_for, home, pn, pj, one, two)


def on_device(gradient, old_basis, moment_one, moment_two, slot_expert, cost):
    slots = gradient.shape[0]
    owners = lax.axis_size("owner")
    owner_now = lax.axis_index("owner")
    shard_now = lax.axis_index("shard")
    table = slot_expert.reshape(owners, slots)
    mine = lax.dynamic_index_in_dim(table, owner_now, 0, keepdims=False)
    homes = jnp.arange(owners)
    slot_for = jnp.sum(jnp.where(mine[None, :] // slots == homes[:, None], jnp.arange(slots)[None, :], 0), axis=1)
    own_ids = owner_now * slots + jnp.arange(slots)
    hits = table[None, :, :] == own_ids[:, None, None]
    holder = jnp.sum(jnp.where(hits, homes[None, :, None], 0), axis=(1, 2))
    expert_for = jnp.sum(jnp.where(hits, jnp.arange(slots)[:, None, None], 0), axis=(0, 2))
    count = lax.dynamic_slice_in_dim(cost, owner_now * slots + shard_now, 1)

    gh, gl, kh, kl, z, whole = enter(slot_for, holder, gradient, old_basis)
    basis, projected = refresh(count, gh, gl, kh, kl, z, whole)
    return tuple(leave(expert_for, mine // slots, basis, projected, moment_one, moment_two))


def solution(mesh):
    spec = P("owner", "shard", None)
    return jax.shard_map(
        on_device, mesh=mesh, in_specs=(spec,) * 4 + (P(), P()), out_specs=(spec,) * 4, check_vma=False
    )
```

```python
import functools
import jax, jax.numpy as jnp
from jax import lax
from jax.experimental import pallas as pl
from jax.sharding import PartitionSpec as P
from jax.experimental.pallas import tpu as pltpu

BF = jnp.bfloat16
F32 = jnp.float32

def split(x):
    hi = x.astype(BF)
    return hi, (x - hi.astype(F32)).astype(BF)

def mm(a, b, dims):
    return lax.dot_general(a, b, (dims, ((), ())), preferred_element_type=F32)

NN = ((1,), (0,))
TN = ((0,), (0,))
NT = ((1,), (1,))

def dot3(a, b, dims):
    ah, al = a
    bh, bl = b
    return mm(ah, bh, dims) + (mm(ah, bl, dims) + mm(al, bh, dims))

PANEL, GROUP = 32, 16


def factor(c_ref, xh, xl, ls, rs):
    nb, sub_nb = PANEL, GROUP
    n = c_ref.shape[0]
    for p in range(n // nb):
        lo = p * nb
        need = [h for h in range(4) if (h < 2 and h * 128 + 128 > lo) or (h >= 2 and (h - 2) * 128 < lo + nb)]
        sub = lax.broadcasted_iota(jnp.int32, (nb, 128), 0)
        s = {}
        for h in need:
            if h < 2:
                s[h] = c_ref[lo:lo + nb, 128 * h:128 * h + 128]
            else:
                l = lax.broadcasted_iota(jnp.int32, (nb, 128), 1) + 128 * (h - 2)
                s[h] = jnp.where(l == sub + lo, 1.0, 0.0)
        a0, a1 = need[0] * 128, need[-1] * 128 + 128
        cuts = []
        if p > 1:
            cuts.append((0, 3 * (lo - nb)))
        if p > 0:
            cuts.append((3 * (lo - nb), 3 * lo))
        for (x, y) in cuts:
            d = mm(ls[x:y, lo:lo + nb], rs[x:y, a0:a1], TN)
            for h in need:
                s[h] = s[h] - d[:, 128 * h - a0:128 * h - a0 + 128]
        hd = lo // 128
        off = lo - hd * 128
        pivots = []
        done = []
        for g in range(nb // sub_nb):
            b = g * sub_nb
            rows = nb - b
            rsub = lax.broadcasted_iota(jnp.int32, (rows, 128), 0)
            cols = [jnp.broadcast_to(s[hd][:, off + b + k:off + b + k + 1], (rows, 128)) for k in range(sub_nb)]
            for j in range(sub_nb):
                d = cols[j][j:j + 1, :]
                r = 1.0 / d
                pivots.append(d)
                m = jnp.where(rsub > j, cols[j] * r, 0.0)
                for k in range(j + 1, sub_nb):
                    cols[k] = cols[k] - m * cols[k][j:j + 1, :]
                for h in need:
                    s[h] = s[h] - m * s[h][j:j + 1, :]
            done.append({h: s[h][0:sub_nb] for h in need})
            if rows > sub_nb:
                s = {h: s[h][sub_nb:] for h in need}
        scale = lax.rsqrt(jnp.concatenate(pivots, axis=0))
        for h in range(4):
            if h not in need:
                o = jnp.zeros((nb, 128), F32)
            else:
                o = jnp.concatenate([t[h] for t in done], axis=0) * scale
                if h == hd:
                    l = lax.broadcasted_iota(jnp.int32, (nb, 128), 1) + 128 * h
                    o = jnp.where(l >= sub + lo, o, 0.0)
            cs = slice(128 * h, 128 * h + 128)
            hi = o.astype(BF)
            lw = (o - hi.astype(F32)).astype(BF)
            if h >= 2:
                xs = slice(128 * (h - 2), 128 * (h - 2) + 128)
                xh[lo:lo + nb, xs] = hi
                xl[lo:lo + nb, xs] = lw
            b = 3 * lo
            rs[b:b + nb, cs] = hi
            rs[b + nb:b + 2 * nb, cs] = lw
            rs[b + 2 * nb:b + 3 * nb, cs] = hi
            if h < 2:
                ls[b:b + nb, cs] = hi
                ls[b + nb:b + 2 * nb, cs] = hi
                ls[b + 2 * nb:b + 3 * nb, cs] = lw


MESH = pl.DeviceIdType.MESH
V = pltpu.VMEM


def greet(groups):
    barrier = pltpu.get_barrier_semaphore()
    total = 0
    for axis, size in groups:
        me = lax.axis_index(axis)

        @pl.loop(1, size)
        def _(d):
            pl.semaphore_signal(barrier, inc=1, device_id={axis: lax.rem(me + d, size)}, device_id_type=MESH)

        total += size - 1
    pl.semaphore_wait(barrier, total)


def remote(src, dst, send, recv, axis, target):
    return pltpu.make_async_remote_copy(
        src_ref=src, dst_ref=dst, send_sem=send, recv_sem=recv, device_id={axis: target}, device_id_type=MESH
    )


def slot_at(table, owner, slots, home):
    found = 0
    for j in range(slots):
        found = jnp.where(lax.div(table[owner * slots + j], slots) == home, j, found)
    return found


def enter_body(shards, owners, table, g_ref, b_ref, gh_out, gl_out, kh_out, kl_out, z_out, p_out,
               gland, gh, gl, kacc, kh, kl, stage, landed, stage2, pland,
               g_send, g_recv, a_send, a_recv, b_send, b_recv, own_sem, h_sem, l_sem, p_sem, k_sem):
    s_me = lax.axis_index("shard")
    o_me = lax.axis_index("owner")
    greet((("shard", shards), ("owner", owners)))

    def at_shard(d):
        return lax.rem(s_me + d, shards)

    def from_shard(d):
        return lax.rem(s_me - d + shards, shards)

    def at_owner(d):
        return lax.rem(o_me + d, owners)

    def from_owner(d):
        return lax.rem(o_me - d + owners, owners)

    own = pltpu.make_async_copy(g_ref.at[s_me], gland.at[s_me], own_sem)
    own.start()

    slots = shards

    @pl.loop(1, owners)
    def _(d):
        t = at_owner(d)
        stage[t] = b_ref[slot_at(table, o_me, slots, t)]
        remote(stage.at[t], landed.at[o_me], a_send.at[d], a_recv.at[d], "owner", t).start()

    @pl.loop(1, shards)
    def _(d):
        t = at_shard(d)
        remote(g_ref.at[t], gland.at[s_me], g_send.at[d], g_recv.at[d], "shard", t).start()

    landed[o_me] = b_ref[slot_at(table, o_me, slots, o_me)]
    kacc[...] = jnp.zeros_like(kacc)
    own.wait()
    tiles = kacc.shape[0] // 256

    def gram(f):
        h, l = split(gland[f])
        gh[f] = h
        gl[f] = l
        pltpu.make_async_copy(gh.at[f], gh_out.at[f], h_sem.at[f]).start()
        pltpu.make_async_copy(gl.at[f], gl_out.at[f], l_sem.at[f]).start()
        for a in range(tiles):
            ra = slice(256 * a, 256 * a + 256)
            for b in range(a, tiles):
                rb = slice(256 * b, 256 * b + 256)
                kacc[ra, rb] += dot3((h[:, ra], l[:, ra]), (h[:, rb], l[:, rb]), TN)

    gram(s_me)

    def take_gram(d):
        f = from_shard(d)
        remote(g_ref.at[at_shard(d)], gland.at[f], g_send.at[d], g_recv.at[d], "shard", at_shard(d)).wait_recv()
        gram(f)

    half = EARLY
    pl.loop(1, half)(take_gram)

    @pl.loop(1, owners)
    def _(d):
        remote(stage.at[at_owner(d)], landed.at[from_owner(d)], a_send.at[d], a_recv.at[d], "owner", at_owner(d)).wait()

    def holder(i):
        def add(o, found):
            for j in range(slots):
                found = jnp.where(table[o * slots + j] == o_me * slots + i, o, found)
            return found

        return lax.fori_loop(0, owners, add, 0)

    @pl.loop(1, shards)
    def _(d):
        t = at_shard(d)
        stage2[t] = landed[holder(t)]
        remote(stage2.at[t], pland.at[s_me], b_send.at[d], b_recv.at[d], "shard", t).start()

    pland[s_me] = landed[holder(s_me)]
    pl.loop(half, shards)(take_gram)

    for a in range(tiles):
        ra = slice(256 * a, 256 * a + 256)
        for b in range(a, tiles):
            rb = slice(256 * b, 256 * b + 256)
            h, l = split(kacc[ra, rb])
            kh[ra, rb] = h
            kl[ra, rb] = l
            if b > a:
                h, l = split(kacc[ra, rb].T)
                kh[rb, ra] = h
                kl[rb, ra] = l

    save_k = (pltpu.make_async_copy(kh, kh_out, k_sem.at[0]), pltpu.make_async_copy(kl, kl_out, k_sem.at[1]))
    for copy in save_k:
        copy.start()

    def project(f):
        pltpu.make_async_copy(pland.at[f], p_out.at[f], p_sem.at[f]).start()
        return dot3((gh[f], gl[f]), split(pland[f]), TN)

    z_out[...] = project(s_me)

    @pl.loop(1, shards)
    def _(d):
        f = from_shard(d)
        remote(stage2.at[at_shard(d)], pland.at[f], b_send.at[d], b_recv.at[d], "shard", at_shard(d)).wait()
        z_out[...] += project(f)

    @pl.loop(1, shards)
    def _(d):
        remote(g_ref.at[at_shard(d)], gland.at[from_shard(d)], g_send.at[d], g_recv.at[d], "shard", at_shard(d)).wait_send()

    @pl.loop(0, shards)
    def _(f):
        pltpu.make_async_copy(gh.at[f], gh_out.at[f], h_sem.at[f]).wait()
        pltpu.make_async_copy(gl.at[f], gl_out.at[f], l_sem.at[f]).wait()
        pltpu.make_async_copy(pland.at[f], p_out.at[f], p_sem.at[f]).wait()

    for copy in save_k:
        copy.wait()


EARLY = 5


def enter(table, gradient, basis):
    shards, rows, cols = gradient.shape
    rank = basis.shape[2]
    owners = table.shape[0] // basis.shape[0]
    sem = pltpu.SemaphoreType.DMA
    smem = pl.BlockSpec(memory_space=pltpu.SMEM)
    vmem = pl.BlockSpec(memory_space=V)
    hbm = pl.BlockSpec(memory_space=pl.ANY)
    return pl.pallas_call(
        functools.partial(enter_body, shards, owners),
        out_shape=(
            jax.ShapeDtypeStruct((shards, rows, cols), BF),
            jax.ShapeDtypeStruct((shards, rows, cols), BF),
            jax.ShapeDtypeStruct((cols, cols), BF),
            jax.ShapeDtypeStruct((cols, cols), BF),
            jax.ShapeDtypeStruct((cols, rank), F32),
            jax.ShapeDtypeStruct((shards, rows, rank), F32),
        ),
        in_specs=[smem, hbm, vmem],
        out_specs=(hbm, hbm, hbm, hbm, vmem, hbm),
        scratch_shapes=[
            V((shards, rows, cols), F32), V((shards, rows, cols), BF), V((shards, rows, cols), BF), V((cols, cols), F32), V((cols, cols), BF), V((cols, cols), BF),
            V((owners, rows, rank), F32), V((owners, rows, rank), F32), V((shards, rows, rank), F32), V((shards, rows, rank), F32),
            sem((shards,)), sem((shards,)), sem((owners,)), sem((owners,)), sem((shards,)), sem((shards,)),
            sem, sem((shards,)), sem((shards,)), sem((shards,)), sem((2,)),
        ],
        compiler_params=pltpu.CompilerParams(
            collective_id=0, has_side_effects=True, vmem_limit_bytes=56 * 1024 * 1024
        ),
        name="enter",
    )(table, gradient, basis)


def body(table, cost, kh_ref, kl_ref, zin_ref, mh_ref, ml_ref, pj_ref, keep_ref, home_ref, z_ref, w_ref, c_ref, xh, xl, ls, rs):
    s_me = lax.axis_index("shard")
    o_me = lax.axis_index("owner")
    shards, part, cols = pj_ref.shape
    rank = zin_ref.shape[1]
    count = cost[o_me * shards + s_me]
    keep_ref[0] = jnp.where(count > 0, 0.0, 1.0)
    for j in range(shards):
        home_ref[j] = lax.div(table[o_me * shards + j], shards)
    z_ref[...] = zin_ref[...]

    @pl.loop(0, count)
    def _(it):
        z = split(z_ref[...])
        w_ref[...] = dot3((kh_ref[...], kl_ref[...]), z, NN)
        w = split(w_ref[...])
        c_ref[...] = dot3(z, w, TN)
        factor(c_ref, xh, xl, ls, rs)
        x = (xh[...], xl[...])
        z_ref[...] = dot3(w, x, NT)

        @pl.when(it == count - 1)
        def _():
            h, l = split(dot3(z, x, NT))
            mh_ref[...] = h
            ml_ref[...] = l

    @pl.when(count == 0)
    def _():
        mh_ref[...] = jnp.zeros_like(mh_ref)
        ml_ref[...] = jnp.zeros_like(ml_ref)

    for c in range(cols // 256):
        t = z_ref[256 * c:256 * c + 256, :].T
        for s in range(shards):
            pj_ref[s, :, 256 * c:256 * c + 256] = t[part * s:part * s + part, :]


def refresh(table, cost, shards, kh, kl, z):
    cols, rank = z.shape
    smem = pl.BlockSpec(memory_space=pltpu.SMEM)
    vmem = pl.BlockSpec(memory_space=V)
    return pl.pallas_call(
        body,
        out_shape=(
            jax.ShapeDtypeStruct((cols, rank), BF),
            jax.ShapeDtypeStruct((cols, rank), BF),
            jax.ShapeDtypeStruct((shards, rank // shards, cols), F32),
            jax.ShapeDtypeStruct((1,), F32),
            jax.ShapeDtypeStruct((shards,), jnp.int32),
        ),
        in_specs=[smem, smem, vmem, vmem, vmem],
        out_specs=(vmem, vmem, vmem, smem, smem),
        scratch_shapes=[
            V((cols, rank), F32), V((cols, rank), F32), V((rank, rank), F32), V((rank, rank), BF), V((rank, rank), BF),
            V((3 * rank, rank), BF), V((3 * rank, 2 * rank), BF),
        ],
        compiler_params=pltpu.CompilerParams(vmem_limit_bytes=56 * 1024 * 1024),
        name="refresh",
    )(table, cost, kh, kl, z)


BETA_ONE = 0.9
BETA_TWO = 0.99
EPSILON = 1e-08
GALORE_SCALE = 0.25
CHUNKS = 2


def adam(one, two, projected):
    one = BETA_ONE * one + (1.0 - BETA_ONE) * projected
    two = BETA_TWO * two + (1.0 - BETA_TWO) * projected * projected
    return one, two


def leave_body(shards, owners, table, keep_ref, mh_ref, ml_ref, pj_ref, gh_hbm, gl_hbm, p_hbm, one_ref, two_ref,
               back_a, back_b, normed_out, proj_out,
               gh, gl, p_in, pn, pj1, pj_stage, pj2, pn1a, pn1b, pn_stage, normed,
               h_sem, l_sem, i_sem, j_send, j_recv, jo_send, jo_recv, p_send, p_recv, po_send, po_recv,
               n_send, n_recv, f_send, f_recv, own_sem):
    s_me = lax.axis_index("shard")
    o_me = lax.axis_index("owner")
    slots = one_ref.shape[0]
    pn1, back = (pn1a, pn1b), (back_a, back_b)
    chunk = pn1a.shape[1]

    def at_shard(d):
        return lax.rem(s_me + d, shards)

    def from_shard(d):
        return lax.rem(s_me - d + shards, shards)

    def at_owner(d):
        return lax.rem(o_me + d, owners)

    def from_owner(d):
        return lax.rem(o_me - d + owners, owners)

    def rows(c):
        return slice(c * chunk, (c + 1) * chunk)

    def loads(t):
        return (
            pltpu.make_async_copy(gh_hbm.at[t], gh.at[t], h_sem.at[t]),
            pltpu.make_async_copy(gl_hbm.at[t], gl.at[t], l_sem.at[t]),
            pltpu.make_async_copy(p_hbm.at[t], p_in.at[t], i_sem.at[t]),
        )

    @pl.loop(1, shards + 1)
    def _(d):
        for copy in loads(at_shard(d)):
            copy.start()

    greet((("shard", shards), ("owner", owners)))

    @pl.loop(1, shards)
    def _(d):
        t = at_shard(d)
        remote(pj_ref.at[t], pj1.at[s_me], j_send.at[d], j_recv.at[d], "shard", t).start()

    pj1[s_me] = pj_ref[s_me]
    keep = keep_ref[0]

    def basis_rows(t, c):
        return dot3((gh[t, rows(c)], gl[t, rows(c)]), (mh_ref[...], ml_ref[...]), NN) + keep * p_in[t, rows(c)]

    for c in range(CHUNKS):

        @pl.loop(1, shards)
        def _(d):
            t = at_shard(d)
            if c == 0:
                for copy in loads(t):
                    copy.wait()
            pn[c, t] = basis_rows(t, c)
            remote(pn.at[c, t], pn1[c].at[s_me], p_send.at[c, d], p_recv.at[c, d], "shard", t).start()

        if c == 0:
            for copy in loads(s_me):
                copy.wait()
        pn1[c][s_me] = basis_rows(s_me, c)

    def expert_at(owner):
        found = 0
        for j in range(slots):
            e = table[owner * slots + j]
            found = jnp.where(lax.div(e, slots) == o_me, lax.rem(e, slots), found)
        return found

    @pl.loop(1, shards)
    def _(d):
        remote(pj_ref.at[at_shard(d)], pj1.at[from_shard(d)], j_send.at[d], j_recv.at[d], "shard", at_shard(d)).wait()

    @pl.loop(1, owners)
    def _(d):
        t = at_owner(d)
        pj_stage[t] = pj1[expert_at(t)]
        remote(pj_stage.at[t], pj2.at[o_me], jo_send.at[d], jo_recv.at[d], "owner", t).start()

    pj2[o_me] = pj1[expert_at(o_me)]
    own = []
    for c in range(CHUNKS):

        @pl.loop(1, shards)
        def _(d):
            t = at_shard(d)
            remote(pn.at[c, t], pn1[c].at[from_shard(d)], p_send.at[c, d], p_recv.at[c, d], "shard", t).wait()

        @pl.loop(1, owners)
        def _(d):
            t = at_owner(d)
            pn_stage[c, t] = pn1[c][expert_at(t)]
            remote(pn_stage.at[c, t], back[c].at[o_me], po_send.at[c, d], po_recv.at[c, d], "owner", t).start()

        pn_stage[c, o_me] = pn1[c][expert_at(o_me)]
        own.append(pltpu.make_async_copy(pn_stage.at[c, o_me], back[c].at[o_me], own_sem.at[c]))
        own[-1].start()

    @pl.loop(1, owners)
    def _(d):
        remote(pj_stage.at[at_owner(d)], pj2.at[from_owner(d)], jo_send.at[d], jo_recv.at[d], "owner", at_owner(d)).wait()

    @pl.loop(0, slots)
    def _(j):
        projected = pj2[lax.div(table[o_me * slots + j], slots)]
        proj_out[j] = projected
        one, two = adam(one_ref[j], two_ref[j], projected)
        normed[j] = one / (jnp.sqrt(two) + EPSILON)

    other = s_me + 1 - 2 * lax.rem(s_me, 2)
    chips = shards // 2

    @pl.loop(1, chips)
    def _(k):
        t = at_shard(2 * k)
        remote(normed, normed_out.at[s_me], n_send.at[k], n_recv.at[k], "shard", t).start()

    remote(normed, normed_out.at[s_me], f_send.at[0], f_recv.at[0], "shard", other).start()
    own.append(pltpu.make_async_copy(normed, normed_out.at[s_me], own_sem.at[CHUNKS]))
    own[-1].start()

    @pl.loop(1, chips)
    def _(k):
        f = from_shard(2 * k)
        remote(normed, normed_out.at[f], n_send.at[k], n_recv.at[k], "shard", at_shard(2 * k)).wait()
        remote(normed_out.at[f], normed_out.at[f], f_send.at[k], f_recv.at[k], "shard", other).start()

    @pl.loop(0, chips)
    def _(k):
        g = lax.rem(other - 2 * k + shards, shards)
        remote(normed, normed_out.at[g], f_send.at[k], f_recv.at[k], "shard", other).wait()

    for copy in own:
        copy.wait()

    for c in range(CHUNKS):

        @pl.loop(1, owners)
        def _(d):
            t = at_owner(d)
            remote(pn_stage.at[c, t], back[c].at[from_owner(d)], po_send.at[c, d], po_recv.at[c, d], "owner", t).wait()


def leave(table, keep, mh, ml, pj, gh, gl, p, one, two):
    shards, rows, cols = gh.shape
    rank = p.shape[2]
    part = pj.shape[1]
    slots = one.shape[0]
    owners = table.shape[0] // slots
    chunk = rows // CHUNKS
    dma = pltpu.SemaphoreType.DMA
    smem = pl.BlockSpec(memory_space=pltpu.SMEM)
    vmem = pl.BlockSpec(memory_space=V)
    hbm = pl.BlockSpec(memory_space=pl.ANY)
    return pl.pallas_call(
        functools.partial(leave_body, shards, owners),
        out_shape=(
            jax.ShapeDtypeStruct((owners, chunk, rank), F32),
            jax.ShapeDtypeStruct((owners, chunk, rank), F32),
            jax.ShapeDtypeStruct((shards, slots, part, cols), F32),
            jax.ShapeDtypeStruct((slots, part, cols), F32),
        ),
        in_specs=[smem, smem, vmem, vmem, vmem, hbm, hbm, hbm, vmem, vmem],
        out_specs=(hbm, hbm, hbm, vmem),
        scratch_shapes=[
            V(gh.shape, BF), V(gh.shape, BF), V(p.shape, F32), V((CHUNKS, shards, chunk, rank), F32),
            V((shards, part, cols), F32), V((owners, part, cols), F32), V((owners, part, cols), F32),
            V((shards, chunk, rank), F32), V((shards, chunk, rank), F32), V((CHUNKS, owners, chunk, rank), F32),
            V((slots, part, cols), F32),
            dma((shards,)), dma((shards,)), dma((shards,)),
            dma((shards,)), dma((shards,)), dma((owners,)), dma((owners,)),
            dma((CHUNKS, shards)), dma((CHUNKS, shards)), dma((CHUNKS, owners)), dma((CHUNKS, owners)),
            dma((shards // 2,)), dma((shards // 2,)), dma((shards // 2,)), dma((shards // 2,)), dma((CHUNKS + 1,)),
        ],
        compiler_params=pltpu.CompilerParams(
            collective_id=1, has_side_effects=True, vmem_limit_bytes=56 * 1024 * 1024
        ),
        name="leave",
    )(table, keep, mh, ml, pj, gh, gl, p, one, two)


def finish_body(home_ref, back_a, back_b, normed_ref, proj_ref, one_ref, two_ref, basis_out, one_out, two_out, update_out):
    one_out[0], two_out[0] = adam(one_ref[0], two_ref[0], proj_ref[0])
    shards, _, part, cols = normed_ref.shape
    normed = split(normed_ref[:, 0].reshape(shards * part, cols))
    chunk = back_a.shape[1]
    for c, ref in enumerate((back_a, back_b)):
        at = slice(c * chunk, (c + 1) * chunk)
        basis_out[0, at] = ref[0]
        update_out[0, at] = (GALORE_SCALE * dot3(split(ref[0]), normed, NN)).astype(BF)


def finish(home, back_a, back_b, normed, projected, one, two):
    shards, slots, part, cols = normed.shape
    _, chunk, rank = back_a.shape
    small = pl.BlockSpec((1, part, cols), lambda j, home: (j, 0, 0))
    return pl.pallas_call(
        finish_body,
        out_shape=(
            jax.ShapeDtypeStruct((slots, 2 * chunk, rank), F32),
            jax.ShapeDtypeStruct(one.shape, F32),
            jax.ShapeDtypeStruct(two.shape, F32),
            jax.ShapeDtypeStruct((slots, 2 * chunk, cols), BF),
        ),
        grid_spec=pltpu.PrefetchScalarGridSpec(
            num_scalar_prefetch=1,
            grid=(slots,),
            in_specs=[
                pl.BlockSpec((1, chunk, rank), lambda j, home: (home[j], 0, 0)),
                pl.BlockSpec((1, chunk, rank), lambda j, home: (home[j], 0, 0)),
                pl.BlockSpec((shards, 1, part, cols), lambda j, home: (0, j, 0, 0)),
                small, small, small,
            ],
            out_specs=(
                pl.BlockSpec((1, 2 * chunk, rank), lambda j, home: (j, 0, 0)),
                small, small,
                pl.BlockSpec((1, 2 * chunk, cols), lambda j, home: (j, 0, 0)),
            ),
        ),
        compiler_params=pltpu.CompilerParams(vmem_limit_bytes=32 * 1024 * 1024),
        name="finish",
    )(home, back_a, back_b, normed, projected, one, two)


def on_device(gradient, old_basis, moment_one, moment_two, slot_expert, cost):
    gh, gl, kh, kl, z, p = enter(slot_expert, gradient, old_basis)
    mh, ml, pj, keep, home = refresh(slot_expert, cost, gradient.shape[0], kh, kl, z)
    back_a, back_b, normed, projected = leave(slot_expert, keep, mh, ml, pj, gh, gl, p, moment_one, moment_two)
    return tuple(finish(home, back_a, back_b, normed, projected, moment_one, moment_two))


def solution(mesh):
    spec = P("owner", "shard", None)
    return jax.shard_map(
        on_device, mesh=mesh, in_specs=(spec,) * 4 + (P(), P()), out_specs=(spec,) * 4, check_vma=False
    )
```

```python
import functools
import jax, jax.numpy as jnp
from jax import lax
from jax.experimental import pallas as pl
from jax.sharding import PartitionSpec as P
from jax.experimental.pallas import tpu as pltpu

BF = jnp.bfloat16
F32 = jnp.float32

def split(x):
    hi = x.astype(BF)
    return hi, (x - hi.astype(F32)).astype(BF)

def mm(a, b, dims):
    return lax.dot_general(a, b, (dims, ((), ())), preferred_element_type=F32)

NN = ((1,), (0,))
TN = ((0,), (0,))
NT = ((1,), (1,))

def dot3(a, b, dims):
    ah, al = a
    bh, bl = b
    return mm(ah, bh, dims) + (mm(ah, bl, dims) + mm(al, bh, dims))

PANEL, GROUP = 32, 16


def factor(c_ref, xh, xl, ls, rs):
    nb, sub_nb = PANEL, GROUP
    n = c_ref.shape[0]
    for p in range(n // nb):
        lo = p * nb
        need = [h for h in range(4) if (h < 2 and h * 128 + 128 > lo) or (h >= 2 and (h - 2) * 128 < lo + nb)]
        sub = lax.broadcasted_iota(jnp.int32, (nb, 128), 0)
        s = {}
        for h in need:
            if h < 2:
                s[h] = c_ref[lo:lo + nb, 128 * h:128 * h + 128]
            else:
                l = lax.broadcasted_iota(jnp.int32, (nb, 128), 1) + 128 * (h - 2)
                s[h] = jnp.where(l == sub + lo, 1.0, 0.0)
        a0, a1 = need[0] * 128, need[-1] * 128 + 128
        cuts = []
        if p > 1:
            cuts.append((0, 3 * (lo - nb)))
        if p > 0:
            cuts.append((3 * (lo - nb), 3 * lo))
        for (x, y) in cuts:
            d = mm(ls[x:y, lo:lo + nb], rs[x:y, a0:a1], TN)
            for h in need:
                s[h] = s[h] - d[:, 128 * h - a0:128 * h - a0 + 128]
        hd = lo // 128
        off = lo - hd * 128
        pivots = []
        done = []
        for g in range(nb // sub_nb):
            b = g * sub_nb
            rows = nb - b
            rsub = lax.broadcasted_iota(jnp.int32, (rows, 128), 0)
            cols = [jnp.broadcast_to(s[hd][:, off + b + k:off + b + k + 1], (rows, 128)) for k in range(sub_nb)]
            for j in range(sub_nb):
                d = cols[j][j:j + 1, :]
                r = 1.0 / d
                pivots.append(d)
                m = jnp.where(rsub > j, cols[j] * r, 0.0)
                for k in range(j + 1, sub_nb):
                    cols[k] = cols[k] - m * cols[k][j:j + 1, :]
                for h in need:
                    s[h] = s[h] - m * s[h][j:j + 1, :]
            done.append({h: s[h][0:sub_nb] for h in need})
            if rows > sub_nb:
                s = {h: s[h][sub_nb:] for h in need}
        scale = lax.rsqrt(jnp.concatenate(pivots, axis=0))
        for h in range(4):
            if h not in need:
                o = jnp.zeros((nb, 128), F32)
            else:
                o = jnp.concatenate([t[h] for t in done], axis=0) * scale
                if h == hd:
                    l = lax.broadcasted_iota(jnp.int32, (nb, 128), 1) + 128 * h
                    o = jnp.where(l >= sub + lo, o, 0.0)
            cs = slice(128 * h, 128 * h + 128)
            hi = o.astype(BF)
            lw = (o - hi.astype(F32)).astype(BF)
            if h >= 2:
                xs = slice(128 * (h - 2), 128 * (h - 2) + 128)
                xh[lo:lo + nb, xs] = hi
                xl[lo:lo + nb, xs] = lw
            b = 3 * lo
            rs[b:b + nb, cs] = hi
            rs[b + nb:b + 2 * nb, cs] = lw
            rs[b + 2 * nb:b + 3 * nb, cs] = hi
            if h < 2:
                ls[b:b + nb, cs] = hi
                ls[b + nb:b + 2 * nb, cs] = hi
                ls[b + 2 * nb:b + 3 * nb, cs] = lw


MESH = pl.DeviceIdType.MESH
V = pltpu.VMEM


def greet(groups):
    barrier = pltpu.get_barrier_semaphore()
    total = 0
    for axis, size in groups:
        me = lax.axis_index(axis)

        @pl.loop(1, size)
        def _(d):
            pl.semaphore_signal(barrier, inc=1, device_id={axis: lax.rem(me + d, size)}, device_id_type=MESH)

        total += size - 1
    pl.semaphore_wait(barrier, total)


STEPS = (
    (1, 1), (3, 3), (1, 3), (3, 1), (1, 0), (0, 1), (3, 0), (0, 3), (2, 0), (0, 2), (2, 2), (2, 1), (1, 2), (2, 3), (3, 2),
)
SIDE = 4


def partners(me):
    z, y = lax.div(me, SIDE), lax.rem(me, SIDE)
    for k, (dy, dz) in enumerate(STEPS):
        to = lax.rem(z + dz, SIDE) * SIDE + lax.rem(y + dy, SIDE)
        source = lax.rem(z + SIDE - dz, SIDE) * SIDE + lax.rem(y + SIDE - dy, SIDE)
        yield k, to, source


def remote(src, dst, send, recv, axis, target):
    return pltpu.make_async_remote_copy(
        src_ref=src, dst_ref=dst, send_sem=send, recv_sem=recv, device_id={axis: target}, device_id_type=MESH
    )


def slot_at(table, owner, slots, home):
    found = 0
    for j in range(slots):
        found = jnp.where(lax.div(table[owner * slots + j], slots) == home, j, found)
    return found


def enter_body(shards, owners, table, g_ref, b_ref, gh_out, gl_out, kh_out, kl_out, z_out, p_out,
               gland, gh, gl, kacc, kh, kl, stage, landed, stage2, pland,
               g_send, g_recv, a_send, a_recv, b_send, b_recv, own_sem, h_sem, l_sem, p_sem, k_sem):
    s_me = lax.axis_index("shard")
    o_me = lax.axis_index("owner")
    greet((("shard", shards), ("owner", owners)))
    slots = shards

    def at_shard(d):
        return lax.rem(s_me + d, shards)

    def from_shard(d):
        return lax.rem(s_me - d + shards, shards)

    own = pltpu.make_async_copy(g_ref.at[s_me], gland.at[s_me], own_sem)
    own.start()

    @pl.loop(1, shards)
    def _(d):
        t = at_shard(d)
        remote(g_ref.at[t], gland.at[s_me], g_send.at[d], g_recv.at[d], "shard", t).start()

    for k, t, _ in partners(o_me):
        stage[t] = b_ref[slot_at(table, o_me, slots, t)]
        remote(stage.at[t], landed.at[o_me], a_send.at[k], a_recv.at[k], "owner", t).start()

    landed[o_me] = b_ref[slot_at(table, o_me, slots, o_me)]
    kacc[...] = jnp.zeros_like(kacc)
    own.wait()
    tiles = kacc.shape[0] // 256

    def gram(f):
        h, l = split(gland[f])
        gh[f] = h
        gl[f] = l
        pltpu.make_async_copy(gh.at[f], gh_out.at[f], h_sem.at[f]).start()
        pltpu.make_async_copy(gl.at[f], gl_out.at[f], l_sem.at[f]).start()
        for a in range(tiles):
            ra = slice(256 * a, 256 * a + 256)
            for b in range(a, tiles):
                rb = slice(256 * b, 256 * b + 256)
                kacc[ra, rb] += dot3((h[:, ra], l[:, ra]), (h[:, rb], l[:, rb]), TN)

    gram(s_me)

    def take_gram(d):
        f = from_shard(d)
        remote(g_ref.at[at_shard(d)], gland.at[f], g_send.at[d], g_recv.at[d], "shard", at_shard(d)).wait_recv()
        gram(f)

    half = EARLY
    pl.loop(1, half)(take_gram)

    for k, t, source in partners(o_me):
        remote(stage.at[t], landed.at[source], a_send.at[k], a_recv.at[k], "owner", t).wait()

    def holder(i):
        def add(o, found):
            for j in range(slots):
                found = jnp.where(table[o * slots + j] == o_me * slots + i, o, found)
            return found

        return lax.fori_loop(0, owners, add, 0)

    @pl.loop(1, shards)
    def _(d):
        t = at_shard(d)
        stage2[t] = landed[holder(t)]
        remote(stage2.at[t], pland.at[s_me], b_send.at[d], b_recv.at[d], "shard", t).start()

    pland[s_me] = landed[holder(s_me)]
    pl.loop(half, shards)(take_gram)

    for a in range(tiles):
        ra = slice(256 * a, 256 * a + 256)
        for b in range(a, tiles):
            rb = slice(256 * b, 256 * b + 256)
            h, l = split(kacc[ra, rb])
            kh[ra, rb] = h
            kl[ra, rb] = l
            if b > a:
                h, l = split(kacc[ra, rb].T)
                kh[rb, ra] = h
                kl[rb, ra] = l

    save_k = (pltpu.make_async_copy(kh, kh_out, k_sem.at[0]), pltpu.make_async_copy(kl, kl_out, k_sem.at[1]))
    for copy in save_k:
        copy.start()

    def project(f):
        pltpu.make_async_copy(pland.at[f], p_out.at[f], p_sem.at[f]).start()
        return dot3((gh[f], gl[f]), split(pland[f]), TN)

    z_out[...] = project(s_me)

    @pl.loop(1, shards)
    def _(d):
        f = from_shard(d)
        remote(stage2.at[at_shard(d)], pland.at[f], b_send.at[d], b_recv.at[d], "shard", at_shard(d)).wait()
        z_out[...] += project(f)

    @pl.loop(1, shards)
    def _(d):
        remote(g_ref.at[at_shard(d)], gland.at[from_shard(d)], g_send.at[d], g_recv.at[d], "shard", at_shard(d)).wait_send()

    @pl.loop(0, shards)
    def _(f):
        pltpu.make_async_copy(gh.at[f], gh_out.at[f], h_sem.at[f]).wait()
        pltpu.make_async_copy(gl.at[f], gl_out.at[f], l_sem.at[f]).wait()
        pltpu.make_async_copy(pland.at[f], p_out.at[f], p_sem.at[f]).wait()

    for copy in save_k:
        copy.wait()


EARLY = 5


def enter(table, gradient, basis):
    shards, rows, cols = gradient.shape
    rank = basis.shape[2]
    owners = table.shape[0] // basis.shape[0]
    sem = pltpu.SemaphoreType.DMA
    smem = pl.BlockSpec(memory_space=pltpu.SMEM)
    vmem = pl.BlockSpec(memory_space=V)
    hbm = pl.BlockSpec(memory_space=pl.ANY)
    return pl.pallas_call(
        functools.partial(enter_body, shards, owners),
        out_shape=(
            jax.ShapeDtypeStruct((shards, rows, cols), BF),
            jax.ShapeDtypeStruct((shards, rows, cols), BF),
            jax.ShapeDtypeStruct((cols, cols), BF),
            jax.ShapeDtypeStruct((cols, cols), BF),
            jax.ShapeDtypeStruct((cols, rank), F32),
            jax.ShapeDtypeStruct((shards, rows, rank), F32),
        ),
        in_specs=[smem, hbm, vmem],
        out_specs=(hbm, hbm, hbm, hbm, vmem, hbm),
        scratch_shapes=[
            V((shards, rows, cols), F32), V((shards, rows, cols), BF), V((shards, rows, cols), BF), V((cols, cols), F32), V((cols, cols), BF), V((cols, cols), BF),
            V((owners, rows, rank), F32), V((owners, rows, rank), F32), V((shards, rows, rank), F32), V((shards, rows, rank), F32),
            sem((shards,)), sem((shards,)), sem((owners,)), sem((owners,)), sem((shards,)), sem((shards,)),
            sem, sem((shards,)), sem((shards,)), sem((shards,)), sem((2,)),
        ],
        compiler_params=pltpu.CompilerParams(
            collective_id=0, has_side_effects=True, vmem_limit_bytes=56 * 1024 * 1024
        ),
        name="enter",
    )(table, gradient, basis)


def body(table, cost, kh_ref, kl_ref, zin_ref, mh_ref, ml_ref, pj_ref, keep_ref, home_ref, z_ref, w_ref, c_ref, xh, xl, ls, rs):
    s_me = lax.axis_index("shard")
    o_me = lax.axis_index("owner")
    shards, part, cols = pj_ref.shape
    rank = zin_ref.shape[1]
    count = cost[o_me * shards + s_me]
    keep_ref[0] = jnp.where(count > 0, 0.0, 1.0)
    for j in range(shards):
        home_ref[j] = lax.div(table[o_me * shards + j], shards)
    z_ref[...] = zin_ref[...]

    @pl.loop(0, count)
    def _(it):
        z = split(z_ref[...])
        w_ref[...] = dot3((kh_ref[...], kl_ref[...]), z, NN)
        w = split(w_ref[...])
        c_ref[...] = dot3(z, w, TN)
        factor(c_ref, xh, xl, ls, rs)
        x = (xh[...], xl[...])
        z_ref[...] = dot3(w, x, NT)

        @pl.when(it == count - 1)
        def _():
            h, l = split(dot3(z, x, NT))
            mh_ref[...] = h
            ml_ref[...] = l

    @pl.when(count == 0)
    def _():
        mh_ref[...] = jnp.zeros_like(mh_ref)
        ml_ref[...] = jnp.zeros_like(ml_ref)

    for c in range(cols // 256):
        t = z_ref[256 * c:256 * c + 256, :].T
        for s in range(shards):
            pj_ref[s, :, 256 * c:256 * c + 256] = t[part * s:part * s + part, :]


def refresh(table, cost, shards, kh, kl, z):
    cols, rank = z.shape
    smem = pl.BlockSpec(memory_space=pltpu.SMEM)
    vmem = pl.BlockSpec(memory_space=V)
    return pl.pallas_call(
        body,
        out_shape=(
            jax.ShapeDtypeStruct((cols, rank), BF),
            jax.ShapeDtypeStruct((cols, rank), BF),
            jax.ShapeDtypeStruct((shards, rank // shards, cols), F32),
            jax.ShapeDtypeStruct((1,), F32),
            jax.ShapeDtypeStruct((shards,), jnp.int32),
        ),
        in_specs=[smem, smem, vmem, vmem, vmem],
        out_specs=(vmem, vmem, vmem, smem, smem),
        scratch_shapes=[
            V((cols, rank), F32), V((cols, rank), F32), V((rank, rank), F32), V((rank, rank), BF), V((rank, rank), BF),
            V((3 * rank, rank), BF), V((3 * rank, 2 * rank), BF),
        ],
        compiler_params=pltpu.CompilerParams(vmem_limit_bytes=56 * 1024 * 1024),
        name="refresh",
    )(table, cost, kh, kl, z)


BETA_ONE = 0.9
BETA_TWO = 0.99
EPSILON = 1e-08
GALORE_SCALE = 0.25
CHUNKS = 2


def adam(one, two, projected):
    one = BETA_ONE * one + (1.0 - BETA_ONE) * projected
    two = BETA_TWO * two + (1.0 - BETA_TWO) * projected * projected
    return one, two


def leave_body(shards, owners, table, keep_ref, mh_ref, ml_ref, pj_ref, gh_hbm, gl_hbm, p_hbm, one_ref, two_ref,
               back_a, back_b, normed_out, proj_out,
               gh, gl, p_in, pn, pj1, pj_stage, pj2, pn1a, pn1b, pn_stage, normed,
               h_sem, l_sem, i_sem, j_send, j_recv, jo_send, jo_recv, p_send, p_recv, po_send, po_recv,
               n_send, n_recv, f_send, f_recv, own_sem):
    s_me = lax.axis_index("shard")
    o_me = lax.axis_index("owner")
    slots = one_ref.shape[0]
    pn1, back = (pn1a, pn1b), (back_a, back_b)
    chunk = pn1a.shape[1]

    def at_shard(d):
        return lax.rem(s_me + d, shards)

    def from_shard(d):
        return lax.rem(s_me - d + shards, shards)

    def rows(c):
        return slice(c * chunk, (c + 1) * chunk)

    def loads(t):
        return (
            pltpu.make_async_copy(gh_hbm.at[t], gh.at[t], h_sem.at[t]),
            pltpu.make_async_copy(gl_hbm.at[t], gl.at[t], l_sem.at[t]),
            pltpu.make_async_copy(p_hbm.at[t], p_in.at[t], i_sem.at[t]),
        )

    @pl.loop(1, shards + 1)
    def _(d):
        for copy in loads(at_shard(d)):
            copy.start()

    greet((("shard", shards), ("owner", owners)))

    @pl.loop(1, shards)
    def _(d):
        t = at_shard(d)
        remote(pj_ref.at[t], pj1.at[s_me], j_send.at[d], j_recv.at[d], "shard", t).start()

    pj1[s_me] = pj_ref[s_me]
    keep = keep_ref[0]

    def basis_rows(t, c):
        return dot3((gh[t, rows(c)], gl[t, rows(c)]), (mh_ref[...], ml_ref[...]), NN) + keep * p_in[t, rows(c)]

    for c in range(CHUNKS):

        @pl.loop(1, shards)
        def _(d):
            t = at_shard(d)
            if c == 0:
                for copy in loads(t):
                    copy.wait()
            pn[c, t] = basis_rows(t, c)
            remote(pn.at[c, t], pn1[c].at[s_me], p_send.at[c, d], p_recv.at[c, d], "shard", t).start()

        if c == 0:
            for copy in loads(s_me):
                copy.wait()
        pn1[c][s_me] = basis_rows(s_me, c)

    def expert_at(owner):
        found = 0
        for j in range(slots):
            e = table[owner * slots + j]
            found = jnp.where(lax.div(e, slots) == o_me, lax.rem(e, slots), found)
        return found

    @pl.loop(1, shards)
    def _(d):
        remote(pj_ref.at[at_shard(d)], pj1.at[from_shard(d)], j_send.at[d], j_recv.at[d], "shard", at_shard(d)).wait()

    for k, t, _ in partners(o_me):
        pj_stage[t] = pj1[expert_at(t)]
        remote(pj_stage.at[t], pj2.at[o_me], jo_send.at[k], jo_recv.at[k], "owner", t).start()

    pj2[o_me] = pj1[expert_at(o_me)]
    own = []
    for c in range(CHUNKS):

        @pl.loop(1, shards)
        def _(d):
            t = at_shard(d)
            remote(pn.at[c, t], pn1[c].at[from_shard(d)], p_send.at[c, d], p_recv.at[c, d], "shard", t).wait()

        for k, t, _ in partners(o_me):
            pn_stage[c, t] = pn1[c][expert_at(t)]
            remote(pn_stage.at[c, t], back[c].at[o_me], po_send.at[c, k], po_recv.at[c, k], "owner", t).start()

        pn_stage[c, o_me] = pn1[c][expert_at(o_me)]
        own.append(pltpu.make_async_copy(pn_stage.at[c, o_me], back[c].at[o_me], own_sem.at[c]))
        own[-1].start()

    for k, t, source in partners(o_me):
        remote(pj_stage.at[t], pj2.at[source], jo_send.at[k], jo_recv.at[k], "owner", t).wait()

    @pl.loop(0, slots)
    def _(j):
        projected = pj2[lax.div(table[o_me * slots + j], slots)]
        proj_out[j] = projected
        one, two = adam(one_ref[j], two_ref[j], projected)
        normed[j] = one / (jnp.sqrt(two) + EPSILON)

    other = s_me + 1 - 2 * lax.rem(s_me, 2)
    chips = shards // 2

    @pl.loop(1, chips)
    def _(k):
        t = at_shard(2 * k)
        remote(normed, normed_out.at[s_me], n_send.at[k], n_recv.at[k], "shard", t).start()

    remote(normed, normed_out.at[s_me], f_send.at[0], f_recv.at[0], "shard", other).start()
    own.append(pltpu.make_async_copy(normed, normed_out.at[s_me], own_sem.at[CHUNKS]))
    own[-1].start()

    @pl.loop(1, chips)
    def _(k):
        f = from_shard(2 * k)
        remote(normed, normed_out.at[f], n_send.at[k], n_recv.at[k], "shard", at_shard(2 * k)).wait()
        remote(normed_out.at[f], normed_out.at[f], f_send.at[k], f_recv.at[k], "shard", other).start()

    @pl.loop(0, chips)
    def _(k):
        g = lax.rem(other - 2 * k + shards, shards)
        remote(normed, normed_out.at[g], f_send.at[k], f_recv.at[k], "shard", other).wait()

    for copy in own:
        copy.wait()

    for c in range(CHUNKS):

        for k, t, source in partners(o_me):
            remote(pn_stage.at[c, t], back[c].at[source], po_send.at[c, k], po_recv.at[c, k], "owner", t).wait()


def leave(table, keep, mh, ml, pj, gh, gl, p, one, two):
    shards, rows, cols = gh.shape
    rank = p.shape[2]
    part = pj.shape[1]
    slots = one.shape[0]
    owners = table.shape[0] // slots
    chunk = rows // CHUNKS
    dma = pltpu.SemaphoreType.DMA
    smem = pl.BlockSpec(memory_space=pltpu.SMEM)
    vmem = pl.BlockSpec(memory_space=V)
    hbm = pl.BlockSpec(memory_space=pl.ANY)
    return pl.pallas_call(
        functools.partial(leave_body, shards, owners),
        out_shape=(
            jax.ShapeDtypeStruct((owners, chunk, rank), F32),
            jax.ShapeDtypeStruct((owners, chunk, rank), F32),
            jax.ShapeDtypeStruct((shards, slots, part, cols), F32),
            jax.ShapeDtypeStruct((slots, part, cols), F32),
        ),
        in_specs=[smem, smem, vmem, vmem, vmem, hbm, hbm, hbm, vmem, vmem],
        out_specs=(hbm, hbm, hbm, vmem),
        scratch_shapes=[
            V(gh.shape, BF), V(gh.shape, BF), V(p.shape, F32), V((CHUNKS, shards, chunk, rank), F32),
            V((shards, part, cols), F32), V((owners, part, cols), F32), V((owners, part, cols), F32),
            V((shards, chunk, rank), F32), V((shards, chunk, rank), F32), V((CHUNKS, owners, chunk, rank), F32),
            V((slots, part, cols), F32),
            dma((shards,)), dma((shards,)), dma((shards,)),
            dma((shards,)), dma((shards,)), dma((owners,)), dma((owners,)),
            dma((CHUNKS, shards)), dma((CHUNKS, shards)), dma((CHUNKS, owners)), dma((CHUNKS, owners)),
            dma((shards // 2,)), dma((shards // 2,)), dma((shards // 2,)), dma((shards // 2,)), dma((CHUNKS + 1,)),
        ],
        compiler_params=pltpu.CompilerParams(
            collective_id=1, has_side_effects=True, vmem_limit_bytes=56 * 1024 * 1024
        ),
        name="leave",
    )(table, keep, mh, ml, pj, gh, gl, p, one, two)


def finish_body(home_ref, back_a, back_b, normed_ref, proj_ref, one_ref, two_ref, basis_out, one_out, two_out, update_out):
    one_out[0], two_out[0] = adam(one_ref[0], two_ref[0], proj_ref[0])
    shards, _, part, cols = normed_ref.shape
    normed = split(normed_ref[:, 0].reshape(shards * part, cols))
    chunk = back_a.shape[1]
    for c, ref in enumerate((back_a, back_b)):
        at = slice(c * chunk, (c + 1) * chunk)
        basis_out[0, at] = ref[0]
        update_out[0, at] = (GALORE_SCALE * dot3(split(ref[0]), normed, NN)).astype(BF)


def finish(home, back_a, back_b, normed, projected, one, two):
    shards, slots, part, cols = normed.shape
    _, chunk, rank = back_a.shape
    small = pl.BlockSpec((1, part, cols), lambda j, home: (j, 0, 0))
    return pl.pallas_call(
        finish_body,
        out_shape=(
            jax.ShapeDtypeStruct((slots, 2 * chunk, rank), F32),
            jax.ShapeDtypeStruct(one.shape, F32),
            jax.ShapeDtypeStruct(two.shape, F32),
            jax.ShapeDtypeStruct((slots, 2 * chunk, cols), BF),
        ),
        grid_spec=pltpu.PrefetchScalarGridSpec(
            num_scalar_prefetch=1,
            grid=(slots,),
            in_specs=[
                pl.BlockSpec((1, chunk, rank), lambda j, home: (home[j], 0, 0)),
                pl.BlockSpec((1, chunk, rank), lambda j, home: (home[j], 0, 0)),
                pl.BlockSpec((shards, 1, part, cols), lambda j, home: (0, j, 0, 0)),
                small, small, small,
            ],
            out_specs=(
                pl.BlockSpec((1, 2 * chunk, rank), lambda j, home: (j, 0, 0)),
                small, small,
                pl.BlockSpec((1, 2 * chunk, cols), lambda j, home: (j, 0, 0)),
            ),
        ),
        compiler_params=pltpu.CompilerParams(vmem_limit_bytes=60 * 1024 * 1024),
        name="finish",
    )(home, back_a, back_b, normed, projected, one, two)


def on_device(gradient, old_basis, moment_one, moment_two, slot_expert, cost):
    gh, gl, kh, kl, z, p = enter(slot_expert, gradient, old_basis)
    mh, ml, pj, keep, home = refresh(slot_expert, cost, gradient.shape[0], kh, kl, z)
    back_a, back_b, normed, projected = leave(slot_expert, keep, mh, ml, pj, gh, gl, p, moment_one, moment_two)
    return tuple(finish(home, back_a, back_b, normed, projected, moment_one, moment_two))


def solution(mesh):
    spec = P("owner", "shard", None)
    return jax.shard_map(
        on_device, mesh=mesh, in_specs=(spec,) * 4 + (P(), P()), out_specs=(spec,) * 4, check_vma=False
    )
```

```python
import functools
import jax, jax.numpy as jnp
from jax import lax
from jax.experimental import pallas as pl
from jax.sharding import PartitionSpec as P
from jax.experimental.pallas import tpu as pltpu

BF = jnp.bfloat16
F32 = jnp.float32

def split(x):
    hi = x.astype(BF)
    return hi, (x - hi.astype(F32)).astype(BF)

def mm(a, b, dims):
    return lax.dot_general(a, b, (dims, ((), ())), preferred_element_type=F32)

NN = ((1,), (0,))
TN = ((0,), (0,))
NT = ((1,), (1,))

def dot3(a, b, dims):
    ah, al = a
    bh, bl = b
    return mm(ah, bh, dims) + (mm(ah, bl, dims) + mm(al, bh, dims))

PANEL, GROUP = 32, 16


def factor(c_ref, xh, xl, ls, rs):
    nb, sub_nb = PANEL, GROUP
    n = c_ref.shape[0]
    for p in range(n // nb):
        lo = p * nb
        need = [h for h in range(4) if (h < 2 and h * 128 + 128 > lo) or (h >= 2 and (h - 2) * 128 < lo + nb)]
        sub = lax.broadcasted_iota(jnp.int32, (nb, 128), 0)
        s = {}
        for h in need:
            if h < 2:
                s[h] = c_ref[lo:lo + nb, 128 * h:128 * h + 128]
            else:
                l = lax.broadcasted_iota(jnp.int32, (nb, 128), 1) + 128 * (h - 2)
                s[h] = jnp.where(l == sub + lo, 1.0, 0.0)
        a0, a1 = need[0] * 128, need[-1] * 128 + 128
        cuts = []
        if p > 1:
            cuts.append((0, 3 * (lo - nb)))
        if p > 0:
            cuts.append((3 * (lo - nb), 3 * lo))
        for (x, y) in cuts:
            d = mm(ls[x:y, lo:lo + nb], rs[x:y, a0:a1], TN)
            for h in need:
                s[h] = s[h] - d[:, 128 * h - a0:128 * h - a0 + 128]
        hd = lo // 128
        off = lo - hd * 128
        pivots = []
        done = []
        for g in range(nb // sub_nb):
            b = g * sub_nb
            rows = nb - b
            rsub = lax.broadcasted_iota(jnp.int32, (rows, 128), 0)
            cols = [jnp.broadcast_to(s[hd][:, off + b + k:off + b + k + 1], (rows, 128)) for k in range(sub_nb)]
            for j in range(sub_nb):
                d = cols[j][j:j + 1, :]
                r = 1.0 / d
                pivots.append(d)
                m = jnp.where(rsub > j, cols[j] * r, 0.0)
                for k in range(j + 1, sub_nb):
                    cols[k] = cols[k] - m * cols[k][j:j + 1, :]
                for h in need:
                    s[h] = s[h] - m * s[h][j:j + 1, :]
            done.append({h: s[h][0:sub_nb] for h in need})
            if rows > sub_nb:
                s = {h: s[h][sub_nb:] for h in need}
        scale = lax.rsqrt(jnp.concatenate(pivots, axis=0))
        for h in range(4):
            if h not in need:
                o = jnp.zeros((nb, 128), F32)
            else:
                o = jnp.concatenate([t[h] for t in done], axis=0) * scale
                if h == hd:
                    l = lax.broadcasted_iota(jnp.int32, (nb, 128), 1) + 128 * h
                    o = jnp.where(l >= sub + lo, o, 0.0)
            cs = slice(128 * h, 128 * h + 128)
            hi = o.astype(BF)
            lw = (o - hi.astype(F32)).astype(BF)
            if h >= 2:
                xs = slice(128 * (h - 2), 128 * (h - 2) + 128)
                xh[lo:lo + nb, xs] = hi
                xl[lo:lo + nb, xs] = lw
            b = 3 * lo
            rs[b:b + nb, cs] = hi
            rs[b + nb:b + 2 * nb, cs] = lw
            rs[b + 2 * nb:b + 3 * nb, cs] = hi
            if h < 2:
                ls[b:b + nb, cs] = hi
                ls[b + nb:b + 2 * nb, cs] = hi
                ls[b + 2 * nb:b + 3 * nb, cs] = lw


MESH = pl.DeviceIdType.MESH
V = pltpu.VMEM


def greet(groups):
    barrier = pltpu.get_barrier_semaphore()
    total = 0
    for axis, size in groups:
        me = lax.axis_index(axis)

        @pl.loop(1, size)
        def _(d):
            pl.semaphore_signal(barrier, inc=1, device_id={axis: lax.rem(me + d, size)}, device_id_type=MESH)

        total += size - 1
    pl.semaphore_wait(barrier, total)


STEPS = (
    (1, 1), (3, 3), (1, 3), (3, 1), (1, 0), (0, 1), (3, 0), (0, 3), (2, 0), (0, 2), (2, 2), (2, 1), (1, 2), (2, 3), (3, 2),
)
SIDE = 4


def partners(me):
    z, y = lax.div(me, SIDE), lax.rem(me, SIDE)
    for k, (dy, dz) in enumerate(STEPS):
        to = lax.rem(z + dz, SIDE) * SIDE + lax.rem(y + dy, SIDE)
        source = lax.rem(z + SIDE - dz, SIDE) * SIDE + lax.rem(y + SIDE - dy, SIDE)
        yield k, to, source


def remote(src, dst, send, recv, axis, target):
    return pltpu.make_async_remote_copy(
        src_ref=src, dst_ref=dst, send_sem=send, recv_sem=recv, device_id={axis: target}, device_id_type=MESH
    )


def slot_at(table, owner, slots, home):
    found = 0
    for j in range(slots):
        found = jnp.where(lax.div(table[owner * slots + j], slots) == home, j, found)
    return found


def enter_body(shards, owners, table, g_ref, b_hbm, gh_out, gl_out, kh_out, kl_out, z_out, p_out,
               b_ref, gland, gh, gl, kacc, kh, kl, stage, landed, stage2, pland,
               g_send, g_recv, a_send, a_recv, b_send, b_recv, own_sem, in_sem, h_sem, l_sem, p_sem, k_sem):
    s_me = lax.axis_index("shard")
    o_me = lax.axis_index("owner")
    load = pltpu.make_async_copy(b_hbm, b_ref, in_sem)
    load.start()
    greet((("shard", shards), ("owner", owners)))
    slots = shards

    def at_shard(d):
        return lax.rem(s_me + d, shards)

    def from_shard(d):
        return lax.rem(s_me - d + shards, shards)

    own = pltpu.make_async_copy(g_ref.at[s_me], gland.at[s_me], own_sem)
    own.start()

    @pl.loop(1, shards)
    def _(d):
        t = at_shard(d)
        remote(g_ref.at[t], gland.at[s_me], g_send.at[d], g_recv.at[d], "shard", t).start()

    load.wait()
    for k, t, _ in partners(o_me):
        stage[t] = b_ref[slot_at(table, o_me, slots, t)]
        remote(stage.at[t], landed.at[o_me], a_send.at[k], a_recv.at[k], "owner", t).start()

    landed[o_me] = b_ref[slot_at(table, o_me, slots, o_me)]
    kacc[...] = jnp.zeros_like(kacc)
    own.wait()
    tiles = kacc.shape[0] // 256

    def gram(f):
        h, l = split(gland[f])
        gh[f] = h
        gl[f] = l
        pltpu.make_async_copy(gh.at[f], gh_out.at[f], h_sem.at[f]).start()
        pltpu.make_async_copy(gl.at[f], gl_out.at[f], l_sem.at[f]).start()
        for a in range(tiles):
            ra = slice(256 * a, 256 * a + 256)
            for b in range(a, tiles):
                rb = slice(256 * b, 256 * b + 256)
                kacc[ra, rb] += dot3((h[:, ra], l[:, ra]), (h[:, rb], l[:, rb]), TN)

    gram(s_me)

    def take_gram(d):
        f = from_shard(d)
        remote(g_ref.at[at_shard(d)], gland.at[f], g_send.at[d], g_recv.at[d], "shard", at_shard(d)).wait_recv()
        gram(f)

    half = EARLY
    pl.loop(1, half)(take_gram)

    for k, t, source in partners(o_me):
        remote(stage.at[t], landed.at[source], a_send.at[k], a_recv.at[k], "owner", t).wait()

    def holder(i):
        def add(o, found):
            for j in range(slots):
                found = jnp.where(table[o * slots + j] == o_me * slots + i, o, found)
            return found

        return lax.fori_loop(0, owners, add, 0)

    @pl.loop(1, shards)
    def _(d):
        t = at_shard(d)
        stage2[t] = landed[holder(t)]
        remote(stage2.at[t], pland.at[s_me], b_send.at[d], b_recv.at[d], "shard", t).start()

    pland[s_me] = landed[holder(s_me)]
    pl.loop(half, shards)(take_gram)

    for a in range(tiles):
        ra = slice(256 * a, 256 * a + 256)
        for b in range(a, tiles):
            rb = slice(256 * b, 256 * b + 256)
            h, l = split(kacc[ra, rb])
            kh[ra, rb] = h
            kl[ra, rb] = l
            if b > a:
                h, l = split(kacc[ra, rb].T)
                kh[rb, ra] = h
                kl[rb, ra] = l

    save_k = (pltpu.make_async_copy(kh, kh_out, k_sem.at[0]), pltpu.make_async_copy(kl, kl_out, k_sem.at[1]))
    for copy in save_k:
        copy.start()

    def project(f):
        pltpu.make_async_copy(pland.at[f], p_out.at[f], p_sem.at[f]).start()
        return dot3(split(pland[f]), (gh[f], gl[f]), TN)

    z_out[...] = project(s_me)

    @pl.loop(1, shards)
    def _(d):
        f = from_shard(d)
        remote(stage2.at[at_shard(d)], pland.at[f], b_send.at[d], b_recv.at[d], "shard", at_shard(d)).wait()
        z_out[...] += project(f)

    @pl.loop(1, shards)
    def _(d):
        remote(g_ref.at[at_shard(d)], gland.at[from_shard(d)], g_send.at[d], g_recv.at[d], "shard", at_shard(d)).wait_send()

    @pl.loop(0, shards)
    def _(f):
        pltpu.make_async_copy(gh.at[f], gh_out.at[f], h_sem.at[f]).wait()
        pltpu.make_async_copy(gl.at[f], gl_out.at[f], l_sem.at[f]).wait()
        pltpu.make_async_copy(pland.at[f], p_out.at[f], p_sem.at[f]).wait()

    for copy in save_k:
        copy.wait()


EARLY = 5


def enter(table, gradient, basis):
    shards, rows, cols = gradient.shape
    rank = basis.shape[2]
    owners = table.shape[0] // basis.shape[0]
    sem = pltpu.SemaphoreType.DMA
    smem = pl.BlockSpec(memory_space=pltpu.SMEM)
    vmem = pl.BlockSpec(memory_space=V)
    hbm = pl.BlockSpec(memory_space=pl.ANY)
    return pl.pallas_call(
        functools.partial(enter_body, shards, owners),
        out_shape=(
            jax.ShapeDtypeStruct((shards, rows, cols), BF),
            jax.ShapeDtypeStruct((shards, rows, cols), BF),
            jax.ShapeDtypeStruct((cols, cols), BF),
            jax.ShapeDtypeStruct((cols, cols), BF),
            jax.ShapeDtypeStruct((rank, cols), F32),
            jax.ShapeDtypeStruct((shards, rows, rank), F32),
        ),
        in_specs=[smem, hbm, hbm],
        out_specs=(hbm, hbm, hbm, hbm, vmem, hbm),
        scratch_shapes=[
            V((shards, rows, rank), F32), V((shards, rows, cols), F32), V((shards, rows, cols), BF), V((shards, rows, cols), BF), V((cols, cols), F32), V((cols, cols), BF), V((cols, cols), BF),
            V((owners, rows, rank), F32), V((owners, rows, rank), F32), V((shards, rows, rank), F32), V((shards, rows, rank), F32),
            sem((shards,)), sem((shards,)), sem((owners,)), sem((owners,)), sem((shards,)), sem((shards,)),
            sem, sem, sem((shards,)), sem((shards,)), sem((shards,)), sem((2,)),
        ],
        compiler_params=pltpu.CompilerParams(
            collective_id=0, has_side_effects=True, vmem_limit_bytes=56 * 1024 * 1024
        ),
        name="enter",
    )(table, gradient, basis)


def body(table, cost, kh_ref, kl_ref, zin_ref, mh_ref, ml_ref, pj_ref, keep_ref, home_ref, z_ref, w_ref, c_ref, xh, xl, ls, rs):
    s_me = lax.axis_index("shard")
    o_me = lax.axis_index("owner")
    shards, part, cols = pj_ref.shape
    count = cost[o_me * shards + s_me]
    keep_ref[0] = jnp.where(count > 0, 0.0, 1.0)
    for j in range(shards):
        home_ref[j] = lax.div(table[o_me * shards + j], shards)
    z_ref[...] = zin_ref[...]

    @pl.loop(0, count)
    def _(it):
        z = split(z_ref[...])
        w_ref[...] = dot3(z, (kh_ref[...], kl_ref[...]), NN)
        w = split(w_ref[...])
        c_ref[...] = dot3(z, w, NT)
        factor(c_ref, xh, xl, ls, rs)
        x = (xh[...], xl[...])
        z_ref[...] = dot3(x, w, NN)

        @pl.when(it == count - 1)
        def _():
            h, l = split(dot3(x, z, NN))
            mh_ref[...] = h
            ml_ref[...] = l

    @pl.when(count == 0)
    def _():
        mh_ref[...] = jnp.zeros_like(mh_ref)
        ml_ref[...] = jnp.zeros_like(ml_ref)

    for s in range(shards):
        pj_ref[s] = z_ref[part * s:part * s + part, :]


def refresh(table, cost, shards, kh, kl, z):
    rank, cols = z.shape
    smem = pl.BlockSpec(memory_space=pltpu.SMEM)
    vmem = pl.BlockSpec(memory_space=V)
    return pl.pallas_call(
        body,
        out_shape=(
            jax.ShapeDtypeStruct((rank, cols), BF),
            jax.ShapeDtypeStruct((rank, cols), BF),
            jax.ShapeDtypeStruct((shards, rank // shards, cols), F32),
            jax.ShapeDtypeStruct((1,), F32),
            jax.ShapeDtypeStruct((shards,), jnp.int32),
        ),
        in_specs=[smem, smem, vmem, vmem, vmem],
        out_specs=(vmem, vmem, vmem, smem, smem),
        scratch_shapes=[
            V((rank, cols), F32), V((rank, cols), F32), V((rank, rank), F32), V((rank, rank), BF), V((rank, rank), BF),
            V((3 * rank, rank), BF), V((3 * rank, 2 * rank), BF),
        ],
        compiler_params=pltpu.CompilerParams(vmem_limit_bytes=56 * 1024 * 1024),
        name="refresh",
    )(table, cost, kh, kl, z)


BETA_ONE = 0.9
BETA_TWO = 0.99
EPSILON = 1e-08
GALORE_SCALE = 0.25
CHUNKS = 2


def adam(one, two, projected):
    one = BETA_ONE * one + (1.0 - BETA_ONE) * projected
    two = BETA_TWO * two + (1.0 - BETA_TWO) * projected * projected
    return one, two


def leave_body(shards, owners, table, keep_ref, mh_ref, ml_ref, pj_ref, gh_hbm, gl_hbm, p_hbm, one_ref, two_ref,
               back_a, back_b, normed_out, proj_out,
               gh, gl, p_in, pn, pj1a, pj1b, pj_stage, pj2, pn1a, pn1b, pn_stage, normed,
               h_sem, l_sem, i_sem, j_send, j_recv, jo_send, jo_recv, p_send, p_recv, po_send, po_recv,
               n_send, n_recv, f_send, f_recv, own_sem):
    s_me = lax.axis_index("shard")
    o_me = lax.axis_index("owner")
    slots = one_ref.shape[0]
    pn1, back, pj1 = (pn1a, pn1b), (back_a, back_b), (pj1a, pj1b)
    half = pj1a.shape[1]
    chunk = pn1a.shape[1]

    def at_shard(d):
        return lax.rem(s_me + d, shards)

    def from_shard(d):
        return lax.rem(s_me - d + shards, shards)

    def rows(c):
        return slice(c * chunk, (c + 1) * chunk)

    def loads(t):
        return (
            pltpu.make_async_copy(gh_hbm.at[t], gh.at[t], h_sem.at[t]),
            pltpu.make_async_copy(gl_hbm.at[t], gl.at[t], l_sem.at[t]),
            pltpu.make_async_copy(p_hbm.at[t], p_in.at[t], i_sem.at[t]),
        )

    @pl.loop(1, shards + 1)
    def _(d):
        for copy in loads(at_shard(d)):
            copy.start()

    greet((("shard", shards), ("owner", owners)))

    def part(q):
        return slice(q * half, (q + 1) * half)

    for q in range(2):

        @pl.loop(1, shards)
        def _(d):
            t = at_shard(d)
            remote(pj_ref.at[t, part(q)], pj1[q].at[s_me], j_send.at[q, d], j_recv.at[q, d], "shard", t).start()

        pj1[q][s_me] = pj_ref[s_me, part(q)]

    keep = keep_ref[0]

    def basis_rows(t, c):
        return dot3((gh[t, rows(c)], gl[t, rows(c)]), (mh_ref[...], ml_ref[...]), NT) + keep * p_in[t, rows(c)]

    def send_basis(c):
        @pl.loop(1, shards)
        def _(d):
            t = at_shard(d)
            if c == 0:
                for copy in loads(t):
                    copy.wait()
            pn[c, t] = basis_rows(t, c)
            remote(pn.at[c, t], pn1[c].at[s_me], p_send.at[c, d], p_recv.at[c, d], "shard", t).start()

        if c == 0:
            for copy in loads(s_me):
                copy.wait()
        pn1[c][s_me] = basis_rows(s_me, c)

    def expert_at(owner):
        found = 0
        for j in range(slots):
            e = table[owner * slots + j]
            found = jnp.where(lax.div(e, slots) == o_me, lax.rem(e, slots), found)
        return found

    send_basis(0)
    for q in range(2):

        @pl.loop(1, shards)
        def _(d):
            t = at_shard(d)
            remote(pj_ref.at[t, part(q)], pj1[q].at[from_shard(d)], j_send.at[q, d], j_recv.at[q, d], "shard", t).wait()

        for k, t, _ in partners(o_me):
            pj_stage[q, t] = pj1[q][expert_at(t)]
            remote(pj_stage.at[q, t], pj2.at[q, o_me], jo_send.at[q, k], jo_recv.at[q, k], "owner", t).start()

        pj2[q, o_me] = pj1[q][expert_at(o_me)]

    for c in range(1, CHUNKS):
        send_basis(c)

    own = []
    for c in range(CHUNKS):

        @pl.loop(1, shards)
        def _(d):
            t = at_shard(d)
            remote(pn.at[c, t], pn1[c].at[from_shard(d)], p_send.at[c, d], p_recv.at[c, d], "shard", t).wait()

        for k, t, _ in partners(o_me):
            pn_stage[c, t] = pn1[c][expert_at(t)]
            remote(pn_stage.at[c, t], back[c].at[o_me], po_send.at[c, k], po_recv.at[c, k], "owner", t).start()

        pn_stage[c, o_me] = pn1[c][expert_at(o_me)]
        own.append(pltpu.make_async_copy(pn_stage.at[c, o_me], back[c].at[o_me], own_sem.at[c]))
        own[-1].start()

    for q in range(2):
        for k, t, source in partners(o_me):
            remote(pj_stage.at[q, t], pj2.at[q, source], jo_send.at[q, k], jo_recv.at[q, k], "owner", t).wait()

    @pl.loop(0, slots)
    def _(j):
        home = lax.div(table[o_me * slots + j], slots)
        projected = jnp.concatenate([pj2[0, home], pj2[1, home]], axis=0)
        proj_out[j] = projected
        one, two = adam(one_ref[j], two_ref[j], projected)
        normed[j] = one / (jnp.sqrt(two) + EPSILON)

    other = s_me + 1 - 2 * lax.rem(s_me, 2)
    chips = shards // 2

    @pl.loop(1, chips)
    def _(k):
        t = at_shard(2 * k)
        remote(normed, normed_out.at[s_me], n_send.at[k], n_recv.at[k], "shard", t).start()

    remote(normed, normed_out.at[s_me], f_send.at[0], f_recv.at[0], "shard", other).start()
    own.append(pltpu.make_async_copy(normed, normed_out.at[s_me], own_sem.at[CHUNKS]))
    own[-1].start()

    @pl.loop(1, chips)
    def _(k):
        f = from_shard(2 * k)
        remote(normed, normed_out.at[f], n_send.at[k], n_recv.at[k], "shard", at_shard(2 * k)).wait()
        remote(normed_out.at[f], normed_out.at[f], f_send.at[k], f_recv.at[k], "shard", other).start()

    @pl.loop(0, chips)
    def _(k):
        g = lax.rem(other - 2 * k + shards, shards)
        remote(normed, normed_out.at[g], f_send.at[k], f_recv.at[k], "shard", other).wait()

    for copy in own:
        copy.wait()

    for c in range(CHUNKS):

        for k, t, source in partners(o_me):
            remote(pn_stage.at[c, t], back[c].at[source], po_send.at[c, k], po_recv.at[c, k], "owner", t).wait()


def leave(table, keep, mh, ml, pj, gh, gl, p, one, two):
    shards, rows, cols = gh.shape
    rank = p.shape[2]
    part = pj.shape[1]
    slots = one.shape[0]
    owners = table.shape[0] // slots
    chunk = rows // CHUNKS
    dma = pltpu.SemaphoreType.DMA
    smem = pl.BlockSpec(memory_space=pltpu.SMEM)
    vmem = pl.BlockSpec(memory_space=V)
    hbm = pl.BlockSpec(memory_space=pl.ANY)
    return pl.pallas_call(
        functools.partial(leave_body, shards, owners),
        out_shape=(
            jax.ShapeDtypeStruct((owners, chunk, rank), F32),
            jax.ShapeDtypeStruct((owners, chunk, rank), F32),
            jax.ShapeDtypeStruct((shards, slots, part, cols), F32),
            jax.ShapeDtypeStruct((slots, part, cols), F32),
        ),
        in_specs=[smem, smem, vmem, vmem, vmem, hbm, hbm, hbm, vmem, vmem],
        out_specs=(hbm, hbm, hbm, vmem),
        scratch_shapes=[
            V(gh.shape, BF), V(gh.shape, BF), V(p.shape, F32), V((CHUNKS, shards, chunk, rank), F32),
            V((shards, part // 2, cols), F32), V((shards, part // 2, cols), F32),
            V((2, owners, part // 2, cols), F32), V((2, owners, part // 2, cols), F32),
            V((shards, chunk, rank), F32), V((shards, chunk, rank), F32), V((CHUNKS, owners, chunk, rank), F32),
            V((slots, part, cols), F32),
            dma((shards,)), dma((shards,)), dma((shards,)),
            dma((2, shards)), dma((2, shards)), dma((2, owners)), dma((2, owners)),
            dma((CHUNKS, shards)), dma((CHUNKS, shards)), dma((CHUNKS, owners)), dma((CHUNKS, owners)),
            dma((shards // 2,)), dma((shards // 2,)), dma((shards // 2,)), dma((shards // 2,)), dma((CHUNKS + 1,)),
        ],
        compiler_params=pltpu.CompilerParams(
            collective_id=1, has_side_effects=True, vmem_limit_bytes=56 * 1024 * 1024
        ),
        name="leave",
    )(table, keep, mh, ml, pj, gh, gl, p, one, two)


def finish_body(home_ref, back_a, back_b, normed_ref, proj_ref, one_ref, two_ref, basis_out, one_out, two_out, update_out,
                basis, normed, proj, one, two, update, b_sem, n_sem, m_sem, bo_sem, u_sem, mo_sem):
    slots, rows, _ = basis.shape
    chunk = rows // 2
    shards, part, cols = normed.shape[1:]

    def halves(j):
        return [
            pltpu.make_async_copy(ref.at[home_ref[j]], basis.at[j, c * chunk:(c + 1) * chunk], b_sem.at[c, j])
            for c, ref in enumerate((back_a, back_b))
        ]

    def step(j):
        return pltpu.make_async_copy(normed_ref.at[:, j], normed.at[j], n_sem.at[j])

    def basis_save(j):
        return pltpu.make_async_copy(basis.at[j], basis_out.at[j], bo_sem.at[j])

    def update_save(j):
        return pltpu.make_async_copy(update.at[j], update_out.at[j], u_sem.at[j])

    moments = [
        pltpu.make_async_copy(src, dst, m_sem.at[k])
        for k, (src, dst) in enumerate(((proj_ref, proj), (one_ref, one), (two_ref, two)))
    ]

    @pl.loop(0, slots)
    def _(j):
        for copy in halves(j):
            copy.start()
        step(j).start()

    for copy in moments:
        copy.start()

    @pl.loop(0, slots)
    def _(j):
        for copy in halves(j):
            copy.wait()
        basis_save(j).start()
        step(j).wait()
        product = dot3(split(basis[j]), split(normed[j].reshape(shards * part, cols)), NN)
        update[j] = (GALORE_SCALE * product).astype(BF)
        update_save(j).start()

    for copy in moments:
        copy.wait()
    one[...], two[...] = adam(one[...], two[...], proj[...])
    saves = [
        pltpu.make_async_copy(src, dst, mo_sem.at[k]) for k, (src, dst) in enumerate(((one, one_out), (two, two_out)))
    ]
    for copy in saves:
        copy.start()

    @pl.loop(0, slots)
    def _(j):
        basis_save(j).wait()
        update_save(j).wait()

    for copy in saves:
        copy.wait()


def finish(home, back_a, back_b, normed, projected, one, two):
    shards, slots, part, cols = normed.shape
    _, chunk, rank = back_a.shape
    dma = pltpu.SemaphoreType.DMA
    hbm = pl.BlockSpec(memory_space=pl.ANY)
    return pl.pallas_call(
        finish_body,
        out_shape=(
            jax.ShapeDtypeStruct((slots, 2 * chunk, rank), F32),
            jax.ShapeDtypeStruct(one.shape, F32),
            jax.ShapeDtypeStruct(two.shape, F32),
            jax.ShapeDtypeStruct((slots, 2 * chunk, cols), BF),
        ),
        in_specs=[pl.BlockSpec(memory_space=pltpu.SMEM)] + [hbm] * 6,
        out_specs=(hbm,) * 4,
        scratch_shapes=[
            V((slots, 2 * chunk, rank), F32), V((slots, shards, part, cols), F32),
            V(one.shape, F32), V(one.shape, F32), V(one.shape, F32), V((slots, 2 * chunk, cols), BF),
            dma((2, slots)), dma((slots,)), dma((3,)), dma((slots,)), dma((slots,)), dma((2,)),
        ],
        compiler_params=pltpu.CompilerParams(vmem_limit_bytes=60 * 1024 * 1024),
        name="finish",
    )(home, back_a, back_b, normed, projected, one, two)


def on_device(gradient, old_basis, moment_one, moment_two, slot_expert, cost):
    gh, gl, kh, kl, z, p = enter(slot_expert, gradient, old_basis)
    mh, ml, pj, keep, home = refresh(slot_expert, cost, gradient.shape[0], kh, kl, z)
    back_a, back_b, normed, projected = leave(slot_expert, keep, mh, ml, pj, gh, gl, p, moment_one, moment_two)
    return tuple(finish(home, back_a, back_b, normed, projected, moment_one, moment_two))


def solution(mesh):
    spec = P("owner", "shard", None)
    return jax.shard_map(
        on_device, mesh=mesh, in_specs=(spec,) * 4 + (P(), P()), out_specs=(spec,) * 4, check_vma=False
    )
```

```python
import functools
import jax, jax.numpy as jnp
from jax import lax
from jax.experimental import pallas as pl
from jax.sharding import PartitionSpec as P
from jax.experimental.pallas import tpu as pltpu

BF = jnp.bfloat16
F32 = jnp.float32

def split(x):
    hi = x.astype(BF)
    return hi, (x - hi.astype(F32)).astype(BF)

def mm(a, b, dims):
    return lax.dot_general(a, b, (dims, ((), ())), preferred_element_type=F32)

NN = ((1,), (0,))
TN = ((0,), (0,))
NT = ((1,), (1,))

def dot3(a, b, dims):
    ah, al = a
    bh, bl = b
    return mm(ah, bh, dims) + (mm(ah, bl, dims) + mm(al, bh, dims))

PANEL, GROUP = 32, 16


def factor(c_ref, xh, xl, ls, rs):
    nb, sub_nb = PANEL, GROUP
    n = c_ref.shape[0]
    tile = lax.broadcasted_iota(jnp.int32, (8, 128), 0)
    for p in range(n // nb):
        lo = p * nb
        need = [h for h in range(4) if (h < 2 and h * 128 + 128 > lo) or (h >= 2 and (h - 2) * 128 < lo + nb)]
        sub = lax.broadcasted_iota(jnp.int32, (nb, 128), 0)
        s = {}
        for h in need:
            if h < 2:
                s[h] = c_ref[lo:lo + nb, 128 * h:128 * h + 128]
            else:
                l = lax.broadcasted_iota(jnp.int32, (nb, 128), 1) + 128 * (h - 2)
                s[h] = jnp.where(l == sub + lo, 1.0, 0.0)
        a0, a1 = need[0] * 128, need[-1] * 128 + 128
        cuts = []
        if p > 1:
            cuts.append((0, 3 * (lo - nb)))
        if p > 0:
            cuts.append((3 * (lo - nb), 3 * lo))
        for (x, y) in cuts:
            d = mm(ls[x:y, lo:lo + nb], rs[x:y, a0:a1], TN)
            for h in need:
                s[h] = s[h] - d[:, 128 * h - a0:128 * h - a0 + 128]
        hd = lo // 128
        off = lo - hd * 128
        pivots = []
        done = []
        for g in range(nb // sub_nb):
            b = g * sub_nb
            cols = [jnp.broadcast_to(s[hd][:, off + b + k:off + b + k + 1], (nb - b, 128)) for k in range(sub_nb)]
            for j in range(sub_nb):
                jj = j % 8
                d = cols[j][jj:jj + 1, :]
                pivots.append(d)
                m = cols[j] * (1.0 / d)
                for k in range(j + 1, sub_nb):
                    cols[k] = cols[k] - m * cols[k][jj:jj + 1, :]
                low = jnp.where(tile > jj, m[0:8], 0.0)
                if m.shape[0] > 8:
                    low = jnp.concatenate([low, m[8:]], axis=0)
                for h in need:
                    s[h] = s[h] - low * s[h][jj:jj + 1, :]
                if jj == 7:
                    done.append({h: s[h][0:8] for h in need})
                    if m.shape[0] > 8:
                        s = {h: s[h][8:] for h in need}
                        cols = [t[8:] for t in cols]
        scale = lax.rsqrt(jnp.concatenate(pivots, axis=0))
        for h in range(4):
            if h not in need:
                o = jnp.zeros((nb, 128), F32)
            else:
                o = jnp.concatenate([t[h] for t in done], axis=0) * scale
                if h == hd:
                    l = lax.broadcasted_iota(jnp.int32, (nb, 128), 1) + 128 * h
                    o = jnp.where(l >= sub + lo, o, 0.0)
            cs = slice(128 * h, 128 * h + 128)
            hi = o.astype(BF)
            lw = (o - hi.astype(F32)).astype(BF)
            if h >= 2:
                xs = slice(128 * (h - 2), 128 * (h - 2) + 128)
                xh[lo:lo + nb, xs] = hi
                xl[lo:lo + nb, xs] = lw
            b = 3 * lo
            rs[b:b + nb, cs] = hi
            rs[b + nb:b + 2 * nb, cs] = lw
            rs[b + 2 * nb:b + 3 * nb, cs] = hi
            if h < 2:
                ls[b:b + nb, cs] = hi
                ls[b + nb:b + 2 * nb, cs] = hi
                ls[b + 2 * nb:b + 3 * nb, cs] = lw


MESH = pl.DeviceIdType.MESH
V = pltpu.VMEM


def greet(groups):
    barrier = pltpu.get_barrier_semaphore()
    total = 0
    for axis, size in groups:
        me = lax.axis_index(axis)

        @pl.loop(1, size)
        def _(d):
            pl.semaphore_signal(barrier, inc=1, device_id={axis: lax.rem(me + d, size)}, device_id_type=MESH)

        total += size - 1
    pl.semaphore_wait(barrier, total)


STEPS = (
    (1, 1), (3, 3), (1, 3), (3, 1), (1, 0), (0, 1), (3, 0), (0, 3), (2, 0), (0, 2), (2, 2), (2, 1), (1, 2), (2, 3), (3, 2),
)
SIDE = 4


def partners(me):
    z, y = lax.div(me, SIDE), lax.rem(me, SIDE)
    for k, (dy, dz) in enumerate(STEPS):
        to = lax.rem(z + dz, SIDE) * SIDE + lax.rem(y + dy, SIDE)
        source = lax.rem(z + SIDE - dz, SIDE) * SIDE + lax.rem(y + SIDE - dy, SIDE)
        yield k, to, source


def remote(src, dst, send, recv, axis, target):
    return pltpu.make_async_remote_copy(
        src_ref=src, dst_ref=dst, send_sem=send, recv_sem=recv, device_id={axis: target}, device_id_type=MESH
    )


def slot_at(table, owner, slots, home):
    found = 0
    for j in range(slots):
        found = jnp.where(lax.div(table[owner * slots + j], slots) == home, j, found)
    return found


def enter_body(shards, owners, table, g_ref, b_hbm, gh_out, gl_out, kh_out, kl_out, z_out, p_out,
               b_ref, gland, gh, gl, kacc, kh, kl, stage, landed, stage2, pland,
               g_send, g_recv, a_send, a_recv, b_send, b_recv, own_sem, in_sem, h_sem, l_sem, p_sem, k_sem):
    s_me = lax.axis_index("shard")
    o_me = lax.axis_index("owner")
    load = pltpu.make_async_copy(b_hbm, b_ref, in_sem)
    load.start()
    greet((("shard", shards), ("owner", owners)))
    slots = shards

    def at_shard(d):
        return lax.rem(s_me + d, shards)

    def from_shard(d):
        return lax.rem(s_me - d + shards, shards)

    own = pltpu.make_async_copy(g_ref.at[s_me], gland.at[s_me], own_sem)
    own.start()

    @pl.loop(1, shards)
    def _(d):
        t = at_shard(d)
        remote(g_ref.at[t], gland.at[s_me], g_send.at[d], g_recv.at[d], "shard", t).start()

    load.wait()
    for k, t, _ in partners(o_me):
        stage[t] = b_ref[slot_at(table, o_me, slots, t)]
        remote(stage.at[t], landed.at[o_me], a_send.at[k], a_recv.at[k], "owner", t).start()

    landed[o_me] = b_ref[slot_at(table, o_me, slots, o_me)]
    kacc[...] = jnp.zeros_like(kacc)
    own.wait()
    tiles = kacc.shape[0] // 256

    def gram(f):
        h, l = split(gland[f])
        gh[f] = h
        gl[f] = l
        pltpu.make_async_copy(gh.at[f], gh_out.at[f], h_sem.at[f]).start()
        pltpu.make_async_copy(gl.at[f], gl_out.at[f], l_sem.at[f]).start()
        for a in range(tiles):
            ra = slice(256 * a, 256 * a + 256)
            for b in range(a, tiles):
                rb = slice(256 * b, 256 * b + 256)
                kacc[ra, rb] += dot3((h[:, ra], l[:, ra]), (h[:, rb], l[:, rb]), TN)

    gram(s_me)

    def take_gram(d):
        f = from_shard(d)
        remote(g_ref.at[at_shard(d)], gland.at[f], g_send.at[d], g_recv.at[d], "shard", at_shard(d)).wait_recv()
        gram(f)

    half = EARLY
    pl.loop(1, half)(take_gram)

    for k, t, source in partners(o_me):
        remote(stage.at[t], landed.at[source], a_send.at[k], a_recv.at[k], "owner", t).wait()

    def holder(i):
        def add(o, found):
            for j in range(slots):
                found = jnp.where(table[o * slots + j] == o_me * slots + i, o, found)
            return found

        return lax.fori_loop(0, owners, add, 0)

    @pl.loop(1, shards)
    def _(d):
        t = at_shard(d)
        stage2[t] = landed[holder(t)]
        remote(stage2.at[t], pland.at[s_me], b_send.at[d], b_recv.at[d], "shard", t).start()

    pland[s_me] = landed[holder(s_me)]
    pl.loop(half, shards)(take_gram)

    for a in range(tiles):
        ra = slice(256 * a, 256 * a + 256)
        for b in range(a, tiles):
            rb = slice(256 * b, 256 * b + 256)
            h, l = split(kacc[ra, rb])
            kh[ra, rb] = h
            kl[ra, rb] = l
            if b > a:
                h, l = split(kacc[ra, rb].T)
                kh[rb, ra] = h
                kl[rb, ra] = l

    save_k = (pltpu.make_async_copy(kh, kh_out, k_sem.at[0]), pltpu.make_async_copy(kl, kl_out, k_sem.at[1]))
    for copy in save_k:
        copy.start()

    def project(f):
        pltpu.make_async_copy(pland.at[f], p_out.at[f], p_sem.at[f]).start()
        return dot3(split(pland[f]), (gh[f], gl[f]), TN)

    z_out[...] = project(s_me)

    @pl.loop(1, shards)
    def _(d):
        f = from_shard(d)
        remote(stage2.at[at_shard(d)], pland.at[f], b_send.at[d], b_recv.at[d], "shard", at_shard(d)).wait()
        z_out[...] += project(f)

    @pl.loop(1, shards)
    def _(d):
        remote(g_ref.at[at_shard(d)], gland.at[from_shard(d)], g_send.at[d], g_recv.at[d], "shard", at_shard(d)).wait_send()

    @pl.loop(0, shards)
    def _(f):
        pltpu.make_async_copy(gh.at[f], gh_out.at[f], h_sem.at[f]).wait()
        pltpu.make_async_copy(gl.at[f], gl_out.at[f], l_sem.at[f]).wait()
        pltpu.make_async_copy(pland.at[f], p_out.at[f], p_sem.at[f]).wait()

    for copy in save_k:
        copy.wait()


EARLY = 5


def enter(table, gradient, basis):
    shards, rows, cols = gradient.shape
    rank = basis.shape[2]
    owners = table.shape[0] // basis.shape[0]
    sem = pltpu.SemaphoreType.DMA
    smem = pl.BlockSpec(memory_space=pltpu.SMEM)
    vmem = pl.BlockSpec(memory_space=V)
    hbm = pl.BlockSpec(memory_space=pl.ANY)
    return pl.pallas_call(
        functools.partial(enter_body, shards, owners),
        out_shape=(
            jax.ShapeDtypeStruct((shards, rows, cols), BF),
            jax.ShapeDtypeStruct((shards, rows, cols), BF),
            jax.ShapeDtypeStruct((cols, cols), BF),
            jax.ShapeDtypeStruct((cols, cols), BF),
            jax.ShapeDtypeStruct((rank, cols), F32),
            jax.ShapeDtypeStruct((shards, rows, rank), F32),
        ),
        in_specs=[smem, hbm, hbm],
        out_specs=(hbm, hbm, hbm, hbm, vmem, hbm),
        scratch_shapes=[
            V((shards, rows, rank), F32), V((shards, rows, cols), F32), V((shards, rows, cols), BF), V((shards, rows, cols), BF), V((cols, cols), F32), V((cols, cols), BF), V((cols, cols), BF),
            V((owners, rows, rank), F32), V((owners, rows, rank), F32), V((shards, rows, rank), F32), V((shards, rows, rank), F32),
            sem((shards,)), sem((shards,)), sem((owners,)), sem((owners,)), sem((shards,)), sem((shards,)),
            sem, sem, sem((shards,)), sem((shards,)), sem((shards,)), sem((2,)),
        ],
        compiler_params=pltpu.CompilerParams(
            collective_id=0, has_side_effects=True, vmem_limit_bytes=56 * 1024 * 1024
        ),
        name="enter",
    )(table, gradient, basis)


def body(table, cost, kh_ref, kl_ref, zin_ref, mh_ref, ml_ref, pj_ref, keep_ref, home_ref, z_ref, w_ref, c_ref, xh, xl, ls, rs):
    s_me = lax.axis_index("shard")
    o_me = lax.axis_index("owner")
    shards, part, cols = pj_ref.shape
    count = cost[o_me * shards + s_me]
    keep_ref[0] = jnp.where(count > 0, 0.0, 1.0)
    for j in range(shards):
        home_ref[j] = lax.div(table[o_me * shards + j], shards)
    z_ref[...] = zin_ref[...]

    @pl.loop(0, count)
    def _(it):
        z = split(z_ref[...])
        w_ref[...] = dot3(z, (kh_ref[...], kl_ref[...]), NN)
        w = split(w_ref[...])
        c_ref[...] = dot3(z, w, NT)
        factor(c_ref, xh, xl, ls, rs)
        x = (xh[...], xl[...])
        z_ref[...] = dot3(x, w, NN)

        @pl.when(it == count - 1)
        def _():
            h, l = split(dot3(x, z, NN))
            mh_ref[...] = h
            ml_ref[...] = l

    @pl.when(count == 0)
    def _():
        mh_ref[...] = jnp.zeros_like(mh_ref)
        ml_ref[...] = jnp.zeros_like(ml_ref)

    for s in range(shards):
        pj_ref[s] = z_ref[part * s:part * s + part, :]


def refresh(table, cost, shards, kh, kl, z):
    rank, cols = z.shape
    smem = pl.BlockSpec(memory_space=pltpu.SMEM)
    vmem = pl.BlockSpec(memory_space=V)
    return pl.pallas_call(
        body,
        out_shape=(
            jax.ShapeDtypeStruct((rank, cols), BF),
            jax.ShapeDtypeStruct((rank, cols), BF),
            jax.ShapeDtypeStruct((shards, rank // shards, cols), F32),
            jax.ShapeDtypeStruct((1,), F32),
            jax.ShapeDtypeStruct((shards,), jnp.int32),
        ),
        in_specs=[smem, smem, vmem, vmem, vmem],
        out_specs=(vmem, vmem, vmem, smem, smem),
        scratch_shapes=[
            V((rank, cols), F32), V((rank, cols), F32), V((rank, rank), F32), V((rank, rank), BF), V((rank, rank), BF),
            V((3 * rank, rank), BF), V((3 * rank, 2 * rank), BF),
        ],
        compiler_params=pltpu.CompilerParams(vmem_limit_bytes=56 * 1024 * 1024),
        name="refresh",
    )(table, cost, kh, kl, z)


BETA_ONE = 0.9
BETA_TWO = 0.99
EPSILON = 1e-08
GALORE_SCALE = 0.25
CHUNKS = 2


def adam(one, two, projected):
    one = BETA_ONE * one + (1.0 - BETA_ONE) * projected
    two = BETA_TWO * two + (1.0 - BETA_TWO) * projected * projected
    return one, two


def leave_body(shards, owners, table, keep_ref, mh_ref, ml_ref, pj_ref, gh_hbm, gl_hbm, p_hbm, one_hbm, two_hbm,
               back_a, back_b, normed_out, proj_out,
               one_ref, two_ref, gh, gl, p_in, pn, pj1a, pj1b, pj_stage, pj2, pn1a, pn1b, pn_stage, normed,
               h_sem, l_sem, i_sem, j_send, j_recv, jo_send, jo_recv, p_send, p_recv, po_send, po_recv,
               n_send, n_recv, f_send, f_recv, own_sem, m_sem):
    s_me = lax.axis_index("shard")
    o_me = lax.axis_index("owner")
    slots = one_ref.shape[0]
    pn1, back, pj1 = (pn1a, pn1b), (back_a, back_b), (pj1a, pj1b)
    half = pj1a.shape[1]
    chunk = pn1a.shape[1]

    def at_shard(d):
        return lax.rem(s_me + d, shards)

    def from_shard(d):
        return lax.rem(s_me - d + shards, shards)

    def rows(c):
        return slice(c * chunk, (c + 1) * chunk)

    def loads(t):
        return (
            pltpu.make_async_copy(gh_hbm.at[t], gh.at[t], h_sem.at[t]),
            pltpu.make_async_copy(gl_hbm.at[t], gl.at[t], l_sem.at[t]),
            pltpu.make_async_copy(p_hbm.at[t], p_in.at[t], i_sem.at[t]),
        )

    @pl.loop(1, shards + 1)
    def _(d):
        for copy in loads(at_shard(d)):
            copy.start()

    moments = (pltpu.make_async_copy(one_hbm, one_ref, m_sem.at[0]), pltpu.make_async_copy(two_hbm, two_ref, m_sem.at[1]))
    for copy in moments:
        copy.start()
    greet((("shard", shards), ("owner", owners)))

    def part(q):
        return slice(q * half, (q + 1) * half)

    for q in range(2):

        @pl.loop(1, shards)
        def _(d):
            t = at_shard(d)
            remote(pj_ref.at[t, part(q)], pj1[q].at[s_me], j_send.at[q, d], j_recv.at[q, d], "shard", t).start()

        pltpu.make_async_copy(pj_ref.at[s_me, part(q)], pj1[q].at[s_me], m_sem.at[2 + q]).start()

    keep = keep_ref[0]

    def basis_rows(t, c):
        return dot3((gh[t, rows(c)], gl[t, rows(c)]), (mh_ref[...], ml_ref[...]), NT) + keep * p_in[t, rows(c)]

    def send_basis(c):
        @pl.loop(1, shards)
        def _(d):
            t = at_shard(d)
            if c == 0:
                for copy in loads(t):
                    copy.wait()
            pn[c, t] = basis_rows(t, c)
            remote(pn.at[c, t], pn1[c].at[s_me], p_send.at[c, d], p_recv.at[c, d], "shard", t).start()

        if c == 0:
            for copy in loads(s_me):
                copy.wait()
        pn1[c][s_me] = basis_rows(s_me, c)

    def expert_at(owner):
        found = 0
        for j in range(slots):
            e = table[owner * slots + j]
            found = jnp.where(lax.div(e, slots) == o_me, lax.rem(e, slots), found)
        return found

    for q in range(2):

        @pl.loop(1, shards)
        def _(d):
            t = at_shard(d)
            remote(pj_ref.at[t, part(q)], pj1[q].at[from_shard(d)], j_send.at[q, d], j_recv.at[q, d], "shard", t).wait()

        pltpu.make_async_copy(pj_ref.at[s_me, part(q)], pj1[q].at[s_me], m_sem.at[2 + q]).wait()
        for k, t, _ in partners(o_me):
            pj_stage[q, t] = pj1[q][expert_at(t)]
            remote(pj_stage.at[q, t], pj2.at[q, o_me], jo_send.at[q, k], jo_recv.at[q, k], "owner", t).start()

        pj2[q, o_me] = pj1[q][expert_at(o_me)]

    for c in range(0, CHUNKS):
        send_basis(c)

    own = []

    def pass_basis(c):

        @pl.loop(1, shards)
        def _(d):
            t = at_shard(d)
            remote(pn.at[c, t], pn1[c].at[from_shard(d)], p_send.at[c, d], p_recv.at[c, d], "shard", t).wait()

        for k, t, _ in partners(o_me):
            pn_stage[c, t] = pn1[c][expert_at(t)]
            remote(pn_stage.at[c, t], back[c].at[o_me], po_send.at[c, k], po_recv.at[c, k], "owner", t).start()

        pn_stage[c, o_me] = pn1[c][expert_at(o_me)]
        own.append(pltpu.make_async_copy(pn_stage.at[c, o_me], back[c].at[o_me], own_sem.at[c]))
        own[-1].start()

    for c in range(CHUNKS):
        pass_basis(c)

    for q in range(2):
        for k, t, source in partners(o_me):
            remote(pj_stage.at[q, t], pj2.at[q, source], jo_send.at[q, k], jo_recv.at[q, k], "owner", t).wait()

    for copy in moments:
        copy.wait()

    @pl.loop(0, slots)
    def _(j):
        home = lax.div(table[o_me * slots + j], slots)
        projected = jnp.concatenate([pj2[0, home], pj2[1, home]], axis=0)
        proj_out[j] = projected
        one, two = adam(one_ref[j], two_ref[j], projected)
        normed[j] = one / (jnp.sqrt(two) + EPSILON)

    other = s_me + 1 - 2 * lax.rem(s_me, 2)
    chips = shards // 2

    @pl.loop(1, chips)
    def _(k):
        t = at_shard(2 * k)
        remote(normed, normed_out.at[s_me], n_send.at[k], n_recv.at[k], "shard", t).start()

    remote(normed, normed_out.at[s_me], f_send.at[0], f_recv.at[0], "shard", other).start()
    own.append(pltpu.make_async_copy(normed, normed_out.at[s_me], own_sem.at[CHUNKS]))
    own[-1].start()

    @pl.loop(1, chips)
    def _(k):
        f = from_shard(2 * k)
        remote(normed, normed_out.at[f], n_send.at[k], n_recv.at[k], "shard", at_shard(2 * k)).wait()
        remote(normed_out.at[f], normed_out.at[f], f_send.at[k], f_recv.at[k], "shard", other).start()

    @pl.loop(0, chips)
    def _(k):
        g = lax.rem(other - 2 * k + shards, shards)
        remote(normed, normed_out.at[g], f_send.at[k], f_recv.at[k], "shard", other).wait()

    for copy in own:
        copy.wait()

    for c in range(CHUNKS):

        for k, t, source in partners(o_me):
            remote(pn_stage.at[c, t], back[c].at[source], po_send.at[c, k], po_recv.at[c, k], "owner", t).wait()


def leave(table, keep, mh, ml, pj, gh, gl, p, one, two):
    shards, rows, cols = gh.shape
    rank = p.shape[2]
    part = pj.shape[1]
    slots = one.shape[0]
    owners = table.shape[0] // slots
    chunk = rows // CHUNKS
    dma = pltpu.SemaphoreType.DMA
    smem = pl.BlockSpec(memory_space=pltpu.SMEM)
    vmem = pl.BlockSpec(memory_space=V)
    hbm = pl.BlockSpec(memory_space=pl.ANY)
    return pl.pallas_call(
        functools.partial(leave_body, shards, owners),
        out_shape=(
            jax.ShapeDtypeStruct((owners, chunk, rank), F32),
            jax.ShapeDtypeStruct((owners, chunk, rank), F32),
            jax.ShapeDtypeStruct((shards, slots, part, cols), F32),
            jax.ShapeDtypeStruct((slots, part, cols), F32),
        ),
        in_specs=[smem, smem, vmem, vmem] + [hbm] * 6,
        out_specs=(hbm, hbm, hbm, vmem),
        scratch_shapes=[
            V(one.shape, F32), V(two.shape, F32), V(gh.shape, BF), V(gh.shape, BF), V(p.shape, F32), V((CHUNKS, shards, chunk, rank), F32),
            V((shards, part // 2, cols), F32), V((shards, part // 2, cols), F32),
            V((2, owners, part // 2, cols), F32), V((2, owners, part // 2, cols), F32),
            V((shards, chunk, rank), F32), V((shards, chunk, rank), F32), V((CHUNKS, owners, chunk, rank), F32),
            V((slots, part, cols), F32),
            dma((shards,)), dma((shards,)), dma((shards,)),
            dma((2, shards)), dma((2, shards)), dma((2, owners)), dma((2, owners)),
            dma((CHUNKS, shards)), dma((CHUNKS, shards)), dma((CHUNKS, owners)), dma((CHUNKS, owners)),
            dma((shards // 2,)), dma((shards // 2,)), dma((shards // 2,)), dma((shards // 2,)), dma((CHUNKS + 1,)), dma((4,)),
        ],
        compiler_params=pltpu.CompilerParams(
            collective_id=1, has_side_effects=True, vmem_limit_bytes=56 * 1024 * 1024
        ),
        name="leave",
    )(table, keep, mh, ml, pj, gh, gl, p, one, two)


def finish_body(home_ref, back_a, back_b, normed_ref, proj_ref, one_ref, two_ref, basis_out, one_out, two_out, update_out,
                basis, normed, proj, one, two, update, b_sem, n_sem, m_sem, bo_sem, u_sem, mo_sem):
    slots, rows, _ = basis.shape
    chunk = rows // 2
    shards, part, cols = normed.shape[1:]

    def halves(j):
        return [
            pltpu.make_async_copy(ref.at[home_ref[j]], basis.at[j, c * chunk:(c + 1) * chunk], b_sem.at[c, j])
            for c, ref in enumerate((back_a, back_b))
        ]

    def step(j):
        return pltpu.make_async_copy(normed_ref.at[:, j], normed.at[j], n_sem.at[j])

    def basis_save(j):
        return pltpu.make_async_copy(basis.at[j], basis_out.at[j], bo_sem.at[j])

    def update_save(j):
        return pltpu.make_async_copy(update.at[j], update_out.at[j], u_sem.at[j])

    moments = [
        pltpu.make_async_copy(src, dst, m_sem.at[k])
        for k, (src, dst) in enumerate(((proj_ref, proj), (one_ref, one), (two_ref, two)))
    ]

    @pl.loop(0, slots)
    def _(j):
        for copy in halves(j):
            copy.start()
        step(j).start()

    for copy in moments:
        copy.start()

    @pl.loop(0, slots)
    def _(j):
        for copy in halves(j):
            copy.wait()
        basis_save(j).start()
        step(j).wait()
        product = dot3(split(basis[j]), split(normed[j].reshape(shards * part, cols)), NN)
        update[j] = (GALORE_SCALE * product).astype(BF)
        update_save(j).start()

    for copy in moments:
        copy.wait()
    one[...], two[...] = adam(one[...], two[...], proj[...])
    saves = [
        pltpu.make_async_copy(src, dst, mo_sem.at[k]) for k, (src, dst) in enumerate(((one, one_out), (two, two_out)))
    ]
    for copy in saves:
        copy.start()

    @pl.loop(0, slots)
    def _(j):
        basis_save(j).wait()
        update_save(j).wait()

    for copy in saves:
        copy.wait()


def finish(home, back_a, back_b, normed, projected, one, two):
    shards, slots, part, cols = normed.shape
    _, chunk, rank = back_a.shape
    dma = pltpu.SemaphoreType.DMA
    hbm = pl.BlockSpec(memory_space=pl.ANY)
    return pl.pallas_call(
        finish_body,
        out_shape=(
            jax.ShapeDtypeStruct((slots, 2 * chunk, rank), F32),
            jax.ShapeDtypeStruct(one.shape, F32),
            jax.ShapeDtypeStruct(two.shape, F32),
            jax.ShapeDtypeStruct((slots, 2 * chunk, cols), BF),
        ),
        in_specs=[pl.BlockSpec(memory_space=pltpu.SMEM)] + [hbm] * 6,
        out_specs=(hbm,) * 4,
        scratch_shapes=[
            V((slots, 2 * chunk, rank), F32), V((slots, shards, part, cols), F32),
            V(one.shape, F32), V(one.shape, F32), V(one.shape, F32), V((slots, 2 * chunk, cols), BF),
            dma((2, slots)), dma((slots,)), dma((3,)), dma((slots,)), dma((slots,)), dma((2,)),
        ],
        compiler_params=pltpu.CompilerParams(vmem_limit_bytes=60 * 1024 * 1024),
        name="finish",
    )(home, back_a, back_b, normed, projected, one, two)


def on_device(gradient, old_basis, moment_one, moment_two, slot_expert, cost):
    gh, gl, kh, kl, z, p = enter(slot_expert, gradient, old_basis)
    mh, ml, pj, keep, home = refresh(slot_expert, cost, gradient.shape[0], kh, kl, z)
    back_a, back_b, normed, projected = leave(slot_expert, keep, mh, ml, pj, gh, gl, p, moment_one, moment_two)
    return tuple(finish(home, back_a, back_b, normed, projected, moment_one, moment_two))


def solution(mesh):
    spec = P("owner", "shard", None)
    return jax.shard_map(
        on_device, mesh=mesh, in_specs=(spec,) * 4 + (P(), P()), out_specs=(spec,) * 4, check_vma=False
    )
```

```python
import functools
import jax, jax.numpy as jnp
from jax import lax
from jax.experimental import pallas as pl
from jax.sharding import PartitionSpec as P
from jax.experimental.pallas import tpu as pltpu

BF = jnp.bfloat16
F32 = jnp.float32

def split(x):
    hi = x.astype(BF)
    return hi, (x - hi.astype(F32)).astype(BF)

def mm(a, b, dims):
    return lax.dot_general(a, b, (dims, ((), ())), preferred_element_type=F32)

NN = ((1,), (0,))
TN = ((0,), (0,))
NT = ((1,), (1,))

def dot3(a, b, dims):
    ah, al = a
    bh, bl = b
    return mm(ah, bh, dims) + (mm(ah, bl, dims) + mm(al, bh, dims))

PANEL, GROUP = 32, 16


def factor(c_ref, xh, xl, ls, rs):
    nb, sub_nb = PANEL, GROUP
    n = c_ref.shape[0]
    tile = lax.broadcasted_iota(jnp.int32, (8, 128), 0)
    for p in range(n // nb):
        lo = p * nb
        need = [h for h in range(4) if (h < 2 and h * 128 + 128 > lo) or (h >= 2 and (h - 2) * 128 < lo + nb)]
        sub = lax.broadcasted_iota(jnp.int32, (nb, 128), 0)
        s = {}
        for h in need:
            if h < 2:
                s[h] = c_ref[lo:lo + nb, 128 * h:128 * h + 128]
            else:
                l = lax.broadcasted_iota(jnp.int32, (nb, 128), 1) + 128 * (h - 2)
                s[h] = jnp.where(l == sub + lo, 1.0, 0.0)
        a0, a1 = need[0] * 128, need[-1] * 128 + 128
        cuts = []
        if p > 1:
            cuts.append((0, 3 * (lo - nb)))
        if p > 0:
            cuts.append((3 * (lo - nb), 3 * lo))
        for (x, y) in cuts:
            d = mm(ls[x:y, lo:lo + nb], rs[x:y, a0:a1], TN)
            for h in need:
                s[h] = s[h] - d[:, 128 * h - a0:128 * h - a0 + 128]
        hd = lo // 128
        off = lo - hd * 128
        pivots = []
        done = []
        for g in range(nb // sub_nb):
            b = g * sub_nb
            cols = [jnp.broadcast_to(s[hd][:, off + b + k:off + b + k + 1], (nb - b, 128)) for k in range(sub_nb)]
            for j in range(sub_nb):
                jj = j % 8
                d = cols[j][jj:jj + 1, :]
                pivots.append(d)
                m = cols[j] * (1.0 / d)
                for k in range(j + 1, sub_nb):
                    cols[k] = cols[k] - m * cols[k][jj:jj + 1, :]
                low = jnp.where(tile > jj, m[0:8], 0.0)
                if m.shape[0] > 8:
                    low = jnp.concatenate([low, m[8:]], axis=0)
                for h in need:
                    s[h] = s[h] - low * s[h][jj:jj + 1, :]
                if jj == 7:
                    done.append({h: s[h][0:8] for h in need})
                    if m.shape[0] > 8:
                        s = {h: s[h][8:] for h in need}
                        cols = [t[8:] for t in cols]
        scale = lax.rsqrt(jnp.concatenate(pivots, axis=0))
        for h in range(4):
            if h not in need:
                o = jnp.zeros((nb, 128), F32)
            else:
                o = jnp.concatenate([t[h] for t in done], axis=0) * scale
                if h == hd:
                    l = lax.broadcasted_iota(jnp.int32, (nb, 128), 1) + 128 * h
                    o = jnp.where(l >= sub + lo, o, 0.0)
            cs = slice(128 * h, 128 * h + 128)
            hi = o.astype(BF)
            lw = (o - hi.astype(F32)).astype(BF)
            if h >= 2:
                xs = slice(128 * (h - 2), 128 * (h - 2) + 128)
                xh[lo:lo + nb, xs] = hi
                xl[lo:lo + nb, xs] = lw
            b = 3 * lo
            rs[b:b + nb, cs] = hi
            rs[b + nb:b + 2 * nb, cs] = lw
            rs[b + 2 * nb:b + 3 * nb, cs] = hi
            if h < 2:
                ls[b:b + nb, cs] = hi
                ls[b + nb:b + 2 * nb, cs] = hi
                ls[b + 2 * nb:b + 3 * nb, cs] = lw


MESH = pl.DeviceIdType.MESH
V = pltpu.VMEM


def greet(groups):
    barrier = pltpu.get_barrier_semaphore()
    total = 0
    for axis, size in groups:
        me = lax.axis_index(axis)

        @pl.loop(1, size)
        def _(d):
            pl.semaphore_signal(barrier, inc=1, device_id={axis: lax.rem(me + d, size)}, device_id_type=MESH)

        total += size - 1
    pl.semaphore_wait(barrier, total)


STEPS = (
    (2, 1), (1, 0), (0, 3), (1, 2), (3, 3), (3, 0), (2, 3), (0, 1), (1, 1), (3, 2), (1, 3), (2, 0), (3, 1), (0, 2), (2, 2),
)
SIDE = 4


def partners(me):
    z, y = lax.div(me, SIDE), lax.rem(me, SIDE)
    for k, (dy, dz) in enumerate(STEPS):
        to = lax.rem(z + dz, SIDE) * SIDE + lax.rem(y + dy, SIDE)
        source = lax.rem(z + SIDE - dz, SIDE) * SIDE + lax.rem(y + SIDE - dy, SIDE)
        yield k, to, source


def remote(src, dst, send, recv, axis, target):
    return pltpu.make_async_remote_copy(
        src_ref=src, dst_ref=dst, send_sem=send, recv_sem=recv, device_id={axis: target}, device_id_type=MESH
    )


def slot_at(table, owner, slots, home):
    found = 0
    for j in range(slots):
        found = jnp.where(lax.div(table[owner * slots + j], slots) == home, j, found)
    return found


def enter_body(shards, owners, table, g_ref, b_hbm, gh_out, gl_out, kh_out, kl_out, z_out, p_out,
               b_ref, gland, gh, gl, kacc, kh, kl, stage, landed, stage2, pland,
               g_send, g_recv, a_send, a_recv, b_send, b_recv, own_sem, in_sem, h_sem, l_sem, p_sem, k_sem):
    s_me = lax.axis_index("shard")
    o_me = lax.axis_index("owner")
    load = pltpu.make_async_copy(b_hbm, b_ref, in_sem)
    load.start()
    greet((("shard", shards), ("owner", owners)))
    slots = shards

    def at_shard(d):
        return lax.rem(s_me + d, shards)

    def from_shard(d):
        return lax.rem(s_me - d + shards, shards)

    own = pltpu.make_async_copy(g_ref.at[s_me], gland.at[s_me], own_sem)
    own.start()

    @pl.loop(1, shards)
    def _(d):
        t = at_shard(d)
        remote(g_ref.at[t], gland.at[s_me], g_send.at[d], g_recv.at[d], "shard", t).start()

    load.wait()
    for k, t, _ in partners(o_me):
        stage[t] = b_ref[slot_at(table, o_me, slots, t)]
        remote(stage.at[t], landed.at[o_me], a_send.at[k], a_recv.at[k], "owner", t).start()

    landed[o_me] = b_ref[slot_at(table, o_me, slots, o_me)]
    kacc[...] = jnp.zeros_like(kacc)
    own.wait()
    tiles = kacc.shape[0] // 256

    def gram(f):
        h, l = split(gland[f])
        gh[f] = h
        gl[f] = l
        pltpu.make_async_copy(gh.at[f], gh_out.at[f], h_sem.at[f]).start()
        pltpu.make_async_copy(gl.at[f], gl_out.at[f], l_sem.at[f]).start()
        for a in range(tiles):
            ra = slice(256 * a, 256 * a + 256)
            for b in range(a, tiles):
                rb = slice(256 * b, 256 * b + 256)
                kacc[ra, rb] += dot3((h[:, ra], l[:, ra]), (h[:, rb], l[:, rb]), TN)

    gram(s_me)

    def take_gram(d):
        f = from_shard(d)
        remote(g_ref.at[at_shard(d)], gland.at[f], g_send.at[d], g_recv.at[d], "shard", at_shard(d)).wait_recv()
        gram(f)

    half = EARLY
    pl.loop(1, half)(take_gram)

    for k, t, source in partners(o_me):
        remote(stage.at[t], landed.at[source], a_send.at[k], a_recv.at[k], "owner", t).wait()

    def holder(i):
        def add(o, found):
            for j in range(slots):
                found = jnp.where(table[o * slots + j] == o_me * slots + i, o, found)
            return found

        return lax.fori_loop(0, owners, add, 0)

    @pl.loop(1, shards)
    def _(d):
        t = at_shard(d)
        stage2[t] = landed[holder(t)]
        remote(stage2.at[t], pland.at[s_me], b_send.at[d], b_recv.at[d], "shard", t).start()

    pland[s_me] = landed[holder(s_me)]
    pl.loop(half, shards)(take_gram)

    for a in range(tiles):
        ra = slice(256 * a, 256 * a + 256)
        for b in range(a, tiles):
            rb = slice(256 * b, 256 * b + 256)
            h, l = split(kacc[ra, rb])
            kh[ra, rb] = h
            kl[ra, rb] = l
            if b > a:
                h, l = split(kacc[ra, rb].T)
                kh[rb, ra] = h
                kl[rb, ra] = l

    save_k = (pltpu.make_async_copy(kh, kh_out, k_sem.at[0]), pltpu.make_async_copy(kl, kl_out, k_sem.at[1]))
    for copy in save_k:
        copy.start()

    def project(f):
        pltpu.make_async_copy(pland.at[f], p_out.at[f], p_sem.at[f]).start()
        return dot3(split(pland[f]), (gh[f], gl[f]), TN)

    z_out[...] = project(s_me)

    @pl.loop(1, shards)
    def _(d):
        f = from_shard(d)
        remote(stage2.at[at_shard(d)], pland.at[f], b_send.at[d], b_recv.at[d], "shard", at_shard(d)).wait()
        z_out[...] += project(f)

    @pl.loop(1, shards)
    def _(d):
        remote(g_ref.at[at_shard(d)], gland.at[from_shard(d)], g_send.at[d], g_recv.at[d], "shard", at_shard(d)).wait_send()

    @pl.loop(0, shards)
    def _(f):
        pltpu.make_async_copy(gh.at[f], gh_out.at[f], h_sem.at[f]).wait()
        pltpu.make_async_copy(gl.at[f], gl_out.at[f], l_sem.at[f]).wait()
        pltpu.make_async_copy(pland.at[f], p_out.at[f], p_sem.at[f]).wait()

    for copy in save_k:
        copy.wait()


EARLY = 5


def enter(table, gradient, basis):
    shards, rows, cols = gradient.shape
    rank = basis.shape[2]
    owners = table.shape[0] // basis.shape[0]
    sem = pltpu.SemaphoreType.DMA
    smem = pl.BlockSpec(memory_space=pltpu.SMEM)
    vmem = pl.BlockSpec(memory_space=V)
    hbm = pl.BlockSpec(memory_space=pl.ANY)
    return pl.pallas_call(
        functools.partial(enter_body, shards, owners),
        out_shape=(
            jax.ShapeDtypeStruct((shards, rows, cols), BF),
            jax.ShapeDtypeStruct((shards, rows, cols), BF),
            jax.ShapeDtypeStruct((cols, cols), BF),
            jax.ShapeDtypeStruct((cols, cols), BF),
            jax.ShapeDtypeStruct((rank, cols), F32),
            jax.ShapeDtypeStruct((shards, rows, rank), F32),
        ),
        in_specs=[smem, hbm, hbm],
        out_specs=(hbm, hbm, hbm, hbm, vmem, hbm),
        scratch_shapes=[
            V((shards, rows, rank), F32), V((shards, rows, cols), F32), V((shards, rows, cols), BF), V((shards, rows, cols), BF), V((cols, cols), F32), V((cols, cols), BF), V((cols, cols), BF),
            V((owners, rows, rank), F32), V((owners, rows, rank), F32), V((shards, rows, rank), F32), V((shards, rows, rank), F32),
            sem((shards,)), sem((shards,)), sem((owners,)), sem((owners,)), sem((shards,)), sem((shards,)),
            sem, sem, sem((shards,)), sem((shards,)), sem((shards,)), sem((2,)),
        ],
        compiler_params=pltpu.CompilerParams(
            collective_id=0, has_side_effects=True, vmem_limit_bytes=56 * 1024 * 1024
        ),
        name="enter",
    )(table, gradient, basis)


def body(table, cost, kh_ref, kl_ref, zin_ref, mh_ref, ml_ref, pj_ref, keep_ref, home_ref, z_ref, w_ref, c_ref, xh, xl, ls, rs):
    s_me = lax.axis_index("shard")
    o_me = lax.axis_index("owner")
    shards, part, cols = pj_ref.shape
    count = cost[o_me * shards + s_me]
    keep_ref[0] = jnp.where(count > 0, 0.0, 1.0)
    for j in range(shards):
        home_ref[j] = lax.div(table[o_me * shards + j], shards)
    z_ref[...] = zin_ref[...]

    @pl.loop(0, count)
    def _(it):
        z = split(z_ref[...])
        w_ref[...] = dot3(z, (kh_ref[...], kl_ref[...]), NN)
        w = split(w_ref[...])
        c_ref[...] = dot3(z, w, NT)
        factor(c_ref, xh, xl, ls, rs)
        x = (xh[...], xl[...])
        z_ref[...] = dot3(x, w, NN)

        @pl.when(it == count - 1)
        def _():
            h, l = split(dot3(x, z, NN))
            mh_ref[...] = h
            ml_ref[...] = l

    @pl.when(count == 0)
    def _():
        mh_ref[...] = jnp.zeros_like(mh_ref)
        ml_ref[...] = jnp.zeros_like(ml_ref)

    for s in range(shards):
        pj_ref[s] = z_ref[part * s:part * s + part, :]


def refresh(table, cost, shards, kh, kl, z):
    rank, cols = z.shape
    smem = pl.BlockSpec(memory_space=pltpu.SMEM)
    vmem = pl.BlockSpec(memory_space=V)
    return pl.pallas_call(
        body,
        out_shape=(
            jax.ShapeDtypeStruct((rank, cols), BF),
            jax.ShapeDtypeStruct((rank, cols), BF),
            jax.ShapeDtypeStruct((shards, rank // shards, cols), F32),
            jax.ShapeDtypeStruct((1,), F32),
            jax.ShapeDtypeStruct((shards,), jnp.int32),
        ),
        in_specs=[smem, smem, vmem, vmem, vmem],
        out_specs=(vmem, vmem, vmem, smem, smem),
        scratch_shapes=[
            V((rank, cols), F32), V((rank, cols), F32), V((rank, rank), F32), V((rank, rank), BF), V((rank, rank), BF),
            V((3 * rank, rank), BF), V((3 * rank, 2 * rank), BF),
        ],
        compiler_params=pltpu.CompilerParams(vmem_limit_bytes=56 * 1024 * 1024),
        name="refresh",
    )(table, cost, kh, kl, z)


BETA_ONE = 0.9
BETA_TWO = 0.99
EPSILON = 1e-08
GALORE_SCALE = 0.25
CHUNKS = 2


def adam(one, two, projected):
    one = BETA_ONE * one + (1.0 - BETA_ONE) * projected
    two = BETA_TWO * two + (1.0 - BETA_TWO) * projected * projected
    return one, two


def leave_body(shards, owners, table, keep_ref, mh_ref, ml_ref, pj_ref, gh_hbm, gl_hbm, p_hbm, one_hbm, two_hbm,
               back_a, back_b, normed_out, proj_out,
               one_ref, two_ref, gh, gl, p_in, pn, pj1a, pj1b, pj_stage, pj2, pn1a, pn1b, pn_stage, normed,
               h_sem, l_sem, i_sem, j_send, j_recv, jo_send, jo_recv, p_send, p_recv, po_send, po_recv,
               n_send, n_recv, f_send, f_recv, own_sem, m_sem):
    s_me = lax.axis_index("shard")
    o_me = lax.axis_index("owner")
    slots = one_ref.shape[0]
    pn1, back, pj1 = (pn1a, pn1b), (back_a, back_b), (pj1a, pj1b)
    half = pj1a.shape[1]
    chunk = pn1a.shape[1]

    def at_shard(d):
        return lax.rem(s_me + d, shards)

    def from_shard(d):
        return lax.rem(s_me - d + shards, shards)

    def rows(c):
        return slice(c * chunk, (c + 1) * chunk)

    def loads(t):
        return (
            pltpu.make_async_copy(gh_hbm.at[t], gh.at[t], h_sem.at[t]),
            pltpu.make_async_copy(gl_hbm.at[t], gl.at[t], l_sem.at[t]),
            pltpu.make_async_copy(p_hbm.at[t], p_in.at[t], i_sem.at[t]),
        )

    @pl.loop(1, shards + 1)
    def _(d):
        for copy in loads(at_shard(d)):
            copy.start()

    moments = (pltpu.make_async_copy(one_hbm, one_ref, m_sem.at[0]), pltpu.make_async_copy(two_hbm, two_ref, m_sem.at[1]))
    for copy in moments:
        copy.start()
    greet((("shard", shards), ("owner", owners)))

    def part(q):
        return slice(q * half, (q + 1) * half)

    for q in range(2):

        @pl.loop(1, shards)
        def _(d):
            t = at_shard(d)
            remote(pj_ref.at[t, part(q)], pj1[q].at[s_me], j_send.at[q, d], j_recv.at[q, d], "shard", t).start()

        pltpu.make_async_copy(pj_ref.at[s_me, part(q)], pj1[q].at[s_me], m_sem.at[2 + q]).start()

    keep = keep_ref[0]

    def basis_rows(t, c):
        return dot3((gh[t, rows(c)], gl[t, rows(c)]), (mh_ref[...], ml_ref[...]), NT) + keep * p_in[t, rows(c)]

    def send_basis(c):
        @pl.loop(1, shards)
        def _(d):
            t = at_shard(d)
            if c == 0:
                for copy in loads(t):
                    copy.wait()
            pn[c, t] = basis_rows(t, c)
            remote(pn.at[c, t], pn1[c].at[s_me], p_send.at[c, d], p_recv.at[c, d], "shard", t).start()

        if c == 0:
            for copy in loads(s_me):
                copy.wait()
        pn1[c][s_me] = basis_rows(s_me, c)

    def expert_at(owner):
        found = 0
        for j in range(slots):
            e = table[owner * slots + j]
            found = jnp.where(lax.div(e, slots) == o_me, lax.rem(e, slots), found)
        return found

    for q in range(2):

        @pl.loop(1, shards)
        def _(d):
            t = at_shard(d)
            remote(pj_ref.at[t, part(q)], pj1[q].at[from_shard(d)], j_send.at[q, d], j_recv.at[q, d], "shard", t).wait()

        pltpu.make_async_copy(pj_ref.at[s_me, part(q)], pj1[q].at[s_me], m_sem.at[2 + q]).wait()
        for k, t, _ in partners(o_me):
            pj_stage[q, t] = pj1[q][expert_at(t)]
            remote(pj_stage.at[q, t], pj2.at[q, o_me], jo_send.at[q, k], jo_recv.at[q, k], "owner", t).start()

        pj2[q, o_me] = pj1[q][expert_at(o_me)]

    for c in range(0, CHUNKS):
        send_basis(c)

    own = []

    def pass_basis(c):

        @pl.loop(1, shards)
        def _(d):
            t = at_shard(d)
            remote(pn.at[c, t], pn1[c].at[from_shard(d)], p_send.at[c, d], p_recv.at[c, d], "shard", t).wait()

        for k, t, _ in partners(o_me):
            pn_stage[c, t] = pn1[c][expert_at(t)]
            remote(pn_stage.at[c, t], back[c].at[o_me], po_send.at[c, k], po_recv.at[c, k], "owner", t).start()

        pn_stage[c, o_me] = pn1[c][expert_at(o_me)]
        own.append(pltpu.make_async_copy(pn_stage.at[c, o_me], back[c].at[o_me], own_sem.at[c]))
        own[-1].start()

    for c in range(CHUNKS):
        pass_basis(c)

    for q in range(2):
        for k, t, source in partners(o_me):
            remote(pj_stage.at[q, t], pj2.at[q, source], jo_send.at[q, k], jo_recv.at[q, k], "owner", t).wait()

    for copy in moments:
        copy.wait()

    @pl.loop(0, slots)
    def _(j):
        home = lax.div(table[o_me * slots + j], slots)
        projected = jnp.concatenate([pj2[0, home], pj2[1, home]], axis=0)
        proj_out[j] = projected
        one, two = adam(one_ref[j], two_ref[j], projected)
        normed[j] = one / (jnp.sqrt(two) + EPSILON)

    other = s_me + 1 - 2 * lax.rem(s_me, 2)
    chips = shards // 2

    @pl.loop(1, chips)
    def _(k):
        t = at_shard(2 * k)
        remote(normed, normed_out.at[s_me], n_send.at[k], n_recv.at[k], "shard", t).start()

    remote(normed, normed_out.at[s_me], f_send.at[0], f_recv.at[0], "shard", other).start()
    own.append(pltpu.make_async_copy(normed, normed_out.at[s_me], own_sem.at[CHUNKS]))
    own[-1].start()

    @pl.loop(1, chips)
    def _(k):
        f = from_shard(2 * k)
        remote(normed, normed_out.at[f], n_send.at[k], n_recv.at[k], "shard", at_shard(2 * k)).wait()
        remote(normed_out.at[f], normed_out.at[f], f_send.at[k], f_recv.at[k], "shard", other).start()

    @pl.loop(0, chips)
    def _(k):
        g = lax.rem(other - 2 * k + shards, shards)
        remote(normed, normed_out.at[g], f_send.at[k], f_recv.at[k], "shard", other).wait()

    for copy in own:
        copy.wait()

    for c in range(CHUNKS):

        for k, t, source in partners(o_me):
            remote(pn_stage.at[c, t], back[c].at[source], po_send.at[c, k], po_recv.at[c, k], "owner", t).wait()


def leave(table, keep, mh, ml, pj, gh, gl, p, one, two):
    shards, rows, cols = gh.shape
    rank = p.shape[2]
    part = pj.shape[1]
    slots = one.shape[0]
    owners = table.shape[0] // slots
    chunk = rows // CHUNKS
    dma = pltpu.SemaphoreType.DMA
    smem = pl.BlockSpec(memory_space=pltpu.SMEM)
    vmem = pl.BlockSpec(memory_space=V)
    hbm = pl.BlockSpec(memory_space=pl.ANY)
    return pl.pallas_call(
        functools.partial(leave_body, shards, owners),
        out_shape=(
            jax.ShapeDtypeStruct((owners, chunk, rank), F32),
            jax.ShapeDtypeStruct((owners, chunk, rank), F32),
            jax.ShapeDtypeStruct((shards, slots, part, cols), F32),
            jax.ShapeDtypeStruct((slots, part, cols), F32),
        ),
        in_specs=[smem, smem, vmem, vmem] + [hbm] * 6,
        out_specs=(hbm, hbm, hbm, vmem),
        scratch_shapes=[
            V(one.shape, F32), V(two.shape, F32), V(gh.shape, BF), V(gh.shape, BF), V(p.shape, F32), V((CHUNKS, shards, chunk, rank), F32),
            V((shards, part // 2, cols), F32), V((shards, part // 2, cols), F32),
            V((2, owners, part // 2, cols), F32), V((2, owners, part // 2, cols), F32),
            V((shards, chunk, rank), F32), V((shards, chunk, rank), F32), V((CHUNKS, owners, chunk, rank), F32),
            V((slots, part, cols), F32),
            dma((shards,)), dma((shards,)), dma((shards,)),
            dma((2, shards)), dma((2, shards)), dma((2, owners)), dma((2, owners)),
            dma((CHUNKS, shards)), dma((CHUNKS, shards)), dma((CHUNKS, owners)), dma((CHUNKS, owners)),
            dma((shards // 2,)), dma((shards // 2,)), dma((shards // 2,)), dma((shards // 2,)), dma((CHUNKS + 1,)), dma((4,)),
        ],
        compiler_params=pltpu.CompilerParams(
            collective_id=1, has_side_effects=True, vmem_limit_bytes=56 * 1024 * 1024
        ),
        name="leave",
    )(table, keep, mh, ml, pj, gh, gl, p, one, two)


def finish_body(home_ref, back_a, back_b, normed_ref, proj_ref, one_ref, two_ref, basis_out, one_out, two_out, update_out,
                basis, normed, proj, one, two, update, b_sem, n_sem, m_sem, bo_sem, u_sem, mo_sem):
    slots, rows, _ = basis.shape
    chunk = rows // 2
    shards, part, cols = normed.shape[1:]

    def halves(j):
        return [
            pltpu.make_async_copy(ref.at[home_ref[j]], basis.at[j, c * chunk:(c + 1) * chunk], b_sem.at[c, j])
            for c, ref in enumerate((back_a, back_b))
        ]

    def step(j):
        return pltpu.make_async_copy(normed_ref.at[:, j], normed.at[j], n_sem.at[j])

    def basis_save(j):
        return pltpu.make_async_copy(basis.at[j], basis_out.at[j], bo_sem.at[j])

    def update_save(j):
        return pltpu.make_async_copy(update.at[j], update_out.at[j], u_sem.at[j])

    moments = [
        pltpu.make_async_copy(src, dst, m_sem.at[k])
        for k, (src, dst) in enumerate(((proj_ref, proj), (one_ref, one), (two_ref, two)))
    ]

    @pl.loop(0, slots)
    def _(j):
        for copy in halves(j):
            copy.start()
        step(j).start()

    for copy in moments:
        copy.start()

    @pl.loop(0, slots)
    def _(j):
        for copy in halves(j):
            copy.wait()
        basis_save(j).start()
        step(j).wait()
        product = dot3(split(basis[j]), split(normed[j].reshape(shards * part, cols)), NN)
        update[j] = (GALORE_SCALE * product).astype(BF)
        update_save(j).start()

    for copy in moments:
        copy.wait()
    one[...], two[...] = adam(one[...], two[...], proj[...])
    saves = [
        pltpu.make_async_copy(src, dst, mo_sem.at[k]) for k, (src, dst) in enumerate(((one, one_out), (two, two_out)))
    ]
    for copy in saves:
        copy.start()

    @pl.loop(0, slots)
    def _(j):
        basis_save(j).wait()
        update_save(j).wait()

    for copy in saves:
        copy.wait()


def finish(home, back_a, back_b, normed, projected, one, two):
    shards, slots, part, cols = normed.shape
    _, chunk, rank = back_a.shape
    dma = pltpu.SemaphoreType.DMA
    hbm = pl.BlockSpec(memory_space=pl.ANY)
    return pl.pallas_call(
        finish_body,
        out_shape=(
            jax.ShapeDtypeStruct((slots, 2 * chunk, rank), F32),
            jax.ShapeDtypeStruct(one.shape, F32),
            jax.ShapeDtypeStruct(two.shape, F32),
            jax.ShapeDtypeStruct((slots, 2 * chunk, cols), BF),
        ),
        in_specs=[pl.BlockSpec(memory_space=pltpu.SMEM)] + [hbm] * 6,
        out_specs=(hbm,) * 4,
        scratch_shapes=[
            V((slots, 2 * chunk, rank), F32), V((slots, shards, part, cols), F32),
            V(one.shape, F32), V(one.shape, F32), V(one.shape, F32), V((slots, 2 * chunk, cols), BF),
            dma((2, slots)), dma((slots,)), dma((3,)), dma((slots,)), dma((slots,)), dma((2,)),
        ],
        compiler_params=pltpu.CompilerParams(vmem_limit_bytes=60 * 1024 * 1024),
        name="finish",
    )(home, back_a, back_b, normed, projected, one, two)


def on_device(gradient, old_basis, moment_one, moment_two, slot_expert, cost):
    gh, gl, kh, kl, z, p = enter(slot_expert, gradient, old_basis)
    mh, ml, pj, keep, home = refresh(slot_expert, cost, gradient.shape[0], kh, kl, z)
    back_a, back_b, normed, projected = leave(slot_expert, keep, mh, ml, pj, gh, gl, p, moment_one, moment_two)
    return tuple(finish(home, back_a, back_b, normed, projected, moment_one, moment_two))


def solution(mesh):
    spec = P("owner", "shard", None)
    return jax.shard_map(
        on_device, mesh=mesh, in_specs=(spec,) * 4 + (P(), P()), out_specs=(spec,) * 4, check_vma=False
    )
```

```python
import functools
import jax, jax.numpy as jnp
from jax import lax
from jax.experimental import pallas as pl
from jax.sharding import PartitionSpec as P
from jax.experimental.pallas import tpu as pltpu

BF = jnp.bfloat16
F32 = jnp.float32

def split(x):
    hi = x.astype(BF)
    return hi, (x - hi.astype(F32)).astype(BF)

def mm(a, b, dims):
    return lax.dot_general(a, b, (dims, ((), ())), preferred_element_type=F32)

NN = ((1,), (0,))
TN = ((0,), (0,))
NT = ((1,), (1,))

def dot3(a, b, dims):
    ah, al = a
    bh, bl = b
    return mm(ah, bh, dims) + (mm(ah, bl, dims) + mm(al, bh, dims))

PANEL, GROUP = 32, 16


def factor(c_ref, xh, xl, ls, rs):
    nb, sub_nb = PANEL, GROUP
    n = c_ref.shape[0]
    tile = lax.broadcasted_iota(jnp.int32, (8, 128), 0)
    for p in range(n // nb):
        lo = p * nb
        need = [h for h in range(4) if (h < 2 and h * 128 + 128 > lo) or (h >= 2 and (h - 2) * 128 < lo + nb)]
        sub = lax.broadcasted_iota(jnp.int32, (nb, 128), 0)
        s = {}
        for h in need:
            if h < 2:
                s[h] = c_ref[lo:lo + nb, 128 * h:128 * h + 128]
            else:
                l = lax.broadcasted_iota(jnp.int32, (nb, 128), 1) + 128 * (h - 2)
                s[h] = jnp.where(l == sub + lo, 1.0, 0.0)
        a0, a1 = need[0] * 128, need[-1] * 128 + 128
        cuts = []
        if p > 1:
            cuts.append((0, 3 * (lo - nb)))
        if p > 0:
            cuts.append((3 * (lo - nb), 3 * lo))
        for (x, y) in cuts:
            d = mm(ls[x:y, lo:lo + nb], rs[x:y, a0:a1], TN)
            for h in need:
                s[h] = s[h] - d[:, 128 * h - a0:128 * h - a0 + 128]
        hd = lo // 128
        off = lo - hd * 128
        pivots = []
        done = []
        for g in range(nb // sub_nb):
            b = g * sub_nb
            cols = [jnp.broadcast_to(s[hd][:, off + b + k:off + b + k + 1], (nb - b, 128)) for k in range(sub_nb)]
            for j in range(sub_nb):
                jj = j % 8
                d = cols[j][jj:jj + 1, :]
                pivots.append(d)
                m = cols[j] * (1.0 / d)
                for k in range(j + 1, sub_nb):
                    cols[k] = cols[k] - m * cols[k][jj:jj + 1, :]
                low = jnp.where(tile > jj, m[0:8], 0.0)
                if m.shape[0] > 8:
                    low = jnp.concatenate([low, m[8:]], axis=0)
                for h in need:
                    s[h] = s[h] - low * s[h][jj:jj + 1, :]
                if jj == 7:
                    done.append({h: s[h][0:8] for h in need})
                    if m.shape[0] > 8:
                        s = {h: s[h][8:] for h in need}
                        cols = [t[8:] for t in cols]
        scale = lax.rsqrt(jnp.concatenate(pivots, axis=0))
        for h in range(4):
            if h not in need:
                o = jnp.zeros((nb, 128), F32)
            else:
                o = jnp.concatenate([t[h] for t in done], axis=0) * scale
                if h == hd:
                    l = lax.broadcasted_iota(jnp.int32, (nb, 128), 1) + 128 * h
                    o = jnp.where(l >= sub + lo, o, 0.0)
            cs = slice(128 * h, 128 * h + 128)
            hi = o.astype(BF)
            lw = (o - hi.astype(F32)).astype(BF)
            if h >= 2:
                xs = slice(128 * (h - 2), 128 * (h - 2) + 128)
                xh[lo:lo + nb, xs] = hi
                xl[lo:lo + nb, xs] = lw
            b = 3 * lo
            rs[b:b + nb, cs] = hi
            rs[b + nb:b + 2 * nb, cs] = lw
            rs[b + 2 * nb:b + 3 * nb, cs] = hi
            if h < 2:
                ls[b:b + nb, cs] = hi
                ls[b + nb:b + 2 * nb, cs] = hi
                ls[b + 2 * nb:b + 3 * nb, cs] = lw


MESH = pl.DeviceIdType.MESH
V = pltpu.VMEM


def greet(groups):
    barrier = pltpu.get_barrier_semaphore()
    total = 0
    for axis, size in groups:
        me = lax.axis_index(axis)

        @pl.loop(1, size)
        def _(d):
            pl.semaphore_signal(barrier, inc=1, device_id={axis: lax.rem(me + d, size)}, device_id_type=MESH)

        total += size - 1
    pl.semaphore_wait(barrier, total)


STEPS = (
    (2, 1), (1, 0), (0, 3), (1, 2), (3, 3), (3, 0), (2, 3), (0, 1), (1, 1), (3, 2), (1, 3), (2, 0), (3, 1), (0, 2), (2, 2),
)
SIDE = 4


def partners(me):
    z, y = lax.div(me, SIDE), lax.rem(me, SIDE)
    for k, (dy, dz) in enumerate(STEPS):
        to = lax.rem(z + dz, SIDE) * SIDE + lax.rem(y + dy, SIDE)
        source = lax.rem(z + SIDE - dz, SIDE) * SIDE + lax.rem(y + SIDE - dy, SIDE)
        yield k, to, source


def remote(src, dst, send, recv, axis, target):
    return pltpu.make_async_remote_copy(
        src_ref=src, dst_ref=dst, send_sem=send, recv_sem=recv, device_id={axis: target}, device_id_type=MESH
    )


def slot_at(table, owner, slots, home):
    found = 0
    for j in range(slots):
        found = jnp.where(lax.div(table[owner * slots + j], slots) == home, j, found)
    return found


def enter_body(shards, owners, table, g_ref, b_hbm, gh_out, gl_out, kh_out, kl_out, z_out, p_out,
               b_ref, gland, gh, gl, kacc, kh, kl, stage, landed, stage2, pland,
               g_send, g_recv, a_send, a_recv, b_send, b_recv, own_sem, in_sem, h_sem, l_sem, p_sem, k_sem):
    s_me = lax.axis_index("shard")
    o_me = lax.axis_index("owner")
    load = pltpu.make_async_copy(b_hbm, b_ref, in_sem)
    load.start()
    greet((("shard", shards), ("owner", owners)))
    slots = shards

    def at_shard(d):
        return lax.rem(s_me + d, shards)

    def from_shard(d):
        return lax.rem(s_me - d + shards, shards)

    own = pltpu.make_async_copy(g_ref.at[s_me], gland.at[s_me], own_sem)
    own.start()

    @pl.loop(1, shards)
    def _(d):
        t = at_shard(d)
        remote(g_ref.at[t], gland.at[s_me], g_send.at[d], g_recv.at[d], "shard", t).start()

    load.wait()
    for k, t, _ in partners(o_me):
        stage[t] = b_ref[slot_at(table, o_me, slots, t)]
        remote(stage.at[t], landed.at[o_me], a_send.at[k], a_recv.at[k], "owner", t).start()

    landed[o_me] = b_ref[slot_at(table, o_me, slots, o_me)]
    kacc[...] = jnp.zeros_like(kacc)
    own.wait()
    tiles = kacc.shape[0] // 256

    def gram(f):
        h, l = split(gland[f])
        gh[f] = h
        gl[f] = l
        pltpu.make_async_copy(gh.at[f], gh_out.at[f], h_sem.at[f]).start()
        pltpu.make_async_copy(gl.at[f], gl_out.at[f], l_sem.at[f]).start()
        for a in range(tiles):
            ra = slice(256 * a, 256 * a + 256)
            for b in range(a, tiles):
                rb = slice(256 * b, 256 * b + 256)
                kacc[ra, rb] += dot3((h[:, ra], l[:, ra]), (h[:, rb], l[:, rb]), TN)

    gram(s_me)

    def take_gram(d):
        f = from_shard(d)
        remote(g_ref.at[at_shard(d)], gland.at[f], g_send.at[d], g_recv.at[d], "shard", at_shard(d)).wait_recv()
        gram(f)

    half = EARLY
    pl.loop(1, half)(take_gram)

    for k, t, source in partners(o_me):
        remote(stage.at[t], landed.at[source], a_send.at[k], a_recv.at[k], "owner", t).wait()

    def holder(i):
        def add(o, found):
            for j in range(slots):
                found = jnp.where(table[o * slots + j] == o_me * slots + i, o, found)
            return found

        return lax.fori_loop(0, owners, add, 0)

    @pl.loop(1, shards)
    def _(d):
        t = at_shard(d)
        stage2[t] = landed[holder(t)]
        remote(stage2.at[t], pland.at[s_me], b_send.at[d], b_recv.at[d], "shard", t).start()

    pland[s_me] = landed[holder(s_me)]
    pl.loop(half, shards)(take_gram)

    for a in range(tiles):
        ra = slice(256 * a, 256 * a + 256)
        for b in range(a, tiles):
            rb = slice(256 * b, 256 * b + 256)
            h, l = split(kacc[ra, rb])
            kh[ra, rb] = h
            kl[ra, rb] = l
            if b > a:
                h, l = split(kacc[ra, rb].T)
                kh[rb, ra] = h
                kl[rb, ra] = l

    save_k = (pltpu.make_async_copy(kh, kh_out, k_sem.at[0]), pltpu.make_async_copy(kl, kl_out, k_sem.at[1]))
    for copy in save_k:
        copy.start()

    def project(f):
        pltpu.make_async_copy(pland.at[f], p_out.at[f], p_sem.at[f]).start()
        return dot3(split(pland[f]), (gh[f], gl[f]), TN)

    z_out[...] = project(s_me)

    @pl.loop(1, shards)
    def _(d):
        f = from_shard(d)
        remote(stage2.at[at_shard(d)], pland.at[f], b_send.at[d], b_recv.at[d], "shard", at_shard(d)).wait()
        z_out[...] += project(f)

    @pl.loop(1, shards)
    def _(d):
        remote(g_ref.at[at_shard(d)], gland.at[from_shard(d)], g_send.at[d], g_recv.at[d], "shard", at_shard(d)).wait_send()

    @pl.loop(0, shards)
    def _(f):
        pltpu.make_async_copy(gh.at[f], gh_out.at[f], h_sem.at[f]).wait()
        pltpu.make_async_copy(gl.at[f], gl_out.at[f], l_sem.at[f]).wait()
        pltpu.make_async_copy(pland.at[f], p_out.at[f], p_sem.at[f]).wait()

    for copy in save_k:
        copy.wait()


EARLY = 2


def enter(table, gradient, basis):
    shards, rows, cols = gradient.shape
    rank = basis.shape[2]
    owners = table.shape[0] // basis.shape[0]
    sem = pltpu.SemaphoreType.DMA
    smem = pl.BlockSpec(memory_space=pltpu.SMEM)
    vmem = pl.BlockSpec(memory_space=V)
    hbm = pl.BlockSpec(memory_space=pl.ANY)
    return pl.pallas_call(
        functools.partial(enter_body, shards, owners),
        out_shape=(
            jax.ShapeDtypeStruct((shards, rows, cols), BF),
            jax.ShapeDtypeStruct((shards, rows, cols), BF),
            jax.ShapeDtypeStruct((cols, cols), BF),
            jax.ShapeDtypeStruct((cols, cols), BF),
            jax.ShapeDtypeStruct((rank, cols), F32),
            jax.ShapeDtypeStruct((shards, rows, rank), F32),
        ),
        in_specs=[smem, hbm, hbm],
        out_specs=(hbm, hbm, hbm, hbm, vmem, hbm),
        scratch_shapes=[
            V((shards, rows, rank), F32), V((shards, rows, cols), F32), V((shards, rows, cols), BF), V((shards, rows, cols), BF), V((cols, cols), F32), V((cols, cols), BF), V((cols, cols), BF),
            V((owners, rows, rank), F32), V((owners, rows, rank), F32), V((shards, rows, rank), F32), V((shards, rows, rank), F32),
            sem((shards,)), sem((shards,)), sem((owners,)), sem((owners,)), sem((shards,)), sem((shards,)),
            sem, sem, sem((shards,)), sem((shards,)), sem((shards,)), sem((2,)),
        ],
        compiler_params=pltpu.CompilerParams(
            collective_id=0, has_side_effects=True, vmem_limit_bytes=56 * 1024 * 1024
        ),
        name="enter",
    )(table, gradient, basis)


def body(table, cost, kh_ref, kl_ref, zin_ref, mh_ref, ml_ref, pj_ref, keep_ref, home_ref, z_ref, w_ref, c_ref, xh, xl, ls, rs):
    s_me = lax.axis_index("shard")
    o_me = lax.axis_index("owner")
    shards, part, cols = pj_ref.shape
    count = cost[o_me * shards + s_me]
    keep_ref[0] = jnp.where(count > 0, 0.0, 1.0)
    for j in range(shards):
        home_ref[j] = lax.div(table[o_me * shards + j], shards)
    z_ref[...] = zin_ref[...]

    @pl.loop(0, count)
    def _(it):
        z = split(z_ref[...])
        w_ref[...] = dot3(z, (kh_ref[...], kl_ref[...]), NN)
        w = split(w_ref[...])
        c_ref[...] = dot3(z, w, NT)
        factor(c_ref, xh, xl, ls, rs)
        x = (xh[...], xl[...])
        z_ref[...] = dot3(x, w, NN)

        @pl.when(it == count - 1)
        def _():
            h, l = split(dot3(x, z, NN))
            mh_ref[...] = h
            ml_ref[...] = l

    @pl.when(count == 0)
    def _():
        mh_ref[...] = jnp.zeros_like(mh_ref)
        ml_ref[...] = jnp.zeros_like(ml_ref)

    for s in range(shards):
        pj_ref[s] = z_ref[part * s:part * s + part, :]


def refresh(table, cost, shards, kh, kl, z):
    rank, cols = z.shape
    smem = pl.BlockSpec(memory_space=pltpu.SMEM)
    vmem = pl.BlockSpec(memory_space=V)
    return pl.pallas_call(
        body,
        out_shape=(
            jax.ShapeDtypeStruct((rank, cols), BF),
            jax.ShapeDtypeStruct((rank, cols), BF),
            jax.ShapeDtypeStruct((shards, rank // shards, cols), F32),
            jax.ShapeDtypeStruct((1,), F32),
            jax.ShapeDtypeStruct((shards,), jnp.int32),
        ),
        in_specs=[smem, smem, vmem, vmem, vmem],
        out_specs=(vmem, vmem, vmem, smem, smem),
        scratch_shapes=[
            V((rank, cols), F32), V((rank, cols), F32), V((rank, rank), F32), V((rank, rank), BF), V((rank, rank), BF),
            V((3 * rank, rank), BF), V((3 * rank, 2 * rank), BF),
        ],
        compiler_params=pltpu.CompilerParams(vmem_limit_bytes=56 * 1024 * 1024),
        name="refresh",
    )(table, cost, kh, kl, z)


BETA_ONE = 0.9
BETA_TWO = 0.99
EPSILON = 1e-08
GALORE_SCALE = 0.25
CHUNKS = 2


def adam(one, two, projected):
    one = BETA_ONE * one + (1.0 - BETA_ONE) * projected
    two = BETA_TWO * two + (1.0 - BETA_TWO) * projected * projected
    return one, two


def leave_body(shards, owners, table, keep_ref, mh_ref, ml_ref, pj_ref, gh_hbm, gl_hbm, p_hbm, one_hbm, two_hbm,
               back_a, back_b, normed_out, proj_out,
               one_ref, two_ref, gh, gl, p_in, pn, pj1a, pj1b, pj_stage, pj2, pn1a, pn1b, pn_stage, normed,
               h_sem, l_sem, i_sem, j_send, j_recv, jo_send, jo_recv, p_send, p_recv, po_send, po_recv,
               n_send, n_recv, f_send, f_recv, own_sem, m_sem):
    s_me = lax.axis_index("shard")
    o_me = lax.axis_index("owner")
    slots = one_ref.shape[0]
    pn1, back, pj1 = (pn1a, pn1b), (back_a, back_b), (pj1a, pj1b)
    half = pj1a.shape[1]
    chunk = pn1a.shape[1]

    def at_shard(d):
        return lax.rem(s_me + d, shards)

    def from_shard(d):
        return lax.rem(s_me - d + shards, shards)

    def rows(c):
        return slice(c * chunk, (c + 1) * chunk)

    def loads(t):
        return (
            pltpu.make_async_copy(gh_hbm.at[t], gh.at[t], h_sem.at[t]),
            pltpu.make_async_copy(gl_hbm.at[t], gl.at[t], l_sem.at[t]),
            pltpu.make_async_copy(p_hbm.at[t], p_in.at[t], i_sem.at[t]),
        )

    @pl.loop(1, shards + 1)
    def _(d):
        for copy in loads(at_shard(d)):
            copy.start()

    moments = (pltpu.make_async_copy(one_hbm, one_ref, m_sem.at[0]), pltpu.make_async_copy(two_hbm, two_ref, m_sem.at[1]))
    for copy in moments:
        copy.start()
    greet((("shard", shards), ("owner", owners)))

    def part(q):
        return slice(q * half, (q + 1) * half)

    for q in range(2):

        @pl.loop(1, shards)
        def _(d):
            t = at_shard(d)
            remote(pj_ref.at[t, part(q)], pj1[q].at[s_me], j_send.at[q, d], j_recv.at[q, d], "shard", t).start()

        pltpu.make_async_copy(pj_ref.at[s_me, part(q)], pj1[q].at[s_me], m_sem.at[2 + q]).start()

    keep = keep_ref[0]

    def basis_rows(t, c):
        return dot3((gh[t, rows(c)], gl[t, rows(c)]), (mh_ref[...], ml_ref[...]), NT) + keep * p_in[t, rows(c)]

    def send_basis(c):
        @pl.loop(1, shards)
        def _(d):
            t = at_shard(d)
            if c == 0:
                for copy in loads(t):
                    copy.wait()
            pn[c, t] = basis_rows(t, c)
            remote(pn.at[c, t], pn1[c].at[s_me], p_send.at[c, d], p_recv.at[c, d], "shard", t).start()

        if c == 0:
            for copy in loads(s_me):
                copy.wait()
        pn1[c][s_me] = basis_rows(s_me, c)

    def expert_at(owner):
        found = 0
        for j in range(slots):
            e = table[owner * slots + j]
            found = jnp.where(lax.div(e, slots) == o_me, lax.rem(e, slots), found)
        return found

    for q in range(2):

        @pl.loop(1, shards)
        def _(d):
            t = at_shard(d)
            remote(pj_ref.at[t, part(q)], pj1[q].at[from_shard(d)], j_send.at[q, d], j_recv.at[q, d], "shard", t).wait()

        pltpu.make_async_copy(pj_ref.at[s_me, part(q)], pj1[q].at[s_me], m_sem.at[2 + q]).wait()
        for k, t, _ in partners(o_me):
            pj_stage[q, t] = pj1[q][expert_at(t)]
            remote(pj_stage.at[q, t], pj2.at[q, o_me], jo_send.at[q, k], jo_recv.at[q, k], "owner", t).start()

        pj2[q, o_me] = pj1[q][expert_at(o_me)]

    for c in range(0, CHUNKS):
        send_basis(c)

    own = []

    def pass_basis(c):

        @pl.loop(1, shards)
        def _(d):
            t = at_shard(d)
            remote(pn.at[c, t], pn1[c].at[from_shard(d)], p_send.at[c, d], p_recv.at[c, d], "shard", t).wait()

        for k, t, _ in partners(o_me):
            pn_stage[c, t] = pn1[c][expert_at(t)]
            remote(pn_stage.at[c, t], back[c].at[o_me], po_send.at[c, k], po_recv.at[c, k], "owner", t).start()

        pn_stage[c, o_me] = pn1[c][expert_at(o_me)]
        own.append(pltpu.make_async_copy(pn_stage.at[c, o_me], back[c].at[o_me], own_sem.at[c]))
        own[-1].start()

    for c in range(CHUNKS):
        pass_basis(c)

    for q in range(2):
        for k, t, source in partners(o_me):
            remote(pj_stage.at[q, t], pj2.at[q, source], jo_send.at[q, k], jo_recv.at[q, k], "owner", t).wait()

    for copy in moments:
        copy.wait()

    @pl.loop(0, slots)
    def _(j):
        home = lax.div(table[o_me * slots + j], slots)
        projected = jnp.concatenate([pj2[0, home], pj2[1, home]], axis=0)
        proj_out[j] = projected
        one, two = adam(one_ref[j], two_ref[j], projected)
        normed[j] = one / (jnp.sqrt(two) + EPSILON)

    other = s_me + 1 - 2 * lax.rem(s_me, 2)
    chips = shards // 2

    @pl.loop(1, chips)
    def _(k):
        t = at_shard(2 * k)
        remote(normed, normed_out.at[s_me], n_send.at[k], n_recv.at[k], "shard", t).start()

    remote(normed, normed_out.at[s_me], f_send.at[0], f_recv.at[0], "shard", other).start()
    own.append(pltpu.make_async_copy(normed, normed_out.at[s_me], own_sem.at[CHUNKS]))
    own[-1].start()

    @pl.loop(1, chips)
    def _(k):
        f = from_shard(2 * k)
        remote(normed, normed_out.at[f], n_send.at[k], n_recv.at[k], "shard", at_shard(2 * k)).wait()
        remote(normed_out.at[f], normed_out.at[f], f_send.at[k], f_recv.at[k], "shard", other).start()

    @pl.loop(0, chips)
    def _(k):
        g = lax.rem(other - 2 * k + shards, shards)
        remote(normed, normed_out.at[g], f_send.at[k], f_recv.at[k], "shard", other).wait()

    for copy in own:
        copy.wait()

    for c in range(CHUNKS):

        for k, t, source in partners(o_me):
            remote(pn_stage.at[c, t], back[c].at[source], po_send.at[c, k], po_recv.at[c, k], "owner", t).wait()


def leave(table, keep, mh, ml, pj, gh, gl, p, one, two):
    shards, rows, cols = gh.shape
    rank = p.shape[2]
    part = pj.shape[1]
    slots = one.shape[0]
    owners = table.shape[0] // slots
    chunk = rows // CHUNKS
    dma = pltpu.SemaphoreType.DMA
    smem = pl.BlockSpec(memory_space=pltpu.SMEM)
    vmem = pl.BlockSpec(memory_space=V)
    hbm = pl.BlockSpec(memory_space=pl.ANY)
    return pl.pallas_call(
        functools.partial(leave_body, shards, owners),
        out_shape=(
            jax.ShapeDtypeStruct((owners, chunk, rank), F32),
            jax.ShapeDtypeStruct((owners, chunk, rank), F32),
            jax.ShapeDtypeStruct((shards, slots, part, cols), F32),
            jax.ShapeDtypeStruct((slots, part, cols), F32),
        ),
        in_specs=[smem, smem, vmem, vmem] + [hbm] * 6,
        out_specs=(hbm, hbm, hbm, vmem),
        scratch_shapes=[
            V(one.shape, F32), V(two.shape, F32), V(gh.shape, BF), V(gh.shape, BF), V(p.shape, F32), V((CHUNKS, shards, chunk, rank), F32),
            V((shards, part // 2, cols), F32), V((shards, part // 2, cols), F32),
            V((2, owners, part // 2, cols), F32), V((2, owners, part // 2, cols), F32),
            V((shards, chunk, rank), F32), V((shards, chunk, rank), F32), V((CHUNKS, owners, chunk, rank), F32),
            V((slots, part, cols), F32),
            dma((shards,)), dma((shards,)), dma((shards,)),
            dma((2, shards)), dma((2, shards)), dma((2, owners)), dma((2, owners)),
            dma((CHUNKS, shards)), dma((CHUNKS, shards)), dma((CHUNKS, owners)), dma((CHUNKS, owners)),
            dma((shards // 2,)), dma((shards // 2,)), dma((shards // 2,)), dma((shards // 2,)), dma((CHUNKS + 1,)), dma((4,)),
        ],
        compiler_params=pltpu.CompilerParams(
            collective_id=1, has_side_effects=True, vmem_limit_bytes=56 * 1024 * 1024
        ),
        name="leave",
    )(table, keep, mh, ml, pj, gh, gl, p, one, two)


def finish_body(home_ref, back_a, back_b, normed_ref, proj_ref, one_ref, two_ref, basis_out, one_out, two_out, update_out,
                basis, normed, proj, one, two, update, b_sem, n_sem, m_sem, bo_sem, u_sem, mo_sem):
    slots, rows, _ = basis.shape
    chunk = rows // 2
    shards, part, cols = normed.shape[1:]

    def halves(j):
        return [
            pltpu.make_async_copy(ref.at[home_ref[j]], basis.at[j, c * chunk:(c + 1) * chunk], b_sem.at[c, j])
            for c, ref in enumerate((back_a, back_b))
        ]

    def step(j):
        return pltpu.make_async_copy(normed_ref.at[:, j], normed.at[j], n_sem.at[j])

    def basis_save(j):
        return pltpu.make_async_copy(basis.at[j], basis_out.at[j], bo_sem.at[j])

    def update_save(j):
        return pltpu.make_async_copy(update.at[j], update_out.at[j], u_sem.at[j])

    moments = [
        pltpu.make_async_copy(src, dst, m_sem.at[k])
        for k, (src, dst) in enumerate(((proj_ref, proj), (one_ref, one), (two_ref, two)))
    ]

    @pl.loop(0, slots)
    def _(j):
        for copy in halves(j):
            copy.start()
        step(j).start()

    for copy in moments:
        copy.start()

    @pl.loop(0, slots)
    def _(j):
        for copy in halves(j):
            copy.wait()
        basis_save(j).start()
        step(j).wait()
        product = dot3(split(basis[j]), split(normed[j].reshape(shards * part, cols)), NN)
        update[j] = (GALORE_SCALE * product).astype(BF)
        update_save(j).start()

    for copy in moments:
        copy.wait()
    one[...], two[...] = adam(one[...], two[...], proj[...])
    saves = [
        pltpu.make_async_copy(src, dst, mo_sem.at[k]) for k, (src, dst) in enumerate(((one, one_out), (two, two_out)))
    ]
    for copy in saves:
        copy.start()

    @pl.loop(0, slots)
    def _(j):
        basis_save(j).wait()
        update_save(j).wait()

    for copy in saves:
        copy.wait()


def finish(home, back_a, back_b, normed, projected, one, two):
    shards, slots, part, cols = normed.shape
    _, chunk, rank = back_a.shape
    dma = pltpu.SemaphoreType.DMA
    hbm = pl.BlockSpec(memory_space=pl.ANY)
    return pl.pallas_call(
        finish_body,
        out_shape=(
            jax.ShapeDtypeStruct((slots, 2 * chunk, rank), F32),
            jax.ShapeDtypeStruct(one.shape, F32),
            jax.ShapeDtypeStruct(two.shape, F32),
            jax.ShapeDtypeStruct((slots, 2 * chunk, cols), BF),
        ),
        in_specs=[pl.BlockSpec(memory_space=pltpu.SMEM)] + [hbm] * 6,
        out_specs=(hbm,) * 4,
        scratch_shapes=[
            V((slots, 2 * chunk, rank), F32), V((slots, shards, part, cols), F32),
            V(one.shape, F32), V(one.shape, F32), V(one.shape, F32), V((slots, 2 * chunk, cols), BF),
            dma((2, slots)), dma((slots,)), dma((3,)), dma((slots,)), dma((slots,)), dma((2,)),
        ],
        compiler_params=pltpu.CompilerParams(vmem_limit_bytes=60 * 1024 * 1024),
        name="finish",
    )(home, back_a, back_b, normed, projected, one, two)


def on_device(gradient, old_basis, moment_one, moment_two, slot_expert, cost):
    gh, gl, kh, kl, z, p = enter(slot_expert, gradient, old_basis)
    mh, ml, pj, keep, home = refresh(slot_expert, cost, gradient.shape[0], kh, kl, z)
    back_a, back_b, normed, projected = leave(slot_expert, keep, mh, ml, pj, gh, gl, p, moment_one, moment_two)
    return tuple(finish(home, back_a, back_b, normed, projected, moment_one, moment_two))


def solution(mesh):
    spec = P("owner", "shard", None)
    return jax.shard_map(
        on_device, mesh=mesh, in_specs=(spec,) * 4 + (P(), P()), out_specs=(spec,) * 4, check_vma=False
    )
```

```python
import functools
import jax, jax.numpy as jnp
from jax import lax
from jax.experimental import pallas as pl
from jax.sharding import PartitionSpec as P
from jax.experimental.pallas import tpu as pltpu

BF = jnp.bfloat16
F32 = jnp.float32

def split(x):
    hi = x.astype(BF)
    return hi, (x - hi.astype(F32)).astype(BF)

def mm(a, b, dims):
    return lax.dot_general(a, b, (dims, ((), ())), preferred_element_type=F32)

NN = ((1,), (0,))
TN = ((0,), (0,))
NT = ((1,), (1,))

def dot3(a, b, dims):
    ah, al = a
    bh, bl = b
    return mm(ah, bh, dims) + (mm(ah, bl, dims) + mm(al, bh, dims))

PANEL, GROUP = 32, 16


def factor(c_ref, xh, xl, ls, rs):
    nb, sub_nb = PANEL, GROUP
    n = c_ref.shape[0]
    tile = lax.broadcasted_iota(jnp.int32, (8, 128), 0)
    for p in range(n // nb):
        lo = p * nb
        need = [h for h in range(4) if (h < 2 and h * 128 + 128 > lo) or (h >= 2 and (h - 2) * 128 < lo + nb)]
        sub = lax.broadcasted_iota(jnp.int32, (nb, 128), 0)
        s = {}
        for h in need:
            if h < 2:
                s[h] = c_ref[lo:lo + nb, 128 * h:128 * h + 128]
            else:
                l = lax.broadcasted_iota(jnp.int32, (nb, 128), 1) + 128 * (h - 2)
                s[h] = jnp.where(l == sub + lo, 1.0, 0.0)
        a0, a1 = need[0] * 128, need[-1] * 128 + 128
        cuts = []
        if p > 1:
            cuts.append((0, 3 * (lo - nb)))
        if p > 0:
            cuts.append((3 * (lo - nb), 3 * lo))
        for (x, y) in cuts:
            d = mm(ls[x:y, lo:lo + nb], rs[x:y, a0:a1], TN)
            for h in need:
                s[h] = s[h] - d[:, 128 * h - a0:128 * h - a0 + 128]
        hd = lo // 128
        off = lo - hd * 128
        pivots = []
        done = []
        for g in range(nb // sub_nb):
            b = g * sub_nb
            cols = [jnp.broadcast_to(s[hd][:, off + b + k:off + b + k + 1], (nb - b, 128)) for k in range(sub_nb)]
            for j in range(sub_nb):
                jj = j % 8
                d = cols[j][jj:jj + 1, :]
                pivots.append(d)
                m = cols[j] * (1.0 / d)
                for k in range(j + 1, sub_nb):
                    cols[k] = cols[k] - m * cols[k][jj:jj + 1, :]
                low = jnp.where(tile > jj, m[0:8], 0.0)
                if m.shape[0] > 8:
                    low = jnp.concatenate([low, m[8:]], axis=0)
                for h in need:
                    s[h] = s[h] - low * s[h][jj:jj + 1, :]
                if jj == 7:
                    done.append({h: s[h][0:8] for h in need})
                    if m.shape[0] > 8:
                        s = {h: s[h][8:] for h in need}
                        cols = [t[8:] for t in cols]
        scale = lax.rsqrt(jnp.concatenate(pivots, axis=0))
        for h in range(4):
            if h not in need:
                o = jnp.zeros((nb, 128), F32)
            else:
                o = jnp.concatenate([t[h] for t in done], axis=0) * scale
                if h == hd:
                    l = lax.broadcasted_iota(jnp.int32, (nb, 128), 1) + 128 * h
                    o = jnp.where(l >= sub + lo, o, 0.0)
            cs = slice(128 * h, 128 * h + 128)
            hi = o.astype(BF)
            lw = (o - hi.astype(F32)).astype(BF)
            if h >= 2:
                xs = slice(128 * (h - 2), 128 * (h - 2) + 128)
                xh[lo:lo + nb, xs] = hi
                xl[lo:lo + nb, xs] = lw
            b = 3 * lo
            rs[b:b + nb, cs] = hi
            rs[b + nb:b + 2 * nb, cs] = lw
            rs[b + 2 * nb:b + 3 * nb, cs] = hi
            if h < 2:
                ls[b:b + nb, cs] = hi
                ls[b + nb:b + 2 * nb, cs] = hi
                ls[b + 2 * nb:b + 3 * nb, cs] = lw


MESH = pl.DeviceIdType.MESH
V = pltpu.VMEM


def greet(groups):
    barrier = pltpu.get_barrier_semaphore()
    total = 0
    for axis, size in groups:
        me = lax.axis_index(axis)

        @pl.loop(1, size)
        def _(d):
            pl.semaphore_signal(barrier, inc=1, device_id={axis: lax.rem(me + d, size)}, device_id_type=MESH)

        total += size - 1
    pl.semaphore_wait(barrier, total)


STEPS = (
    (2, 1), (1, 0), (0, 3), (1, 2), (3, 3), (3, 0), (2, 3), (0, 1), (1, 1), (3, 2), (1, 3), (2, 0), (3, 1), (0, 2), (2, 2),
)
SIDE = 4


def partners(me):
    z, y = lax.div(me, SIDE), lax.rem(me, SIDE)
    for k, (dy, dz) in enumerate(STEPS):
        to = lax.rem(z + dz, SIDE) * SIDE + lax.rem(y + dy, SIDE)
        source = lax.rem(z + SIDE - dz, SIDE) * SIDE + lax.rem(y + SIDE - dy, SIDE)
        yield k, to, source


def remote(src, dst, send, recv, axis, target):
    return pltpu.make_async_remote_copy(
        src_ref=src, dst_ref=dst, send_sem=send, recv_sem=recv, device_id={axis: target}, device_id_type=MESH
    )


def slot_at(table, owner, slots, home):
    found = 0
    for j in range(slots):
        found = jnp.where(lax.div(table[owner * slots + j], slots) == home, j, found)
    return found


def enter_body(shards, owners, table, g_ref, b_hbm, gh_out, gl_out, kh_out, kl_out, z_out, p_out,
               b_ref, gland, gh, gl, kacc, kh, kl, stage, landed, stage2, pland,
               g_send, g_recv, a_send, a_recv, b_send, b_recv, own_sem, in_sem, h_sem, l_sem, p_sem, k_sem):
    s_me = lax.axis_index("shard")
    o_me = lax.axis_index("owner")
    load = pltpu.make_async_copy(b_hbm, b_ref, in_sem)
    load.start()
    greet((("shard", shards), ("owner", owners)))
    slots = shards

    def at_shard(d):
        return lax.rem(s_me + d, shards)

    def from_shard(d):
        return lax.rem(s_me - d + shards, shards)

    own = pltpu.make_async_copy(g_ref.at[s_me], gland.at[s_me], own_sem)
    own.start()

    @pl.loop(1, shards)
    def _(d):
        t = at_shard(d)
        remote(g_ref.at[t], gland.at[s_me], g_send.at[d], g_recv.at[d], "shard", t).start()

    load.wait()
    for k, t, _ in partners(o_me):
        stage[t] = b_ref[slot_at(table, o_me, slots, t)]
        remote(stage.at[t], landed.at[o_me], a_send.at[k], a_recv.at[k], "owner", t).start()

    landed[o_me] = b_ref[slot_at(table, o_me, slots, o_me)]
    kacc[...] = jnp.zeros_like(kacc)
    own.wait()
    tiles = kacc.shape[0] // 256

    def gram(f):
        h, l = split(gland[f])
        gh[f] = h
        gl[f] = l
        pltpu.make_async_copy(gh.at[f], gh_out.at[f], h_sem.at[f]).start()
        pltpu.make_async_copy(gl.at[f], gl_out.at[f], l_sem.at[f]).start()
        for a in range(tiles):
            ra = slice(256 * a, 256 * a + 256)
            for b in range(a, tiles):
                rb = slice(256 * b, 256 * b + 256)
                kacc[ra, rb] += dot3((h[:, ra], l[:, ra]), (h[:, rb], l[:, rb]), TN)

    gram(s_me)

    def take_gram(d):
        f = from_shard(d)
        remote(g_ref.at[at_shard(d)], gland.at[f], g_send.at[d], g_recv.at[d], "shard", at_shard(d)).wait_recv()
        gram(f)

    half = EARLY
    pl.loop(1, half)(take_gram)

    for k, t, source in partners(o_me):
        remote(stage.at[t], landed.at[source], a_send.at[k], a_recv.at[k], "owner", t).wait()

    def holder(i):
        def add(o, found):
            for j in range(slots):
                found = jnp.where(table[o * slots + j] == o_me * slots + i, o, found)
            return found

        return lax.fori_loop(0, owners, add, 0)

    @pl.loop(1, shards)
    def _(d):
        t = at_shard(d)
        stage2[t] = landed[holder(t)]
        remote(stage2.at[t], pland.at[s_me], b_send.at[d], b_recv.at[d], "shard", t).start()

    pland[s_me] = landed[holder(s_me)]
    pl.loop(half, shards)(take_gram)

    for a in range(tiles):
        ra = slice(256 * a, 256 * a + 256)
        for b in range(a, tiles):
            rb = slice(256 * b, 256 * b + 256)
            h, l = split(kacc[ra, rb])
            kh[ra, rb] = h
            kl[ra, rb] = l
            if b > a:
                h, l = split(kacc[ra, rb].T)
                kh[rb, ra] = h
                kl[rb, ra] = l

    save_k = (pltpu.make_async_copy(kh, kh_out, k_sem.at[0]), pltpu.make_async_copy(kl, kl_out, k_sem.at[1]))
    for copy in save_k:
        copy.start()

    def project(f):
        pltpu.make_async_copy(pland.at[f], p_out.at[f], p_sem.at[f]).start()
        return dot3(split(pland[f]), (gh[f], gl[f]), TN)

    z_out[...] = project(s_me)

    @pl.loop(1, shards)
    def _(d):
        f = from_shard(d)
        remote(stage2.at[at_shard(d)], pland.at[f], b_send.at[d], b_recv.at[d], "shard", at_shard(d)).wait()
        z_out[...] += project(f)

    @pl.loop(1, shards)
    def _(d):
        remote(g_ref.at[at_shard(d)], gland.at[from_shard(d)], g_send.at[d], g_recv.at[d], "shard", at_shard(d)).wait_send()

    @pl.loop(0, shards)
    def _(f):
        pltpu.make_async_copy(gh.at[f], gh_out.at[f], h_sem.at[f]).wait()
        pltpu.make_async_copy(gl.at[f], gl_out.at[f], l_sem.at[f]).wait()
        pltpu.make_async_copy(pland.at[f], p_out.at[f], p_sem.at[f]).wait()

    for copy in save_k:
        copy.wait()


EARLY = 1


def enter(table, gradient, basis):
    shards, rows, cols = gradient.shape
    rank = basis.shape[2]
    owners = table.shape[0] // basis.shape[0]
    sem = pltpu.SemaphoreType.DMA
    smem = pl.BlockSpec(memory_space=pltpu.SMEM)
    vmem = pl.BlockSpec(memory_space=V)
    hbm = pl.BlockSpec(memory_space=pl.ANY)
    return pl.pallas_call(
        functools.partial(enter_body, shards, owners),
        out_shape=(
            jax.ShapeDtypeStruct((shards, rows, cols), BF),
            jax.ShapeDtypeStruct((shards, rows, cols), BF),
            jax.ShapeDtypeStruct((cols, cols), BF),
            jax.ShapeDtypeStruct((cols, cols), BF),
            jax.ShapeDtypeStruct((rank, cols), F32),
            jax.ShapeDtypeStruct((shards, rows, rank), F32),
        ),
        in_specs=[smem, hbm, hbm],
        out_specs=(hbm, hbm, hbm, hbm, vmem, hbm),
        scratch_shapes=[
            V((shards, rows, rank), F32), V((shards, rows, cols), F32), V((shards, rows, cols), BF), V((shards, rows, cols), BF), V((cols, cols), F32), V((cols, cols), BF), V((cols, cols), BF),
            V((owners, rows, rank), F32), V((owners, rows, rank), F32), V((shards, rows, rank), F32), V((shards, rows, rank), F32),
            sem((shards,)), sem((shards,)), sem((owners,)), sem((owners,)), sem((shards,)), sem((shards,)),
            sem, sem, sem((shards,)), sem((shards,)), sem((shards,)), sem((2,)),
        ],
        compiler_params=pltpu.CompilerParams(
            collective_id=0, has_side_effects=True, vmem_limit_bytes=56 * 1024 * 1024
        ),
        name="enter",
    )(table, gradient, basis)


def body(table, cost, kh_ref, kl_ref, zin_ref, mh_ref, ml_ref, pj_ref, keep_ref, home_ref, z_ref, w_ref, c_ref, xh, xl, ls, rs):
    s_me = lax.axis_index("shard")
    o_me = lax.axis_index("owner")
    shards, part, cols = pj_ref.shape
    count = cost[o_me * shards + s_me]
    keep_ref[0] = jnp.where(count > 0, 0.0, 1.0)
    for j in range(shards):
        home_ref[j] = lax.div(table[o_me * shards + j], shards)
    z_ref[...] = zin_ref[...]

    @pl.loop(0, count)
    def _(it):
        z = split(z_ref[...])
        w_ref[...] = dot3(z, (kh_ref[...], kl_ref[...]), NN)
        w = split(w_ref[...])
        c_ref[...] = dot3(z, w, NT)
        factor(c_ref, xh, xl, ls, rs)
        x = (xh[...], xl[...])
        z_ref[...] = dot3(x, w, NN)

        @pl.when(it == count - 1)
        def _():
            h, l = split(dot3(x, z, NN))
            mh_ref[...] = h
            ml_ref[...] = l

    @pl.when(count == 0)
    def _():
        mh_ref[...] = jnp.zeros_like(mh_ref)
        ml_ref[...] = jnp.zeros_like(ml_ref)

    for s in range(shards):
        pj_ref[s] = z_ref[part * s:part * s + part, :]


def refresh(table, cost, shards, kh, kl, z):
    rank, cols = z.shape
    smem = pl.BlockSpec(memory_space=pltpu.SMEM)
    vmem = pl.BlockSpec(memory_space=V)
    return pl.pallas_call(
        body,
        out_shape=(
            jax.ShapeDtypeStruct((rank, cols), BF),
            jax.ShapeDtypeStruct((rank, cols), BF),
            jax.ShapeDtypeStruct((shards, rank // shards, cols), F32),
            jax.ShapeDtypeStruct((1,), F32),
            jax.ShapeDtypeStruct((shards,), jnp.int32),
        ),
        in_specs=[smem, smem, vmem, vmem, vmem],
        out_specs=(vmem, vmem, vmem, smem, smem),
        scratch_shapes=[
            V((rank, cols), F32), V((rank, cols), F32), V((rank, rank), F32), V((rank, rank), BF), V((rank, rank), BF),
            V((3 * rank, rank), BF), V((3 * rank, 2 * rank), BF),
        ],
        compiler_params=pltpu.CompilerParams(vmem_limit_bytes=56 * 1024 * 1024),
        name="refresh",
    )(table, cost, kh, kl, z)


BETA_ONE = 0.9
BETA_TWO = 0.99
EPSILON = 1e-08
GALORE_SCALE = 0.25
CHUNKS = 2


def adam(one, two, projected):
    one = BETA_ONE * one + (1.0 - BETA_ONE) * projected
    two = BETA_TWO * two + (1.0 - BETA_TWO) * projected * projected
    return one, two


def leave_body(shards, owners, table, keep_ref, mh_ref, ml_ref, pj_ref, gh_hbm, gl_hbm, p_hbm, one_hbm, two_hbm,
               back_a, back_b, normed_out, proj_out,
               one_ref, two_ref, gh, gl, p_in, pn, pj1a, pj1b, pj_stage, pj2, pn1a, pn1b, pn_stage, normed,
               h_sem, l_sem, i_sem, j_send, j_recv, jo_send, jo_recv, p_send, p_recv, po_send, po_recv,
               n_send, n_recv, f_send, f_recv, own_sem, m_sem):
    s_me = lax.axis_index("shard")
    o_me = lax.axis_index("owner")
    slots = one_ref.shape[0]
    pn1, back, pj1 = (pn1a, pn1b), (back_a, back_b), (pj1a, pj1b)
    half = pj1a.shape[1]
    chunk = pn1a.shape[1]

    def at_shard(d):
        return lax.rem(s_me + d, shards)

    def from_shard(d):
        return lax.rem(s_me - d + shards, shards)

    def rows(c):
        return slice(c * chunk, (c + 1) * chunk)

    def loads(t):
        return (
            pltpu.make_async_copy(gh_hbm.at[t], gh.at[t], h_sem.at[t]),
            pltpu.make_async_copy(gl_hbm.at[t], gl.at[t], l_sem.at[t]),
            pltpu.make_async_copy(p_hbm.at[t], p_in.at[t], i_sem.at[t]),
        )

    @pl.loop(1, shards + 1)
    def _(d):
        for copy in loads(at_shard(d)):
            copy.start()

    moments = (pltpu.make_async_copy(one_hbm, one_ref, m_sem.at[0]), pltpu.make_async_copy(two_hbm, two_ref, m_sem.at[1]))
    for copy in moments:
        copy.start()
    greet((("shard", shards), ("owner", owners)))

    def part(q):
        return slice(q * half, (q + 1) * half)

    for q in range(2):

        @pl.loop(1, shards)
        def _(d):
            t = at_shard(d)
            remote(pj_ref.at[t, part(q)], pj1[q].at[s_me], j_send.at[q, d], j_recv.at[q, d], "shard", t).start()

        pltpu.make_async_copy(pj_ref.at[s_me, part(q)], pj1[q].at[s_me], m_sem.at[2 + q]).start()

    keep = keep_ref[0]

    def basis_rows(t, c):
        return dot3((gh[t, rows(c)], gl[t, rows(c)]), (mh_ref[...], ml_ref[...]), NT) + keep * p_in[t, rows(c)]

    def send_basis(c):
        @pl.loop(1, shards)
        def _(d):
            t = at_shard(d)
            if c == 0:
                for copy in loads(t):
                    copy.wait()
            pn[c, t] = basis_rows(t, c)
            remote(pn.at[c, t], pn1[c].at[s_me], p_send.at[c, d], p_recv.at[c, d], "shard", t).start()

        if c == 0:
            for copy in loads(s_me):
                copy.wait()
        pn1[c][s_me] = basis_rows(s_me, c)

    def expert_at(owner):
        found = 0
        for j in range(slots):
            e = table[owner * slots + j]
            found = jnp.where(lax.div(e, slots) == o_me, lax.rem(e, slots), found)
        return found

    for q in range(2):

        @pl.loop(1, shards)
        def _(d):
            t = at_shard(d)
            remote(pj_ref.at[t, part(q)], pj1[q].at[from_shard(d)], j_send.at[q, d], j_recv.at[q, d], "shard", t).wait()

        pltpu.make_async_copy(pj_ref.at[s_me, part(q)], pj1[q].at[s_me], m_sem.at[2 + q]).wait()
        for k, t, _ in partners(o_me):
            pj_stage[q, t] = pj1[q][expert_at(t)]
            remote(pj_stage.at[q, t], pj2.at[q, o_me], jo_send.at[q, k], jo_recv.at[q, k], "owner", t).start()

        pj2[q, o_me] = pj1[q][expert_at(o_me)]

    for c in range(0, CHUNKS):
        send_basis(c)

    own = []

    def pass_basis(c):

        @pl.loop(1, shards)
        def _(d):
            t = at_shard(d)
            remote(pn.at[c, t], pn1[c].at[from_shard(d)], p_send.at[c, d], p_recv.at[c, d], "shard", t).wait()

        for k, t, _ in partners(o_me):
            pn_stage[c, t] = pn1[c][expert_at(t)]
            remote(pn_stage.at[c, t], back[c].at[o_me], po_send.at[c, k], po_recv.at[c, k], "owner", t).start()

        pn_stage[c, o_me] = pn1[c][expert_at(o_me)]
        own.append(pltpu.make_async_copy(pn_stage.at[c, o_me], back[c].at[o_me], own_sem.at[c]))
        own[-1].start()

    for c in range(CHUNKS):
        pass_basis(c)

    for q in range(2):
        for k, t, source in partners(o_me):
            remote(pj_stage.at[q, t], pj2.at[q, source], jo_send.at[q, k], jo_recv.at[q, k], "owner", t).wait()

    for copy in moments:
        copy.wait()

    @pl.loop(0, slots)
    def _(j):
        home = lax.div(table[o_me * slots + j], slots)
        projected = jnp.concatenate([pj2[0, home], pj2[1, home]], axis=0)
        proj_out[j] = projected
        one, two = adam(one_ref[j], two_ref[j], projected)
        normed[j] = one / (jnp.sqrt(two) + EPSILON)

    other = s_me + 1 - 2 * lax.rem(s_me, 2)
    chips = shards // 2

    @pl.loop(1, chips)
    def _(k):
        t = at_shard(2 * k)
        remote(normed, normed_out.at[s_me], n_send.at[k], n_recv.at[k], "shard", t).start()

    remote(normed, normed_out.at[s_me], f_send.at[0], f_recv.at[0], "shard", other).start()
    own.append(pltpu.make_async_copy(normed, normed_out.at[s_me], own_sem.at[CHUNKS]))
    own[-1].start()

    @pl.loop(1, chips)
    def _(k):
        f = from_shard(2 * k)
        remote(normed, normed_out.at[f], n_send.at[k], n_recv.at[k], "shard", at_shard(2 * k)).wait()
        remote(normed_out.at[f], normed_out.at[f], f_send.at[k], f_recv.at[k], "shard", other).start()

    @pl.loop(0, chips)
    def _(k):
        g = lax.rem(other - 2 * k + shards, shards)
        remote(normed, normed_out.at[g], f_send.at[k], f_recv.at[k], "shard", other).wait()

    for copy in own:
        copy.wait()

    for c in range(CHUNKS):

        for k, t, source in partners(o_me):
            remote(pn_stage.at[c, t], back[c].at[source], po_send.at[c, k], po_recv.at[c, k], "owner", t).wait()


def leave(table, keep, mh, ml, pj, gh, gl, p, one, two):
    shards, rows, cols = gh.shape
    rank = p.shape[2]
    part = pj.shape[1]
    slots = one.shape[0]
    owners = table.shape[0] // slots
    chunk = rows // CHUNKS
    dma = pltpu.SemaphoreType.DMA
    smem = pl.BlockSpec(memory_space=pltpu.SMEM)
    vmem = pl.BlockSpec(memory_space=V)
    hbm = pl.BlockSpec(memory_space=pl.ANY)
    return pl.pallas_call(
        functools.partial(leave_body, shards, owners),
        out_shape=(
            jax.ShapeDtypeStruct((owners, chunk, rank), F32),
            jax.ShapeDtypeStruct((owners, chunk, rank), F32),
            jax.ShapeDtypeStruct((shards, slots, part, cols), F32),
            jax.ShapeDtypeStruct((slots, part, cols), F32),
        ),
        in_specs=[smem, smem, vmem, vmem] + [hbm] * 6,
        out_specs=(hbm, hbm, hbm, vmem),
        scratch_shapes=[
            V(one.shape, F32), V(two.shape, F32), V(gh.shape, BF), V(gh.shape, BF), V(p.shape, F32), V((CHUNKS, shards, chunk, rank), F32),
            V((shards, part // 2, cols), F32), V((shards, part // 2, cols), F32),
            V((2, owners, part // 2, cols), F32), V((2, owners, part // 2, cols), F32),
            V((shards, chunk, rank), F32), V((shards, chunk, rank), F32), V((CHUNKS, owners, chunk, rank), F32),
            V((slots, part, cols), F32),
            dma((shards,)), dma((shards,)), dma((shards,)),
            dma((2, shards)), dma((2, shards)), dma((2, owners)), dma((2, owners)),
            dma((CHUNKS, shards)), dma((CHUNKS, shards)), dma((CHUNKS, owners)), dma((CHUNKS, owners)),
            dma((shards // 2,)), dma((shards // 2,)), dma((shards // 2,)), dma((shards // 2,)), dma((CHUNKS + 1,)), dma((4,)),
        ],
        compiler_params=pltpu.CompilerParams(
            collective_id=1, has_side_effects=True, vmem_limit_bytes=56 * 1024 * 1024
        ),
        name="leave",
    )(table, keep, mh, ml, pj, gh, gl, p, one, two)


def finish_body(home_ref, back_a, back_b, normed_ref, proj_ref, one_ref, two_ref, basis_out, one_out, two_out, update_out,
                basis, normed, proj, one, two, update, b_sem, n_sem, m_sem, bo_sem, u_sem, mo_sem):
    slots, rows, _ = basis.shape
    chunk = rows // 2
    shards, part, cols = normed.shape[1:]

    def halves(j):
        return [
            pltpu.make_async_copy(ref.at[home_ref[j]], basis.at[j, c * chunk:(c + 1) * chunk], b_sem.at[c, j])
            for c, ref in enumerate((back_a, back_b))
        ]

    def step(j):
        return pltpu.make_async_copy(normed_ref.at[:, j], normed.at[j], n_sem.at[j])

    def basis_save(j):
        return pltpu.make_async_copy(basis.at[j], basis_out.at[j], bo_sem.at[j])

    def update_save(j):
        return pltpu.make_async_copy(update.at[j], update_out.at[j], u_sem.at[j])

    moments = [
        pltpu.make_async_copy(src, dst, m_sem.at[k])
        for k, (src, dst) in enumerate(((proj_ref, proj), (one_ref, one), (two_ref, two)))
    ]

    @pl.loop(0, slots)
    def _(j):
        for copy in halves(j):
            copy.start()
        step(j).start()

    for copy in moments:
        copy.start()

    @pl.loop(0, slots)
    def _(j):
        for copy in halves(j):
            copy.wait()
        basis_save(j).start()
        step(j).wait()
        product = dot3(split(basis[j]), split(normed[j].reshape(shards * part, cols)), NN)
        update[j] = (GALORE_SCALE * product).astype(BF)
        update_save(j).start()

    for copy in moments:
        copy.wait()
    one[...], two[...] = adam(one[...], two[...], proj[...])
    saves = [
        pltpu.make_async_copy(src, dst, mo_sem.at[k]) for k, (src, dst) in enumerate(((one, one_out), (two, two_out)))
    ]
    for copy in saves:
        copy.start()

    @pl.loop(0, slots)
    def _(j):
        basis_save(j).wait()
        update_save(j).wait()

    for copy in saves:
        copy.wait()


def finish(home, back_a, back_b, normed, projected, one, two):
    shards, slots, part, cols = normed.shape
    _, chunk, rank = back_a.shape
    dma = pltpu.SemaphoreType.DMA
    hbm = pl.BlockSpec(memory_space=pl.ANY)
    return pl.pallas_call(
        finish_body,
        out_shape=(
            jax.ShapeDtypeStruct((slots, 2 * chunk, rank), F32),
            jax.ShapeDtypeStruct(one.shape, F32),
            jax.ShapeDtypeStruct(two.shape, F32),
            jax.ShapeDtypeStruct((slots, 2 * chunk, cols), BF),
        ),
        in_specs=[pl.BlockSpec(memory_space=pltpu.SMEM)] + [hbm] * 6,
        out_specs=(hbm,) * 4,
        scratch_shapes=[
            V((slots, 2 * chunk, rank), F32), V((slots, shards, part, cols), F32),
            V(one.shape, F32), V(one.shape, F32), V(one.shape, F32), V((slots, 2 * chunk, cols), BF),
            dma((2, slots)), dma((slots,)), dma((3,)), dma((slots,)), dma((slots,)), dma((2,)),
        ],
        compiler_params=pltpu.CompilerParams(vmem_limit_bytes=60 * 1024 * 1024),
        name="finish",
    )(home, back_a, back_b, normed, projected, one, two)


def on_device(gradient, old_basis, moment_one, moment_two, slot_expert, cost):
    gh, gl, kh, kl, z, p = enter(slot_expert, gradient, old_basis)
    mh, ml, pj, keep, home = refresh(slot_expert, cost, gradient.shape[0], kh, kl, z)
    back_a, back_b, normed, projected = leave(slot_expert, keep, mh, ml, pj, gh, gl, p, moment_one, moment_two)
    return tuple(finish(home, back_a, back_b, normed, projected, moment_one, moment_two))


def solution(mesh):
    spec = P("owner", "shard", None)
    return jax.shard_map(
        on_device, mesh=mesh, in_specs=(spec,) * 4 + (P(), P()), out_specs=(spec,) * 4, check_vma=False
    )
```
